32 devices in a mesh: seq: 4 (over z), head: 8 (over y, x, core).
Axes of the slice: x: 2, y: 2, z: 4, core: 2. Of those that a mesh axis runs over, the one named last changes fastest.
Arguments:
- hidden_in: bfloat16 [4096, 2048], P(('seq', 'head')), may hold values from -6 to 6
- out_grad: bfloat16 [4096, 2048], P(('seq', 'head')), may hold values from -8 to 8
- decays: float32 [4096, 16], P('seq', 'head'), may hold values from 0.4 to 1
- strength: float32 [4096, 16], P('seq', 'head'), may hold values from 0.2 to 0.95
- mixer_in: float32 [2048, 16, 768], P('seq', 'head'), may hold values from -0.125 to 0.125
- mixer_in_rows: float32 [2048], P('seq'), may hold values from 204 to 819
- mixer_in_cols: float32 [16, 768], P('head'), may hold values from 204 to 819
- mixer_out: float32 [16, 256, 2048], P('head', None, 'seq'), may hold values from -0.125 to 0.125
- mixer_out_rows: float32 [16, 256], P('head'), may hold values from 341 to 1365
- mixer_out_cols: float32 [2048], P('seq'), may hold values from 341 to 1365
- feed_in: float32 [2048, 2, 5632], P('head', None, 'seq'), may hold values from -0.125 to 0.125
- feed_in_rows: float32 [2048], P('head'), may hold values from 68 to 273
- feed_in_cols: float32 [2, 5632], P(None, 'seq'), may hold values from 68 to 273
- feed_out: float32 [5632, 2048], P('seq', 'head'), may hold values from -0.078125 to 0.078125
- feed_out_rows: float32 [5632], P('seq'), may hold values from 292 to 1024
- feed_out_cols: float32 [2048], P('head'), may hold values from 292 to 1024
- conv_kernel: float32 [4, 16, 512], P(None, 'head', 'seq'), may hold values from -3 to 3
- conv_second: float32 [4, 16, 512], P(None, 'head', 'seq'), may hold values from 204 to 819
- norm_gains: float32 [2, 2048], replicated, may hold values from 0.35 to 2.8
- gains_second: float32 [2, 2048], replicated, may hold values from 819 to 3072
- head_gain: float32 [256], replicated, may hold values from 0.5 to 1.5
- head_gain_second: float32 [256], replicated, may hold values from 4681 to 16384
Outputs:
- block_out: bfloat16 [4096, 2048], P(('seq', 'head'))
- input_grad: float32 [4096, 2048], P(('seq', 'head'))
- mixer_in_grad: float32 [2048, 16, 768], P('seq', 'head')
- mixer_in_rows_new: float32 [2048], P('seq')
- mixer_in_cols_new: float32 [16, 768], P('head')
- mixer_in_new: float32 [2048, 16, 768], P('seq', 'head')
- mixer_out_grad: float32 [16, 256, 2048], P('head', None, 'seq')
- mixer_out_rows_new: float32 [16, 256], P('head')
- mixer_out_cols_new: float32 [2048], P('seq')
- mixer_out_new: float32 [16, 256, 2048], P('head', None, 'seq')
- feed_in_grad: float32 [2048, 2, 5632], P('head', None, 'seq')
- feed_in_rows_new: float32 [2048], P('head')
- feed_in_cols_new: float32 [2, 5632], P(None, 'seq')
- feed_in_new: float32 [2048, 2, 5632], P('head', None, 'seq')
- feed_out_grad: float32 [5632, 2048], P('seq', 'head')
- feed_out_rows_new: float32 [5632], P('seq')
- feed_out_cols_new: float32 [2048], P('head')
- feed_out_new: float32 [5632, 2048], P('seq', 'head')
- conv_grad: float32 [4, 16, 512], P(None, 'head', 'seq')
- conv_second_new: float32 [4, 16, 512], P(None, 'head', 'seq')
- conv_new: float32 [4, 16, 512], P(None, 'head', 'seq')
- gains_grad: float32 [2, 2048], replicated
- gains_second_new: float32 [2, 2048], replicated
- gains_new: float32 [2, 2048], replicated
- head_gain_grad: float32 [256], replicated
- head_gain_second_new: float32 [256], replicated
- head_gain_new: float32 [256], replicated
The draws below stay inside these ranges and needn't reach their ends.
All inputs are finite; a program needn't handle non-finite values.
Results may differ from the reference program's by a relative error of at most 0.02.
Values may be sent and summed in bfloat16 or wider, within the bound.
No kernel may reach another device: no remote copies, remote signals or barrier semaphores. Data moves between devices by JAX's collectives and lax.ppermute only.
A program may use at most 256 MiB of HBM per device.

```python
import math
import jax
import jax.numpy as jnp
from jax import lax

D = 2048
HEAD_TOTAL = 16
DK = 128
DV = 256
FF = 5632
KC = 4
BLOCK = 64
STEP = 10
SEQUENCE_TOKENS = 4096


def rising_scale(length, spread_ratio):
    fraction = jnp.arange(length, dtype=jnp.float32) / (length - 1)
    return jnp.exp(jnp.log(spread_ratio) * (fraction - 0.5))


def draw_norm_gains(key, part):
    key = jax.random.fold_in(key, 11)
    spread_ratio = 3.0
    factor = jax.random.uniform(key, (2, D), jnp.float32, 0.8, 1.25)
    return factor * rising_scale(D, spread_ratio)[None, :]


def draw_out_grad(key, part):
    key = jax.random.fold_in(key, 12)
    samples = jax.random.normal(key, (SEQUENCE_TOKENS, D), jnp.float32)
    spread_ratio = 3.0
    return jnp.clip(samples * rising_scale(D, spread_ratio)[None, :], -8.0, 8.0).astype(jnp.bfloat16)


def draw_decays(key, part):
    key = jax.random.fold_in(key, 13)
    random_subkeys = jax.random.split(key, 6)
    fast_share = 0.5
    is_fast = jax.random.uniform(random_subkeys[0], (HEAD_TOTAL,), jnp.float32) < fast_share
    slow_rate = jax.random.uniform(random_subkeys[1], (HEAD_TOTAL,), jnp.float32, 0.15, 0.5) / SEQUENCE_TOKENS
    fast_rate = jnp.exp(jax.random.uniform(random_subkeys[2], (HEAD_TOTAL,), jnp.float32, jnp.log(0.06), jnp.log(0.1)))
    base_rate = jnp.where(is_fast, fast_rate, slow_rate)
    jitter = jax.random.uniform(random_subkeys[3], (SEQUENCE_TOKENS, HEAD_TOTAL), jnp.float32, 0.5, 1.5)
    drift = jnp.exp(jnp.log(2.0) * jnp.arange(SEQUENCE_TOKENS, dtype=jnp.float32) / SEQUENCE_TOKENS)
    all_rates = base_rate[None, :] * jitter * drift[:, None]
    spike_position = jax.random.randint(random_subkeys[4], (2,), 0, SEQUENCE_TOKENS)
    spike_loss = jax.random.uniform(random_subkeys[5], (2, HEAD_TOTAL), jnp.float32, 0.2, 0.4)
    is_spike = jnp.arange(SEQUENCE_TOKENS)[:, None] == spike_position[None, :]
    preserved = jnp.prod(jnp.where(is_spike[:, :, None], 1.0 - spike_loss[None], 1.0), axis=1)
    return jnp.exp(-all_rates) * preserved


def steps_of(key, extent, shards, smallest, largest):
    def one(dim, parts):
        draws = jax.random.uniform(jax.random.fold_in(jax.random.fold_in(key, 6), dim), (parts,), jnp.float32, smallest / len(shards), largest / len(shards))
        return jnp.repeat(jnp.exp(draws), extent[dim] // parts).reshape((-1,) + (1,) * (len(extent) - dim - 1))

    gain = one(*shards[0])
    for cut in shards[1:]:
        gain = gain * one(*cut)
    return gain


def bell_draw(own_key, extent, scale, bound, cuts=(), kind=jnp.bfloat16):
    values = jax.random.normal(own_key, extent, jnp.float32) * scale
    if len(cuts) > 0:
        values = steps_of(own_key, extent, cuts, -0.22, 0.18) * values
    return jnp.clip(values, min=-bound, max=bound).astype(kind)


def setup_inputs(seed: int = 0) -> dict:
    streams_of = jax.random.split(jax.random.key(seed), 23)
    return {
        "hidden_in": bell_draw(streams_of[0], (SEQUENCE_TOKENS, D), 1.0, 6.0, ((0, 32),)),
        "out_grad": draw_out_grad(jax.random.fold_in(streams_of[22], 71), 0),
        "decays": draw_decays(jax.random.fold_in(streams_of[22], 71), 0),
        "strength": jnp.clip(0.2 + 0.75 * jax.random.uniform(streams_of[3], (SEQUENCE_TOKENS, HEAD_TOTAL), jnp.float32) ** steps_of(streams_of[3], (SEQUENCE_TOKENS, HEAD_TOTAL), ((0, 4), (1, 8)), -0.2, 0.2), 0.2, 0.95),
        "mixer_in": bell_draw(streams_of[4], (D, HEAD_TOTAL, 2 * DK + 2 * DV), D ** -0.5, 0.125, ((0, 4), (1, 8)), jnp.float32),
        "mixer_in_rows": jnp.clip(jnp.exp(math.log(819.0) - 1.3899641 * jax.random.uniform(streams_of[5], (D,), jnp.float32) ** steps_of(streams_of[5], (D,), ((0, 4),), -0.2, 0.2)), 204.0, 819.0),
        "mixer_in_cols": jnp.clip(jnp.exp(math.log(819.0) - 1.3899641 * jax.random.uniform(streams_of[6], (HEAD_TOTAL, 2 * DK + 2 * DV), jnp.float32) ** steps_of(streams_of[6], (HEAD_TOTAL, 2 * DK + 2 * DV), ((0, 8),), -0.2, 0.2)), 204.0, 819.0),
        "mixer_out": bell_draw(streams_of[7], (HEAD_TOTAL, DV, D), (HEAD_TOTAL * DV // 2) ** -0.5, 0.125, ((0, 8), (2, 4)), jnp.float32),
        "mixer_out_rows": jnp.clip(jnp.exp(math.log(1365.0) - 1.38702723 * jax.random.uniform(streams_of[8], (HEAD_TOTAL, DV), jnp.float32) ** steps_of(streams_of[8], (HEAD_TOTAL, DV), ((0, 8),), -0.2, 0.2)), 341.0, 1365.0),
        "mixer_out_cols": jnp.clip(jnp.exp(math.log(1365.0) - 1.38702723 * jax.random.uniform(streams_of[9], (D,), jnp.float32) ** steps_of(streams_of[9], (D,), ((0, 4),), -0.2, 0.2)), 341.0, 1365.0),
        "feed_in": bell_draw(streams_of[10], (D, 2, FF), D ** -0.5, 0.125, ((0, 8), (2, 4)), jnp.float32),
        "feed_in_rows": jnp.clip(jnp.exp(math.log(273.0) - 1.3899641 * jax.random.uniform(streams_of[11], (D,), jnp.float32) ** steps_of(streams_of[11], (D,), ((0, 8),), -0.2, 0.2)), 68.0, 273.0),
        "feed_in_cols": jnp.clip(jnp.exp(math.log(273.0) - 1.3899641 * jax.random.uniform(streams_of[12], (2, FF), jnp.float32) ** steps_of(streams_of[12], (2, FF), ((1, 4),), -0.2, 0.2)), 68.0, 273.0),
        "feed_out": bell_draw(streams_of[13], (FF, D), FF ** -0.5, 0.078125, ((0, 4), (1, 8)), jnp.float32),
        "feed_out_rows": jnp.clip(jnp.exp(math.log(1024.0) - 1.254718 * jax.random.uniform(streams_of[14], (FF,), jnp.float32) ** steps_of(streams_of[14], (FF,), ((0, 4),), -0.2, 0.2)), 292.0, 1024.0),
        "feed_out_cols": jnp.clip(jnp.exp(math.log(1024.0) - 1.254718 * jax.random.uniform(streams_of[15], (D,), jnp.float32) ** steps_of(streams_of[15], (D,), ((0, 8),), -0.2, 0.2)), 292.0, 1024.0),
        "conv_kernel": bell_draw(streams_of[16], (KC, HEAD_TOTAL, 2 * DK + DV), KC ** -0.5, 3.0, ((1, 8), (2, 4)), jnp.float32),
        "conv_second": jnp.clip(jnp.exp(math.log(819.0) - 1.3899641 * jax.random.uniform(streams_of[17], (KC, HEAD_TOTAL, 2 * DK + DV), jnp.float32) ** steps_of(streams_of[17], (KC, HEAD_TOTAL, 2 * DK + DV), ((1, 8), (2, 4)), -0.2, 0.2)), 204.0, 819.0),
        "norm_gains": draw_norm_gains(jax.random.fold_in(streams_of[22], 71), 0),
        "gains_second": jnp.clip(jnp.exp(jax.random.uniform(streams_of[19], (2, D), jnp.float32, math.log(819.0), math.log(3072.0))), 819.0, 3072.0),
        "head_gain": jnp.clip(1.0 + 0.1 * jax.random.normal(streams_of[20], (DV,), jnp.float32), 0.5, 1.5),
        "head_gain_second": jnp.clip(jnp.exp(jax.random.uniform(streams_of[21], (DV,), jnp.float32, math.log(4681.0), math.log(16384.0))), 4681.0, 16384.0),
    }


HIGHEST = lax.Precision.HIGHEST

@jax.custom_vjp
def low(v):
    return lax.optimization_barrier(v.astype(jnp.bfloat16)).astype(jnp.float32)

@jax.custom_vjp
def low_back(v):
    return v

def low_keep(v):
    return (low(v), None)

def low_pass(kept, grad):
    return (grad,)

def back_keep(v):
    return (v, None)

def back_low(kept, grad):
    return (low(grad),)
low.defvjp(low_keep, low_pass)
low_back.defvjp(back_keep, back_low)

def norm_rows(entries, scale_row):
    return entries * lax.rsqrt(lax.optimization_barrier(jnp.mean(entries * entries, axis=-1, keepdims=True)) + 1e-06) * scale_row

def gate_norm(heads_rows, gate_part, gain_row):
    scaled = heads_rows * lax.rsqrt(lax.optimization_barrier(jnp.mean(heads_rows * heads_rows, axis=-1, keepdims=True)) + 1e-05)
    return scaled * gain_row * jax.nn.silu(gate_part)

def swiglu(gate_up):
    return jax.nn.silu(gate_up[:, 0]) * gate_up[:, 1]

def conv_piece(padded, kernel):
    length = padded.shape[0] - (KC - 1)
    summed = kernel[0] * padded[0:length]
    for offset in range(1, KC):
        summed = summed + kernel[offset] * padded[offset:offset + length]
    active = jax.nn.silu(summed)
    queries = active[..., :DK]
    key_rows = active[..., DK:2 * DK]
    values = active[..., 2 * DK:]
    queries = queries * lax.rsqrt(lax.optimization_barrier(jnp.sum(queries * queries, axis=-1, keepdims=True)) + 1e-06) * DK ** (-0.5)
    key_rows = key_rows * lax.rsqrt(lax.optimization_barrier(jnp.sum(key_rows * key_rows, axis=-1, keepdims=True)) + 1e-06)
    return (queries, key_rows, values)

def block_parts(queries, key_rows, values, log_decay, write_gain):
    cumulated = jnp.cumsum(log_decay, axis=-1)
    block_len = cumulated.shape[-1]
    row_index = lax.broadcasted_iota(jnp.int32, (block_len, block_len), 0)
    col_index = lax.broadcasted_iota(jnp.int32, (block_len, block_len), 1)
    is_below = row_index > col_index
    within = row_index >= col_index
    spread = cumulated[..., :, None] - cumulated[..., None, :]
    decay_ratio = jnp.where(within, jnp.exp(jnp.where(within, spread, 0.0)), 0.0)
    key_dots = jnp.einsum('bncd,bnjd->bncj', key_rows, key_rows, precision=HIGHEST)
    strict_part = jnp.where(is_below, write_gain[..., :, None] * decay_ratio * key_dots, 0.0)
    system = strict_part + jnp.eye(block_len, dtype=strict_part.dtype)
    write_vals = lax.linalg.triangular_solve(system, write_gain[..., None] * values, left_side=True, lower=True, unit_diagonal=True)
    write_keys = lax.linalg.triangular_solve(system, (write_gain * jnp.exp(cumulated))[..., None] * key_rows, left_side=True, lower=True, unit_diagonal=True)
    scores = jnp.where(within, decay_ratio * jnp.einsum('bncd,bnjd->bncj', queries, key_rows, precision=HIGHEST), 0.0)
    query_dec = queries * jnp.exp(cumulated)[..., None]
    key_dec = key_rows * jnp.exp(cumulated[..., -1:] - cumulated)[..., None]
    block_dec = jnp.exp(cumulated[..., -1])
    return (query_dec, key_dec, scores, write_keys, write_vals, block_dec)

def advance(state_now, pieces):
    update = pieces[4] - jnp.einsum('bcd,bde->bce', pieces[3], state_now, precision=HIGHEST)
    outputs = jnp.einsum('bcd,bde->bce', pieces[0], state_now, precision=HIGHEST) + jnp.einsum('bcj,bje->bce', pieces[2], update, precision=HIGHEST)
    state_next = pieces[5][:, None, None] * state_now + jnp.einsum('bcd,bce->bde', pieces[1], update, precision=HIGHEST)
    return (state_next, outputs)

def run_blocks(query_dec, key_dec, scores, write_keys, write_vals, block_dec, start_state):
    by_block = tuple((jnp.moveaxis(member, 1, 0) for member in (query_dec, key_dec, scores, write_keys, write_vals, block_dec)))
    last_state, outputs = lax.scan(jax.checkpoint(advance), start_state, by_block)
    return (jnp.moveaxis(outputs, 0, 1), last_state)

def to_blocks(entries):
    return jnp.moveaxis(entries, 1, 0).reshape(entries.shape[1], entries.shape[0] // BLOCK, BLOCK, entries.shape[2])

def from_blocks(entries):
    return jnp.moveaxis(entries.reshape(entries.shape[0], -1, entries.shape[3]), 0, 1)

def block_forward(rows_in, mix_in, mix_out, kernel, gain_heads, gains, expand, shrink, decays, strength):
    normed = low(norm_rows(rows_in, gains[0]))
    head_cols = 2 * DK + 2 * DV
    conv_width = 2 * DK + DV
    projected = low_back(jnp.dot(normed.astype(jnp.float32), low(mix_in).reshape(D, HEAD_TOTAL * head_cols).astype(jnp.float32), precision=HIGHEST, preferred_element_type=jnp.float32))
    projected = projected.reshape(SEQUENCE_TOKENS, HEAD_TOTAL, head_cols)
    conv_in = projected[..., :conv_width]
    gate_in = projected[..., conv_width:]
    padded = jnp.concatenate([jnp.zeros((KC - 1, HEAD_TOTAL, conv_width), jnp.float32), conv_in], 0)
    queries, key_rows, values = conv_piece(padded, low(kernel))
    log_decay = to_blocks(jnp.log(decays)[..., None])[..., 0]
    write_gain = to_blocks(strength[..., None])[..., 0]
    pieces = block_parts(to_blocks(queries), to_blocks(key_rows), to_blocks(values), log_decay, write_gain)
    outputs, last_state = run_blocks(pieces[0], pieces[1], pieces[2], pieces[3], pieces[4], pieces[5], jnp.zeros((HEAD_TOTAL, DK, DV), jnp.float32))
    gated = low(gate_norm(from_blocks(outputs), gate_in, gain_heads))
    mixed = low_back(jnp.dot(gated.reshape(SEQUENCE_TOKENS, HEAD_TOTAL * DV).astype(jnp.float32), low(mix_out).reshape(HEAD_TOTAL * DV, D).astype(jnp.float32), precision=HIGHEST, preferred_element_type=jnp.float32))
    residual = rows_in + mixed
    normed_two = low(norm_rows(residual, gains[1]))
    gate_up = low_back(jnp.einsum('td,dkf->tkf', normed_two, low(expand), precision=HIGHEST))
    hidden = low(swiglu(gate_up))
    feed_rows = low_back(jnp.dot(hidden.astype(jnp.float32), low(shrink).astype(jnp.float32), precision=HIGHEST, preferred_element_type=jnp.float32))
    return residual + feed_rows

def factored_update(weight, gradient, rows_old, cols_old, beta_two):
    squared = gradient * gradient + 1e-30
    rows_new = beta_two * rows_old + (1.0 - beta_two) * lax.optimization_barrier(jnp.mean(squared, axis=1))
    cols_new = beta_two * cols_old + (1.0 - beta_two) * lax.optimization_barrier(jnp.mean(squared, axis=0))
    second = rows_new[:, None] * cols_new[None, :] / jnp.mean(rows_new)
    update = gradient * lax.rsqrt(second)
    clipped = update / jnp.maximum(1.0, jnp.sqrt(jnp.mean(update * update)))
    scale = 0.3 * jnp.maximum(0.001, jnp.sqrt(jnp.mean(weight * weight)))
    return (rows_new, cols_new, weight - scale * clipped)

def plain_update(weight, gradient, second_old, beta_two):
    second_new = beta_two * second_old + (1.0 - beta_two) * (gradient * gradient + 1e-30)
    update = gradient * lax.rsqrt(second_new)
    clipped = update / jnp.maximum(1.0, jnp.sqrt(lax.optimization_barrier(jnp.mean(update * update, axis=-1, keepdims=True))))
    scale = 0.3 * jnp.maximum(0.001, jnp.sqrt(lax.optimization_barrier(jnp.mean(weight * weight, axis=-1, keepdims=True))))
    return (second_new, weight - scale * clipped)

def reference(hidden_in, out_grad, decays, strength, mixer_in, mixer_in_rows, mixer_in_cols, mixer_out, mixer_out_rows, mixer_out_cols, feed_in, feed_in_rows, feed_in_cols, feed_out, feed_out_rows, feed_out_cols, conv_kernel, conv_second, norm_gains, gains_second, head_gain, head_gain_second):
    beta_two = 1.0 - STEP ** (-0.8)

    def block_fn(rows_in, mix_in, mix_out, kernel, gain_heads, gains, expand, shrink):
        return block_forward(rows_in, mix_in, mix_out, kernel, gain_heads, gains, expand, shrink, decays, strength)
    block_out, pullback = jax.vjp(block_fn, hidden_in.astype(jnp.float32), mixer_in, mixer_out, conv_kernel, head_gain, norm_gains, feed_in, feed_out)
    gradients = pullback(out_grad.astype(jnp.float32))
    input_grad, grad_mix_in, grad_mix_out, grad_kernel, grad_head, grad_gains, grad_expand, grad_shrink = gradients
    head_cols = 2 * DK + 2 * DV
    in_rows, in_cols, in_new = factored_update(mixer_in.reshape(D, HEAD_TOTAL * head_cols), grad_mix_in.reshape(D, HEAD_TOTAL * head_cols), mixer_in_rows, mixer_in_cols.reshape(HEAD_TOTAL * head_cols), beta_two)
    out_rows, out_cols, out_new = factored_update(mixer_out.reshape(HEAD_TOTAL * DV, D), grad_mix_out.reshape(HEAD_TOTAL * DV, D), mixer_out_rows.reshape(HEAD_TOTAL * DV), mixer_out_cols, beta_two)
    expand_rows, expand_cols, expand_new = factored_update(feed_in.reshape(D, 2 * FF), grad_expand.reshape(D, 2 * FF), feed_in_rows, feed_in_cols.reshape(2 * FF), beta_two)
    shrink_rows, shrink_cols, shrink_new = factored_update(feed_out, grad_shrink, feed_out_rows, feed_out_cols, beta_two)
    conv_sq, conv_new = plain_update(conv_kernel.reshape(1, -1), grad_kernel.reshape(1, -1), conv_second.reshape(1, -1), beta_two)
    gains_sq, gains_new = plain_update(norm_gains, grad_gains, gains_second, beta_two)
    head_sq, head_new = plain_update(head_gain.reshape(1, -1), grad_head.reshape(1, -1), head_gain_second.reshape(1, -1), beta_two)
    return (block_out.astype(jnp.bfloat16), input_grad, grad_mix_in, in_rows, in_cols.reshape(HEAD_TOTAL, head_cols), in_new.reshape(D, HEAD_TOTAL, head_cols), grad_mix_out, out_rows.reshape(HEAD_TOTAL, DV), out_cols, out_new.reshape(HEAD_TOTAL, DV, D), grad_expand, expand_rows, expand_cols.reshape(2, FF), expand_new.reshape(D, 2, FF), grad_shrink, shrink_rows, shrink_cols, shrink_new, grad_kernel, conv_sq.reshape(conv_kernel.shape), conv_new.reshape(conv_kernel.shape), grad_gains, gains_sq, gains_new, grad_head, head_sq.reshape(DV), head_new.reshape(DV))
```

```python
import functools
import jax
import jax.numpy as jnp
from jax import lax
from jax.experimental import pallas as pl
from jax.experimental.pallas import tpu as pltpu
from jax.sharding import PartitionSpec as P

DK = 128
DV = 256
KC = 4
D = 2048
HEAD_TOTAL = 16
FF = 5632
STEP = 10
CH = 128
HC = 2 * DK + 2 * DV
CW = 2 * DK + DV
F32 = jnp.float32
BF = jnp.bfloat16


def mm(a, b, dims=((1,), (0,))):
    return lax.dot_general(a.astype(BF), b.astype(BF), (dims, ((), ())), preferred_element_type=F32)


def mm3(a, b, dims=((1,), (0,))):
    ah, bh = a.astype(BF), b.astype(BF)
    al, bl = (a - ah.astype(F32)).astype(BF), (b - bh.astype(F32)).astype(BF)
    one = functools.partial(lax.dot_general, dimension_numbers=(dims, ((), ())), preferred_element_type=F32)
    return one(ah, bh) + (one(ah, bl) + one(al, bh))


TT = ((1,), (1,))
TL = ((0,), (0,))


def sigmoid(v):
    return 1.0 / (1.0 + jnp.exp(-v))


def masks():
    rows = lax.broadcasted_iota(jnp.int32, (CH, CH), 0)
    cols = lax.broadcasted_iota(jnp.int32, (CH, CH), 1)
    return rows, cols


def invert(strict, rows, cols):
    x = jnp.where(rows == cols, 1.0, 0.0) - jnp.where((rows ^ cols) == 1, strict, 0.0)
    size = 2
    while size < CH:
        below = ((rows ^ cols) >= size) & ((rows ^ cols) < 2 * size)
        part = jnp.where(below, strict, 0.0)
        x = x - mm3(mm3(x, part), x)
        size *= 2
    return x


def k1(heads, proj_ref, halo_ref, taps_ref, gcol_ref, grow_ref,
       sum_ref, q_ref, k_ref, tinv_ref, a_ref, w_ref, uv_ref, qe_ref, oz_ref, m_ref, pre_ref, last_ref, x_ref):
    c = pl.program_id(0)
    rows, cols = masks()

    @pl.when(c == 0)
    def _():
        eye = jnp.where(rows == cols, 1.0, 0.0)
        for h in range(heads):
            x_ref[h] = jnp.concatenate([eye, jnp.zeros((CH, DV), F32)], 1)

    for h in range(heads):
        at = h * HC
        ext = jnp.concatenate([halo_ref[:, at:at + CW], proj_ref[:, at:at + CW]], 0)
        summed = taps_ref[0:1, h * CW:(h + 1) * CW] * ext[5:5 + CH]
        for j in range(1, KC):
            summed = summed + taps_ref[j:j + 1, h * CW:(h + 1) * CW] * ext[5 + j:5 + j + CH]
        sum_ref[:, h * CW:(h + 1) * CW] = summed
        act = summed * sigmoid(summed)
        q = act[:, :DK]
        k = act[:, DK:2 * DK]
        v = act[:, 2 * DK:]
        q = q * (lax.rsqrt(jnp.sum(q * q, axis=-1, keepdims=True) + 1e-6) * DK ** -0.5)
        k = k * lax.rsqrt(jnp.sum(k * k, axis=-1, keepdims=True) + 1e-6)
        gcol = gcol_ref[:, h:h + 1]
        beta = gcol_ref[:, heads + h:heads + h + 1]
        grow = grow_ref[0, h:h + 1, :]
        glast = grow[:, CH - 1:CH]
        ratio = jnp.exp(jnp.where(rows >= cols, gcol - grow, -1e30))
        kk = mm3(k, k, TT)
        strict = jnp.where(rows > cols, beta * ratio * kk, 0.0)
        tinv = invert(strict, rows, cols)
        a = ratio * mm(q, k, TT)
        eg = jnp.exp(gcol)
        kd = k * jnp.exp(glast - gcol)
        w = mm3(tinv, (beta * eg) * k)
        uv = mm3(tinv, beta * v)
        qe = q * eg - mm(a, w)
        oz = mm(a, uv)
        m = jnp.where(rows == cols, jnp.exp(glast), 0.0) - mm(kd, w, TL)
        b = mm(kd, uv, TL)
        x = x_ref[h]
        pre_ref[0, h] = x
        x = mm(m, x) + jnp.concatenate([jnp.zeros((CH, DK), F32), b], 1)
        x_ref[h] = x
        last_ref[h] = x
        q_ref[:, h * DK:(h + 1) * DK] = q.astype(BF)
        k_ref[:, h * DK:(h + 1) * DK] = k.astype(BF)
        tinv_ref[0, h] = tinv.astype(BF)
        a_ref[0, h] = a.astype(BF)
        w_ref[:, h * DK:(h + 1) * DK] = w.astype(BF)
        uv_ref[:, h * DV:(h + 1) * DV] = uv
        qe_ref[:, h * DK:(h + 1) * DK] = qe.astype(BF)
        oz_ref[:, h * DV:(h + 1) * DV] = oz
        m_ref[0, h] = m.astype(BF)


def whole(shape):
    return pl.BlockSpec(shape, lambda c: (0,) * len(shape))


def by_rows(width, n, back=False):
    return pl.BlockSpec((CH, width), (lambda c: (n - 1 - c, 0)) if back else (lambda c: (c, 0)))


def by_chunk(shape, n, back=False):
    tail = (0,) * len(shape)
    return pl.BlockSpec((1,) + shape, (lambda c: (n - 1 - c,) + tail) if back else (lambda c: (c,) + tail))


def sds(shape, dt=F32):
    return jax.ShapeDtypeStruct(shape, dt)


PARAMS = pltpu.CompilerParams(vmem_limit_bytes=48 * 1024 * 1024, dimension_semantics=("arbitrary",))


def forward_parts(proj, taps, gcol, grow, tokens, heads):
    n = tokens // CH
    extra = proj.shape[0] // 8 - 1
    halo = pl.BlockSpec((8, heads * HC), lambda c: (jnp.where(c == 0, extra, c * (CH // 8) - 1), 0))
    return pl.pallas_call(
        functools.partial(k1, heads),
        grid=(n,),
        in_specs=[by_rows(heads * HC, n), halo, whole(taps.shape), by_rows(gcol.shape[1], n),
                  by_chunk(grow.shape[1:], n)],
        out_specs=[by_rows(heads * CW, n), by_rows(heads * DK, n), by_rows(heads * DK, n),
                   by_chunk((heads, CH, CH), n), by_chunk((heads, CH, CH), n),
                   by_rows(heads * DK, n), by_rows(heads * DV, n), by_rows(heads * DK, n), by_rows(heads * DV, n),
                   by_chunk((heads, DK, DK), n), by_chunk((heads, DK, DK + DV), n), whole((heads, DK, DK + DV))],
        out_shape=[sds((tokens, heads * CW)), sds((tokens, heads * DK), BF), sds((tokens, heads * DK), BF),
                   sds((n, heads, CH, CH), BF), sds((n, heads, CH, CH), BF),
                   sds((tokens, heads * DK), BF), sds((tokens, heads * DV)), sds((tokens, heads * DK), BF),
                   sds((tokens, heads * DV)), sds((n, heads, DK, DK), BF), sds((n, heads, DK, DK + DV)),
                   sds((heads, DK, DK + DV))],
        scratch_shapes=[pltpu.VMEM((heads, DK, DK + DV), F32)],
        compiler_params=PARAMS,
        name="delta_forward_parts",
    )(proj, proj, taps, gcol, grow)


def k2(heads, start_ref, pre_ref, qe_ref, oz_ref, proj_ref, gain_ref, s_ref, o_ref, gated_ref):
    for h in range(heads):
        pre = pre_ref[0, h]
        s = mm(pre[:, :DK], start_ref[h]) + pre[:, DK:]
        s_ref[0, h] = s.astype(BF)
        o = mm(qe_ref[:, h * DK:(h + 1) * DK], s) + oz_ref[:, h * DV:(h + 1) * DV]
        o_ref[:, h * DV:(h + 1) * DV] = o
        gate = proj_ref[:, h * HC + CW:(h + 1) * HC]
        n = o * lax.rsqrt(jnp.mean(o * o, axis=-1, keepdims=True) + 1e-5)
        gated_ref[:, h * DV:(h + 1) * DV] = (n * gain_ref[...] * (gate * sigmoid(gate))).astype(BF)


def forward_outputs(start, pre, qe, oz, proj, gain, tokens, heads):
    n = tokens // CH
    return pl.pallas_call(
        functools.partial(k2, heads),
        grid=(n,),
        in_specs=[whole(start.shape), by_chunk((heads, DK, DK + DV), n), by_rows(heads * DK, n), by_rows(heads * DV, n),
                  by_rows(heads * HC, n), whole((1, DV))],
        out_specs=[by_chunk((heads, DK, DV), n), by_rows(heads * DV, n), by_rows(heads * DV, n)],
        out_shape=[sds((n, heads, DK, DV), BF), sds((tokens, heads * DV)), sds((tokens, heads * DV), BF)],
        compiler_params=PARAMS,
        name="delta_forward_outputs",
    )(start, pre, qe, oz, proj, gain)


def k3(heads, dg_ref, o_ref, proj_ref, gain_ref, qe_ref, m_ref, do_ref, dgate_ref, dc_ref, last_ref, dgain_ref, d_ref):
    c = pl.program_id(0)

    @pl.when(c == 0)
    def _():
        d_ref[...] = jnp.zeros_like(d_ref)
        dgain_ref[...] = jnp.zeros_like(dgain_ref)

    for h in range(heads):
        o = o_ref[:, h * DV:(h + 1) * DV]
        gate = proj_ref[:, h * HC + CW:(h + 1) * HC]
        dg = dg_ref[:, h * DV:(h + 1) * DV]
        gain = gain_ref[...]
        rstd = lax.rsqrt(jnp.mean(o * o, axis=-1, keepdims=True) + 1e-5)
        n = o * rstd
        sg = sigmoid(gate)
        act = gate * sg
        dgain_ref[...] += jnp.sum(dg * n * act, axis=0, keepdims=True)
        dgate_ref[:, h * DV:(h + 1) * DV] = (dg * n * gain * (sg * (1.0 + gate * (1.0 - sg)))).astype(BF)
        dn = dg * gain * act
        do = rstd * (dn - n * jnp.mean(dn * n, axis=-1, keepdims=True))
        do_ref[:, h * DV:(h + 1) * DV] = do.astype(BF)
        dc = mm(qe_ref[:, h * DK:(h + 1) * DK], do, TL)
        dc_ref[0, h] = dc
        d = mm(m_ref[0, h], d_ref[h], TL) + dc
        d_ref[h] = d
        last_ref[h] = d


def backward_states(dgated, o, proj, gain, qe, m, tokens, heads):
    n = tokens // CH
    return pl.pallas_call(
        functools.partial(k3, heads),
        grid=(n,),
        in_specs=[by_rows(heads * DV, n, True), by_rows(heads * DV, n, True), by_rows(heads * HC, n, True),
                  whole((1, DV)), by_rows(heads * DK, n, True), by_chunk((heads, DK, DK), n, True)],
        out_specs=[by_rows(heads * DV, n, True), by_rows(heads * DV, n, True), by_chunk((heads, DK, DV), n, True),
                   whole((heads, DK, DV)), whole((1, DV))],
        out_shape=[sds((tokens, heads * DV), BF), sds((tokens, heads * DV), BF), sds((n, heads, DK, DV)),
                   sds((heads, DK, DV)), sds((1, DV))],
        scratch_shapes=[pltpu.VMEM((heads, DK, DV), F32)],
        compiler_params=PARAMS,
        name="delta_backward_states",
    )(dgated, o, proj, gain, qe, m)


def normed_pull(raw, grad, scale):
    r = lax.rsqrt(jnp.sum(raw * raw, axis=-1, keepdims=True) + 1e-6)
    n = raw * r
    return (scale * r) * (grad - n * jnp.sum(grad * n, axis=-1, keepdims=True))


def k4(heads, end_ref, dc_ref, m_ref, s_ref, do_ref, uv_ref, w_ref, a_ref, tinv_ref, q_ref, k_ref, sum_ref, proj_ref,
       dgate_ref, halo_ref, taps_ref, gcol_ref, grow_ref, dproj_ref, dhalo_ref, dtaps_ref, ds_ref, rim_ref):
    c = pl.program_id(0)
    last = pl.num_programs(0) - 1
    rows, cols = masks()

    @pl.when(c == 0)
    def _():
        ds_ref[...] = end_ref[...]
        rim_ref[...] = jnp.zeros_like(rim_ref)
        dtaps_ref[...] = jnp.zeros_like(dtaps_ref)

    for h in range(heads):
        ds = ds_ref[h]
        s = s_ref[0, h]
        do = do_ref[:, h * DV:(h + 1) * DV]
        q = q_ref[:, h * DK:(h + 1) * DK]
        k = k_ref[:, h * DK:(h + 1) * DK]
        a = a_ref[0, h]
        gcol = gcol_ref[:, h:h + 1]
        beta = gcol_ref[:, heads + h:heads + h + 1]
        grow = grow_ref[0, h:h + 1, :]
        glast = grow[:, CH - 1:CH]
        ratio = jnp.exp(jnp.where(rows >= cols, gcol - grow, -1e30))
        eg = jnp.exp(gcol)
        el = jnp.exp(glast - gcol)
        u = uv_ref[:, h * DV:(h + 1) * DV] - mm(w_ref[:, h * DK:(h + 1) * DK], s)
        du = mm(a, do, TL) + el * mm(k, ds)
        da = ratio * mm(do, u, TT)
        drv = mm(tinv_ref[0, h], du, TL)
        drk = mm(drv, s, TT)
        dl = jnp.where(rows > cols, (-beta) * ratio * mm(drv, u, TT), 0.0)
        dq = eg * mm(do, s, TT) + mm(da, k)
        dk = el * mm(u, ds, TT) + mm(da, q, TL) - (beta * eg) * drk + mm(dl, k) + mm(dl, k, TL)
        dv = beta * drv
        ds_ref[h] = mm(m_ref[0, h], ds, TL) + dc_ref[0, h]
        summed = sum_ref[:, h * CW:(h + 1) * CW]
        sg = sigmoid(summed)
        act = summed * sg
        dact = jnp.concatenate(
            [normed_pull(act[:, :DK], dq, DK ** -0.5), normed_pull(act[:, DK:2 * DK], dk, 1.0), dv], 1)
        dsum = dact * (sg * (1.0 + summed * (1.0 - sg)))
        rim = rim_ref[:, h * CW:(h + 1) * CW]
        ext = jnp.concatenate([dsum, rim], 0)
        rim_ref[:, h * CW:(h + 1) * CW] = dsum[:8]
        conv_in = proj_ref[:, h * HC:h * HC + CW]
        dconv = jnp.zeros((CH, CW), F32)
        for j in range(KC):
            moved = ext[3 - j:3 - j + CH]
            dconv = dconv + taps_ref[j:j + 1, h * CW:(h + 1) * CW] * moved
            dtaps_ref[j:j + 1, h * CW:(h + 1) * CW] += jnp.sum(moved * conv_in, axis=0, keepdims=True)
        dproj_ref[:, h * HC:h * HC + CW] = dconv.astype(BF)
        dproj_ref[:, h * HC + CW:(h + 1) * HC] = dgate_ref[:, h * DV:(h + 1) * DV]

        @pl.when(c == last)
        def _():
            before = jnp.concatenate([jnp.zeros((8, CW), F32), dsum[:8]], 0)
            conv_halo = halo_ref[:, h * HC:h * HC + CW]
            dhalo = jnp.zeros((8, CW), F32)
            for j in range(KC):
                moved = before[3 - j:3 - j + 8]
                dhalo = dhalo + taps_ref[j:j + 1, h * CW:(h + 1) * CW] * moved
                dtaps_ref[j:j + 1, h * CW:(h + 1) * CW] += jnp.sum(moved * conv_halo, axis=0, keepdims=True)
            dhalo_ref[:, h * HC:h * HC + CW] = jnp.concatenate([jnp.zeros((8, CW), F32), dhalo], 0).astype(BF)
            dhalo_ref[:, h * HC + CW:(h + 1) * HC] = jnp.zeros((16, DV), BF)


def backward_inputs(end, dc, m, s, do, uv, w, a, tinv, q, k, summed, proj, dgate, taps, gcol, grow, tokens, heads):
    n = tokens // CH
    extra = proj.shape[0] // 8 - 1
    rows = functools.partial(by_rows, n=n, back=True)
    chunk = functools.partial(by_chunk, n=n, back=True)
    return pl.pallas_call(
        functools.partial(k4, heads),
        grid=(n,),
        in_specs=[whole((heads, DK, DV)), chunk((heads, DK, DV)), chunk((heads, DK, DK)), chunk((heads, DK, DV)),
                  rows(heads * DV), rows(heads * DV), rows(heads * DK), chunk((heads, CH, CH)), chunk((heads, CH, CH)),
                  rows(heads * DK), rows(heads * DK), rows(heads * CW), rows(heads * HC), rows(heads * DV),
                  pl.BlockSpec((8, heads * HC), lambda c: (extra, 0)), whole(taps.shape),
                  rows(gcol.shape[1]), chunk(grow.shape[1:])],
        out_specs=[rows(heads * HC), whole((16, heads * HC)), whole(taps.shape)],
        out_shape=[sds((tokens, heads * HC), BF), sds((16, heads * HC), BF), sds(taps.shape)],
        scratch_shapes=[pltpu.VMEM((heads, DK, DV), F32), pltpu.VMEM((8, heads * CW), F32)],
        compiler_params=PARAMS,
        name="delta_backward_inputs",
    )(end, dc, m, s, do, uv, w, a, tinv, q, k, summed, proj, dgate, proj, taps, gcol, grow)


def passed_along(x, by):
    count = lax.axis_size("seq")
    return lax.ppermute(x, "seq", [(i, i + by) for i in range(count) if 0 <= i + by < count])


def gather_seq(x, axis=0):
    return lax.all_gather(x, "seq", axis=axis, tiled=True)


def gather_head(x, axis=0):
    return lax.all_gather(x, "head", axis=axis, tiled=True)


def scatter_seq(x, axis=0):
    return lax.psum_scatter(x, "seq", scatter_dimension=axis, tiled=True).astype(F32)


def scatter_head(x, axis=0):
    return lax.psum_scatter(x, "head", scatter_dimension=axis, tiled=True).astype(F32)


def dot(a, b, dims=((1,), (0,)), out=F32):
    return lax.dot_general(a, b, (dims, ((), ())), preferred_element_type=out)


def norm_rows(entries, scale_row):
    return entries * lax.rsqrt(jnp.mean(entries * entries, axis=-1, keepdims=True) + 1e-06) * scale_row


def chain(first, offsets, maps, backward):
    count = lax.axis_size("seq")
    here = lax.axis_index("seq")
    state = jnp.zeros(offsets[0].shape, F32)
    found = state
    order = range(count - 1, 0, -1) if backward else range(count - 1)
    for i in order:
        dims = ((1,), (1,)) if backward else ((2,), (1,))
        moved = lax.dot_general(maps[i], state.astype(BF), (dims, ((0,), (0,))), preferred_element_type=F32)
        state = moved + offsets[i].astype(F32)
        found = jnp.where(here == (i - 1 if backward else i + 1), state, found)
    return found


def plain_update(weight, gradient, second_old, beta_two):
    second_new = beta_two * second_old + (1.0 - beta_two) * (gradient * gradient + 1e-30)
    update = gradient * lax.rsqrt(second_new)
    clipped = update / jnp.maximum(1.0, jnp.sqrt(jnp.mean(update * update, axis=-1, keepdims=True)))
    scale = 0.3 * jnp.maximum(0.001, jnp.sqrt(jnp.mean(weight * weight, axis=-1, keepdims=True)))
    return (second_new, weight - scale * clipped)


def finished(weight, update, weight_total, update_total, entry_count):
    scale = 0.3 * jnp.maximum(0.001, jnp.sqrt(weight_total / entry_count))
    return weight - update * (scale / jnp.maximum(1.0, jnp.sqrt(update_total / entry_count)))


def local(
    hidden_in,
    out_grad,
    decays,
    strength,
    mixer_in,
    mixer_in_rows,
    mixer_in_cols,
    mixer_out,
    mixer_out_rows,
    mixer_out_cols,
    feed_in,
    feed_in_rows,
    feed_in_cols,
    feed_out,
    feed_out_rows,
    feed_out_cols,
    conv_kernel,
    conv_second,
    norm_gains,
    gains_second,
    head_gain,
    head_gain_second,
):
    beta_two = 1.0 - STEP ** (-0.8)
    tokens, heads = decays.shape
    blocks = tokens // CH
    in_span, in_width = mixer_in.shape[0], heads * HC
    out_span = mixer_out.shape[2]
    feed_span, hidden_span = feed_in.shape[0], feed_in.shape[2]
    x = hidden_in.astype(F32)

    taps = gather_seq(conv_kernel.astype(BF), 2).astype(F32).reshape(KC, heads * CW)
    in_w = gather_seq(mixer_in.astype(BF).reshape(in_span, in_width))
    rows_all = gather_head(norm_rows(x, norm_gains[0]).astype(BF))
    out_w = gather_seq(mixer_out.astype(BF).reshape(heads * DV, out_span), 1)
    grad_rows = gather_seq(out_grad)
    expand = gather_head(feed_in.astype(BF).reshape(feed_span, 2 * hidden_span))
    shrink = gather_head(feed_out.astype(BF), 1)

    log_sum = jnp.cumsum(jnp.log(decays).reshape(blocks, CH, heads), axis=1)
    gcol = jnp.concatenate([log_sum.reshape(tokens, heads), strength, jnp.zeros((tokens, 8 - 2 * heads), F32)], 1)
    grow = jnp.concatenate([jnp.swapaxes(log_sum, 1, 2), jnp.zeros((blocks, 8 - heads, CH), F32)], 1)
    gain_row = head_gain[None]
    rows_more = jnp.concatenate([rows_all, passed_along(rows_all[tokens - 16 :], 1)], 0)
    proj = dot(rows_more, in_w)
    (summed, q, k, tinv, scores, w, uv, qe, oz, m, pre, last) = forward_parts(proj, taps, gcol, grow, tokens, heads)
    all_last = lax.all_gather(last.astype(BF), "seq", axis=0)
    maps, offsets = all_last[..., :DK], all_last[..., DK:]
    start = chain(0, offsets, maps, False)
    states, o, gated = forward_outputs(start, pre, qe, oz, proj, gain_row, tokens, heads)
    mixed = scatter_head(dot(gated, out_w, out=BF))
    residual = x + mixed

    normed_two, norm_two_pull = jax.vjp(norm_rows, residual, norm_gains[1])
    feed_rows = gather_seq(normed_two.astype(BF))
    gate_up = dot(feed_rows, expand)
    gate, up = gate_up[:, :hidden_span], gate_up[:, hidden_span:]
    sig = 1.0 / (1.0 + jnp.exp(-gate))
    silu = gate * sig
    hidden = (silu * up).astype(BF)
    d_hidden = dot(grad_rows, shrink, ((1,), (1,)))
    d_gate_up = jnp.concatenate(
        [d_hidden * up * (sig * (1.0 + gate * (1.0 - sig))), d_hidden * silu], 1
    ).astype(BF)
    d_normed_two = scatter_seq(dot(d_gate_up, expand, ((1,), (1,)), BF))
    d_residual_part, d_gain_two = norm_two_pull(d_normed_two)
    d_residual = out_grad.astype(F32) + d_residual_part
    d_rows = gather_head(d_residual.astype(BF))

    d_gated = dot(d_rows, out_w, ((1,), (1,)))
    do, d_gate, dc, d_last, d_head_gain = backward_states(d_gated, o, proj, gain_row, qe, m, tokens, heads)
    end = chain(0, lax.all_gather(d_last.astype(BF), "seq", axis=0), maps, True)
    d_proj, d_halo, d_taps = backward_inputs(
        end, dc, m, states, do, uv, w, scores, tinv, q, k, summed, proj, d_gate, taps, gcol, grow, tokens, heads
    )
    d_proj_more = jnp.concatenate([d_proj, d_halo], 0)
    in_grad = scatter_seq(dot(rows_more, d_proj_more, ((0,), (0,)), BF))
    d_rows_more = dot(d_proj_more, in_w, ((1,), (1,)), BF)
    rim = passed_along(d_rows_more[tokens:], -1)
    d_rows_in = jnp.concatenate([d_rows_more[: tokens - 16], d_rows_more[tokens - 16 : tokens] + rim], 0)
    d_normed = scatter_head(d_rows_in)
    feed_sum = scatter_seq(dot(hidden, shrink, out=BF))
    block_out = (residual + feed_sum).astype(BF)
    out_g = scatter_seq(dot(gated, d_rows, ((0,), (0,)), BF), 1)
    expand_g = scatter_head(dot(feed_rows, d_gate_up, ((0,), (0,)), BF))
    shrink_g = scatter_head(dot(hidden, grad_rows, ((0,), (0,)), BF), 1)
    kernel_grad = scatter_seq(d_taps.reshape(KC, heads, CW).astype(BF), 2)

    _, norm_one_pull = jax.vjp(norm_rows, x, norm_gains[0])
    d_residual_one, d_gain_one = norm_one_pull(d_normed)
    input_grad = d_residual + d_residual_one

    in_sq, out_sq, expand_sq, shrink_sq = in_grad * in_grad, out_g * out_g, expand_g * expand_g, shrink_g * shrink_g
    over_head = jnp.concatenate(
        [
            jnp.sum(in_sq, 1),
            jnp.sum(out_sq, 0),
            jnp.sum(expand_sq, 0),
            jnp.sum(shrink_sq, 1),
        ]
    )
    over_seq = jnp.concatenate(
        [
            jnp.sum(in_sq, 0),
            jnp.sum(out_sq, 1),
            jnp.sum(expand_sq, 1),
            jnp.sum(shrink_sq, 0),
        ]
    )
    over_head = lax.psum(over_head, "head")
    over_seq = lax.psum(over_seq, "seq")

    def cut(vector, sizes):
        at = 0
        pieces = []
        for size in sizes:
            pieces.append(vector[at : at + size])
            at += size
        return pieces

    in_rows_sq, out_cols_sq, expand_cols_sq, shrink_rows_sq = cut(
        over_head, (in_span, out_span, 2 * hidden_span, hidden_span)
    )
    in_cols_sq, out_rows_sq, expand_rows_sq, shrink_cols_sq = cut(
        over_seq, (in_width, heads * DV, feed_span, feed_span)
    )
    in_count = (D, HEAD_TOTAL * HC)
    out_count = (HEAD_TOTAL * DV, D)
    expand_count = (D, 2 * FF)
    shrink_count = (FF, D)

    def moment(old, squares, over):
        return beta_two * old.reshape(-1) + (1.0 - beta_two) * (squares / over + 1e-30)

    in_rows_new = moment(mixer_in_rows, in_rows_sq, in_count[1])
    in_cols_new = moment(mixer_in_cols, in_cols_sq, in_count[0])
    out_rows_new = moment(mixer_out_rows, out_rows_sq, out_count[1])
    out_cols_new = moment(mixer_out_cols, out_cols_sq, out_count[0])
    expand_rows_new = moment(feed_in_rows, expand_rows_sq, expand_count[1])
    expand_cols_new = moment(feed_in_cols, expand_cols_sq, expand_count[0])
    shrink_rows_new = moment(feed_out_rows, shrink_rows_sq, shrink_count[1])
    shrink_cols_new = moment(feed_out_cols, shrink_cols_sq, shrink_count[0])
    in_upd = in_grad * (lax.rsqrt(in_rows_new)[:, None] * lax.rsqrt(in_cols_new)[None])
    out_upd = out_g * (lax.rsqrt(out_rows_new)[:, None] * lax.rsqrt(out_cols_new)[None])
    expand_upd = expand_g * (lax.rsqrt(expand_rows_new)[:, None] * lax.rsqrt(expand_cols_new)[None])
    shrink_upd = shrink_g * (lax.rsqrt(shrink_rows_new)[:, None] * lax.rsqrt(shrink_cols_new)[None])
    conv_second_new = beta_two * conv_second + (1.0 - beta_two) * (kernel_grad * kernel_grad + 1e-30)
    conv_update = kernel_grad * lax.rsqrt(conv_second_new)
    seq_count, head_count = lax.axis_size("seq"), lax.axis_size("head")
    scalars = jnp.stack(
        [
            jnp.sum(in_upd * in_upd),
            jnp.sum(out_upd * out_upd),
            jnp.sum(expand_upd * expand_upd),
            jnp.sum(shrink_upd * shrink_upd),
            jnp.sum(conv_update * conv_update),
            jnp.sum(mixer_in * mixer_in),
            jnp.sum(mixer_out * mixer_out),
            jnp.sum(feed_in * feed_in),
            jnp.sum(feed_out * feed_out),
            jnp.sum(conv_kernel * conv_kernel),
            jnp.sum(in_rows_new) / head_count,
            jnp.sum(out_rows_new) / seq_count,
            jnp.sum(expand_rows_new) / seq_count,
            jnp.sum(shrink_rows_new) / head_count,
        ]
    )
    late = jnp.concatenate([d_gain_one, d_gain_two, d_head_gain[0], scalars])
    late = lax.psum(lax.psum(late, "head"), "seq")
    gains_grad = late[: 2 * D].reshape(2, D)
    head_gain_grad = late[2 * D : 2 * D + DV]
    totals = late[2 * D + DV :]

    def stepped(weight, update, count, slot, shape):
        mean = totals[10 + slot] / count[0]
        entries = count[0] * count[1]
        scale = 0.3 * jnp.maximum(0.001, jnp.sqrt(totals[5 + slot] / entries))
        scale = scale * jnp.sqrt(mean) / jnp.maximum(1.0, jnp.sqrt(totals[slot] * mean / entries))
        return weight - scale * update.reshape(shape)

    in_new = stepped(mixer_in, in_upd, in_count, 0, mixer_in.shape)
    out_new = stepped(mixer_out, out_upd, out_count, 1, mixer_out.shape)
    expand_new = stepped(feed_in, expand_upd, expand_count, 2, feed_in.shape)
    shrink_new = stepped(feed_out, shrink_upd, shrink_count, 3, feed_out.shape)
    conv_new = finished(conv_kernel, conv_update, totals[9], totals[4], KC * HEAD_TOTAL * CW)
    gains_second_new, gains_new = plain_update(norm_gains, gains_grad, gains_second, beta_two)
    head_second_new, head_new = plain_update(
        head_gain[None], head_gain_grad[None], head_gain_second[None], beta_two
    )
    return (
        block_out,
        input_grad,
        in_grad.reshape(mixer_in.shape),
        in_rows_new,
        in_cols_new.reshape(mixer_in_cols.shape),
        in_new,
        out_g.reshape(mixer_out.shape),
        out_rows_new.reshape(mixer_out_rows.shape),
        out_cols_new,
        out_new,
        expand_g.reshape(feed_in.shape),
        expand_rows_new,
        expand_cols_new.reshape(feed_in_cols.shape),
        expand_new,
        shrink_g,
        shrink_rows_new,
        shrink_cols_new,
        shrink_new,
        kernel_grad,
        conv_second_new,
        conv_new,
        gains_grad,
        gains_second_new,
        gains_new,
        head_gain_grad,
        head_second_new[0],
        head_new[0],
    )


def solution(mesh):
    return jax.shard_map(
        local,
        mesh=mesh,
        in_specs=(
            P(("seq", "head"), None),
            P(("seq", "head"), None),
            P("seq", "head"),
            P("seq", "head"),
            P("seq", "head", None),
            P("seq"),
            P("head", None),
            P("head", None, "seq"),
            P("head", None),
            P("seq"),
            P("head", None, "seq"),
            P("head"),
            P(None, "seq"),
            P("seq", "head"),
            P("seq"),
            P("head"),
            P(None, "head", "seq"),
            P(None, "head", "seq"),
            P(),
            P(),
            P(),
            P(),
        ),
        out_specs=(
            P(("seq", "head"), None),
            P(("seq", "head"), None),
            P("seq", "head", None),
            P("seq"),
            P("head", None),
            P("seq", "head", None),
            P("head", None, "seq"),
            P("head", None),
            P("seq"),
            P("head", None, "seq"),
            P("head", None, "seq"),
            P("head"),
            P(None, "seq"),
            P("head", None, "seq"),
            P("seq", "head"),
            P("seq"),
            P("head"),
            P("seq", "head"),
            P(None, "head", "seq"),
            P(None, "head", "seq"),
            P(None, "head", "seq"),
            P(),
            P(),
            P(),
            P(),
            P(),
            P(),
        ),
        check_vma=False,
    )
```

```python
import functools
import jax
import jax.numpy as jnp
import numpy as np
from jax import lax
from jax.experimental import pallas as pl
from jax.experimental.pallas import tpu as pltpu
from jax.sharding import PartitionSpec as P

D = 2048
HEAD_TOTAL = 16
DK = 128
DV = 256
FF = 5632
KC = 4
STEP = 10
CH = 128
RIM = 16
HC = 2 * DK + 2 * DV
CW = 2 * DK + DV
F32 = jnp.float32
BF = jnp.bfloat16
TT = ((1,), (1,))
TL = ((0,), (0,))


def mm(a, b, dims=((1,), (0,))):
    return lax.dot_general(a.astype(BF), b.astype(BF), (dims, ((), ())), preferred_element_type=F32)


def mm3(a, b, dims=((1,), (0,))):
    ah, bh = a.astype(BF), b.astype(BF)
    al, bl = (a - ah.astype(F32)).astype(BF), (b - bh.astype(F32)).astype(BF)
    one = functools.partial(lax.dot_general, dimension_numbers=(dims, ((), ())), preferred_element_type=F32)
    return one(ah, bh) + (one(ah, bl) + one(al, bh))


def sigmoid(v):
    return 1.0 / (1.0 + jnp.exp(-v))


def square_index():
    rows = lax.broadcasted_iota(jnp.int32, (CH, CH), 0)
    cols = lax.broadcasted_iota(jnp.int32, (CH, CH), 1)
    return rows, cols


def invert(strict, rows, cols):
    apart = rows ^ cols
    xs = [jnp.where(rows == cols, 1.0, 0.0) - jnp.where(apart == 1, s, 0.0) for s in strict]
    size = 2
    while size < CH:
        here = (apart >= size) & (apart < 2 * size)
        left = [mm3(x, jnp.where(here, s, 0.0)) for x, s in zip(xs, strict)]
        xs = [x - mm3(y, x) for x, y in zip(xs, left)]
        size *= 2
    return xs


PER = 2


def parts_kernel(heads, p_ref, halo_ref, first_ref, taps_ref, gcol_ref, grow_ref,
                 sum_ref, q_ref, k_ref, tinv_ref, a_ref, w_ref, uv_ref, qe_ref, oz_ref, m_ref, pre_ref, last_ref, x_ref):
    rows, cols = square_index()
    eye = jnp.where(rows == cols, 1.0, 0.0)
    width = heads * DV

    @pl.when(pl.program_id(0) == 0)
    def _():
        for h in range(heads):
            x_ref[h] = jnp.concatenate([eye, jnp.zeros((DK, DV), F32)], 1)

    def convolved(at, size):
        before = jnp.where(pl.program_id(0) == 0, first_ref[RIM - 8:, at:at + size], halo_ref[:, at:at + size])
        ext = jnp.concatenate([before, p_ref[:, at:at + size]], 0)
        summed = taps_ref[0:1, at:at + size] * ext[5:5 + PER * CH]
        for j in range(1, KC):
            summed = summed + taps_ref[j:j + 1, at:at + size] * ext[5 + j:5 + j + PER * CH]
        sum_ref[:, at:at + size] = summed
        return summed * sigmoid(summed)

    stricts, held = [], []
    for h in range(heads):
        act = convolved(2 * h * DK, 2 * DK)
        values = convolved(width + h * DV, DV)
        for c in range(PER):
            at = slice(c * CH, (c + 1) * CH)
            q, k = act[at, :DK], act[at, DK:]
            q = q * (lax.rsqrt(jnp.sum(q * q, axis=-1, keepdims=True) + 1e-6) * DK ** -0.5)
            k = k * lax.rsqrt(jnp.sum(k * k, axis=-1, keepdims=True) + 1e-6)
            gcol, beta = gcol_ref[at, h:h + 1], gcol_ref[at, heads + h:heads + h + 1]
            grow = grow_ref[c, h:h + 1, :]
            ratio = jnp.exp(jnp.where(rows >= cols, gcol - grow, -1e30))
            stricts.append(jnp.where(rows > cols, beta * ratio * mm3(k, k, TT), 0.0))
            held.append((h, c, q, k, values[at], ratio, gcol, beta, grow[:, CH - 1:CH]))
    for (h, c, q, k, v, ratio, gcol, beta, glast), tinv in zip(held, invert(stricts, rows, cols)):
        at, key, val = slice(c * CH, (c + 1) * CH), slice(h * DK, (h + 1) * DK), slice(h * DV, (h + 1) * DV)
        eg = jnp.exp(gcol)
        kd = k * jnp.exp(glast - gcol)
        a = ratio * mm(q, k, TT)
        w = mm3(tinv, (beta * eg) * k)
        uv = mm3(tinv, beta * v)
        m = jnp.exp(glast) * eye - mm(kd, w, TL)
        x = x_ref[h]
        pre_ref[c, h] = x
        x = mm(m, x) + jnp.concatenate([jnp.zeros((DK, DK), F32), mm(kd, uv, TL)], 1)
        x_ref[h] = x
        last_ref[h] = x.astype(BF)
        q_ref[at, key] = q.astype(BF)
        k_ref[at, key] = k.astype(BF)
        tinv_ref[c, h] = tinv.astype(BF)
        a_ref[c, h] = a.astype(BF)
        w_ref[at, key] = w.astype(BF)
        uv_ref[at, val] = uv
        qe_ref[at, key] = (q * eg - mm(a, w)).astype(BF)
        oz_ref[at, val] = mm(a, uv)
        m_ref[c, h] = m.astype(BF)


def whole(shape):
    return pl.BlockSpec(shape, lambda c: (0,) * len(shape))


def by_rows(width, n, back=False):
    return pl.BlockSpec((CH, width), (lambda c: (n - 1 - c, 0)) if back else (lambda c: (c, 0)))


def by_chunk(shape, n, back=False):
    tail = (0,) * len(shape)
    return pl.BlockSpec((1,) + shape, (lambda c: (n - 1 - c,) + tail) if back else (lambda c: (c,) + tail))


def sds(shape, dt=F32):
    return jax.ShapeDtypeStruct(shape, dt)


def call(kernel, name, n, micros, ins, outs, scratch, *operands, room=48):
    return pl.pallas_call(
        kernel,
        grid=(n,),
        in_specs=ins,
        out_specs=[spec for spec, _ in outs],
        out_shape=[shape for _, shape in outs],
        scratch_shapes=scratch,
        compiler_params=pltpu.CompilerParams(
            vmem_limit_bytes=room * 1024 * 1024, dimension_semantics=("arbitrary",)
        ),
        cost_estimate=pl.CostEstimate(flops=micros * 10**5, bytes_accessed=micros * 10**3, transcendentals=0),
        name=name,
    )(*operands)


def delta_parts(p, first, taps, gcol, grow, tokens, heads):
    n, span, width = tokens // CH, PER * CH, heads * DV

    def rows(size, dt=F32):
        return pl.BlockSpec((span, size), lambda c: (c, 0)), sds((tokens, size), dt)

    def chunk(shape, dt=F32):
        tail = (0,) * len(shape)
        return pl.BlockSpec((PER,) + shape, lambda c: (c,) + tail), sds((n,) + shape, dt)

    halo = pl.BlockSpec((8, 2 * width), lambda c: (jnp.maximum(c * (span // 8) - 1, 0), 0))
    return call(
        functools.partial(parts_kernel, heads), "delta_parts", n // PER, 35 * tokens // 1024,
        [rows(2 * width)[0], halo, whole(first.shape), whole(taps.shape), rows(gcol.shape[1])[0], chunk(grow.shape[1:])[0]],
        [rows(2 * width), rows(heads * DK, BF), rows(heads * DK, BF), chunk((heads, CH, CH), BF), chunk((heads, CH, CH), BF),
         rows(heads * DK, BF), rows(width), rows(heads * DK, BF), rows(width), chunk((heads, DK, DK), BF),
         chunk((heads, DK, DK + DV)), (whole((heads, DK, DK + DV)), sds((heads, DK, DK + DV), BF))],
        [pltpu.VMEM((heads, DK, DK + DV), F32)],
        p, p, first, taps, gcol, grow,
    )


def entering(near, h, dims):
    state = near[-1][h].astype(F32)
    for found in near[-2::-1]:
        state = mm(found[h, :, :DK], state, dims) + found[h, :, DK:].astype(F32)
    return state


def outputs_kernel(heads, count, rows_before, pre_ref, qe_ref, oz_ref, gate_ref, gain_ref, *refs):
    near, slots, (s_ref, o_ref, gated_ref, mixed_ref, start_ref) = refs[:count], refs[count:-5], refs[-5:]

    @pl.when(pl.program_id(0) == 0)
    def _():
        for h in range(heads):
            start_ref[h] = entering(near, h, ((1,), (0,)))

    for h in range(heads):
        at = slice(h * DV, (h + 1) * DV)
        pre = pre_ref[0, h]
        s = mm(pre[:, :DK], start_ref[h]) + pre[:, DK:]
        s_ref[0, h] = s.astype(BF)
        o = mm(qe_ref[:, h * DK:(h + 1) * DK], s) + oz_ref[:, at]
        o_ref[:, at] = o
        gate = gate_ref[:, at]
        n = o * lax.rsqrt(jnp.mean(o * o, axis=-1, keepdims=True) + 1e-5)
        gated_ref[:, at] = (n * gain_ref[...] * (gate * sigmoid(gate))).astype(BF)
    gated = gated_ref[...]
    size = slots[0].shape[0] - rows_before
    for i, slot in enumerate(slots):
        mixed_ref[:, i * size:(i + 1) * size] = mm(gated, slot[rows_before:], TT).astype(BF)


def delta_outputs(near, slots, pre, qe, oz, gate, gain, rows_before, tokens, heads):
    n = tokens // CH
    wide = by_rows(heads * DV, n)
    size = len(slots) * (slots[0].shape[0] - rows_before)
    return call(
        functools.partial(outputs_kernel, heads, len(near), rows_before), "delta_outputs", n, 7 * tokens // 1024,
        [by_chunk((heads, DK, DK + DV), n), by_rows(heads * DK, n), wide, wide, whole((1, DV))]
        + [whole(a.shape) for a in (*near, *slots)],
        [(by_chunk((heads, DK, DV), n), sds((n, heads, DK, DV), BF)), (wide, sds((tokens, heads * DV))),
         (wide, sds((tokens, heads * DV), BF)), (by_rows(size, n), sds((tokens, size), BF))],
        [pltpu.VMEM((heads, DK, DV), F32)],
        pre, qe, oz, gate, gain, *near, *slots,
    )


def states_back_kernel(heads, drows_ref, out_ref, o_ref, gate_ref, gain_ref, qe_ref, m_ref, map_ref,
                       do_ref, dgate_ref, dc_ref, last_ref, dgain_ref, d_ref):
    @pl.when(pl.program_id(0) == 0)
    def _():
        d_ref[...] = jnp.zeros_like(d_ref)
        dgain_ref[...] = jnp.zeros_like(dgain_ref)
        last_ref[:, :, :DK] = map_ref[:, :, :DK]

    dgated = mm(drows_ref[...], out_ref[...])
    for h in range(heads):
        at = slice(h * DV, (h + 1) * DV)
        o, gate, dg, gain = o_ref[:, at], gate_ref[:, at], dgated[:, at], gain_ref[...]
        rstd = lax.rsqrt(jnp.mean(o * o, axis=-1, keepdims=True) + 1e-5)
        n = o * rstd
        sg = sigmoid(gate)
        act = gate * sg
        dgain_ref[...] += jnp.sum(dg * n * act, axis=0, keepdims=True)
        dgate_ref[:, at] = (dg * n * gain * (sg * (1.0 + gate * (1.0 - sg)))).astype(BF)
        dn = dg * gain * act
        do = rstd * (dn - n * jnp.mean(dn * n, axis=-1, keepdims=True))
        do_ref[:, at] = do.astype(BF)
        dc = mm(qe_ref[:, h * DK:(h + 1) * DK], do, TL)
        dc_ref[0, h] = dc
        d = mm(m_ref[0, h], d_ref[h], TL) + dc
        d_ref[h] = d
        last_ref[h, :, DK:] = d.astype(BF)


def delta_states_back(drows, out_t, o, gate, gain, qe, m, last, tokens, heads):
    n = tokens // CH
    wide = by_rows(heads * DV, n, True)
    return call(
        functools.partial(states_back_kernel, heads), "delta_states_back", n, 7 * tokens // 1024,
        [by_rows(drows.shape[1], n, True), whole(out_t.shape), wide, wide, whole((1, DV)), by_rows(heads * DK, n, True), by_chunk((heads, DK, DK), n, True),
         whole(last.shape)],
        [(wide, sds((tokens, heads * DV), BF)), (wide, sds((tokens, heads * DV), BF)),
         (by_chunk((heads, DK, DV), n, True), sds((n, heads, DK, DV))),
         (whole(last.shape), sds(last.shape, BF)), (whole((1, DV)), sds((1, DV)))],
        [pltpu.VMEM((heads, DK, DV), F32)],
        drows, out_t, o, gate, gain, qe, m, last,
    )


def normed_pull(raw, grad, scale):
    r = lax.rsqrt(jnp.sum(raw * raw, axis=-1, keepdims=True) + 1e-6)
    n = raw * r
    return (scale * r) * (grad - n * jnp.sum(grad * n, axis=-1, keepdims=True))


def conv_back(dact, at, width, sum_ref, in_ref, taps_ref, out_ref, dtaps_ref, rim_ref):
    where = slice(at, at + width)
    summed = sum_ref[:, where]
    sg = sigmoid(summed)
    dsum = dact * (sg * (1.0 + summed * (1.0 - sg)))
    ext = jnp.concatenate([dsum, rim_ref[:, where]], 0)
    rim_ref[:, where] = dsum[:8]
    conv_in = in_ref[:, where]
    dconv = jnp.zeros((CH, width), F32)
    for j in range(KC):
        moved = ext[3 - j:3 - j + CH]
        dconv = dconv + taps_ref[j:j + 1, where] * moved
        dtaps_ref[j:j + 1, where] += jnp.sum(moved * conv_in, axis=0, keepdims=True)
    out_ref[:, where] = dconv.astype(BF)


def rim_back(first_ref, taps_ref, out_ref, out_at, dtaps_ref, rim_ref):
    before = jnp.concatenate([jnp.zeros_like(rim_ref), rim_ref[...]], 0)
    conv_in = first_ref[RIM - 8:]
    drim = jnp.zeros(rim_ref.shape, F32)
    for j in range(KC):
        moved = before[3 - j:3 - j + 8]
        drim = drim + taps_ref[j:j + 1] * moved
        dtaps_ref[j:j + 1] += jnp.sum(moved * conv_in, axis=0, keepdims=True)
    width = rim_ref.shape[1]
    out_ref[:RIM, out_at:out_at + width] = jnp.concatenate([jnp.zeros_like(drim), drim], 0).astype(BF)


def inputs_back_kernel(heads, dc_ref, m_ref, s_ref, do_ref, uv_ref, w_ref, a_ref, tinv_ref, q_ref, k_ref,
                       sum_ref, p_ref, dgate_ref, first_ref, taps_ref, gcol_ref, grow_ref, *refs):
    near, (dall_ref, dtaps_ref, ds_ref, rim_ref) = refs[:-4], refs[-4:]
    last = pl.num_programs(0) - 1

    @pl.when(pl.program_id(0) == 0)
    def _():
        for h in range(heads):
            ds_ref[h] = entering(near, h, ((0,), (0,)))
        for ref in (rim_ref, dtaps_ref):
            ref[...] = jnp.zeros_like(ref)

    @pl.when(pl.program_id(0) == last)
    def _():
        rim_back(first_ref, taps_ref, dall_ref, 0, dtaps_ref, rim_ref)
        dall_ref[:RIM, 2 * heads * DV:] = jnp.zeros((RIM, heads * DV), BF)

    @pl.when(pl.program_id(0) < last)
    def _():
        rows, cols = square_index()
        dall_ref[:, 2 * heads * DV:] = dgate_ref[...]
        for h in range(heads):
            ds = ds_ref[h]
            s = s_ref[0, h]
            do = do_ref[:, h * DV:(h + 1) * DV]
            q = q_ref[:, h * DK:(h + 1) * DK]
            k = k_ref[:, h * DK:(h + 1) * DK]
            gcol = gcol_ref[:, h:h + 1]
            beta = gcol_ref[:, heads + h:heads + h + 1]
            grow = grow_ref[0, h:h + 1, :]
            glast = grow[:, CH - 1:CH]
            ratio = jnp.exp(jnp.where(rows >= cols, gcol - grow, -1e30))
            eg = jnp.exp(gcol)
            el = jnp.exp(glast - gcol)
            u = uv_ref[:, h * DV:(h + 1) * DV] - mm(w_ref[:, h * DK:(h + 1) * DK], s)
            du = mm(a_ref[0, h], do, TL) + el * mm(k, ds)
            da = ratio * mm(do, u, TT)
            drv = mm(tinv_ref[0, h], du, TL)
            drk = mm(drv, s, TT)
            dl = jnp.where(rows > cols, (-beta) * ratio * mm(drv, u, TT), 0.0)
            dq = eg * mm(do, s, TT) + mm(da, k)
            dk = el * mm(u, ds, TT) + mm(da, q, TL) - (beta * eg) * drk + mm(dl, k) + mm(dl, k, TL)
            ds_ref[h] = mm(m_ref[0, h], ds, TL) + dc_ref[0, h]
            summed = sum_ref[:, 2 * h * DK:2 * (h + 1) * DK]
            act = summed * sigmoid(summed)
            dact = jnp.concatenate([normed_pull(act[:, :DK], dq, DK ** -0.5), normed_pull(act[:, DK:], dk, 1.0)], 1)
            conv_back(dact, 2 * h * DK, 2 * DK, sum_ref, p_ref, taps_ref, dall_ref, dtaps_ref, rim_ref)
            conv_back(beta * drv, (heads + h) * DV, DV, sum_ref, p_ref, taps_ref, dall_ref, dtaps_ref, rim_ref)


def delta_inputs_back(near, dc, m, s, do, uv, w, a, tinv, q, k, summed, p, dgate, first, taps, gcol, grow,
                      tokens, heads):
    n = tokens // CH

    def at(c):
        return jnp.maximum(n - 1 - c, 0)

    def rows(width):
        return pl.BlockSpec((CH, width), lambda c: (at(c), 0))

    def chunk(shape):
        return pl.BlockSpec((1,) + shape, lambda c: (at(c),) + (0,) * len(shape))

    width = heads * DV
    wide, key = rows(width), rows(heads * DK)
    out = pl.BlockSpec((CH, 3 * width), lambda c: (jnp.where(c == n, n, n - 1 - c), 0))
    return call(
        functools.partial(inputs_back_kernel, heads), "delta_inputs_back", n + 1, 19 * tokens // 1024,
        [chunk((heads, DK, DV)), chunk((heads, DK, DK)), chunk((heads, DK, DV)),
         wide, wide, key, chunk((heads, CH, CH)), chunk((heads, CH, CH)), key, key,
         rows(2 * width), rows(2 * width), wide, whole(first.shape), whole(taps.shape), rows(gcol.shape[1]),
         chunk(grow.shape[1:])] + [whole(a.shape) for a in near],
        [(out, sds((tokens + RIM, 3 * width), BF)),
         (whole(taps.shape), sds(taps.shape))],
        [pltpu.VMEM((heads, DK, DV), F32), pltpu.VMEM((8, 2 * width), F32)],
        dc, m, s, do, uv, w, a, tinv, q, k, summed, p, dgate, first, taps, gcol, grow, *near,
    )


def as_column(row):
    size = row.shape[1]
    found = []
    for at in range(0, size, CH):
        part = row[:, at:min(at + CH, size)]
        if part.shape[1] < CH:
            part = jnp.concatenate([part, jnp.zeros((1, CH - part.shape[1]), F32)], 1)
        found.append(jnp.broadcast_to(part, (CH, CH)).T[:min(CH, size - at), 0:1])
    return jnp.concatenate(found, 0)


def moments_kernel(plan, over_head_ref, over_seq_ref, old_ref, carried_ref, place_ref, conv_second_ref,
                   both_ref, go_ref, outg_ref, ex_ref, sh_ref, *outs):
    beta_two = 1.0 - STEP ** (-0.8)
    (in_rows, in_cols, out_rows, out_cols, ex_rows, ex_cols, sh_rows, sh_cols, late_ref, kernel_ref, second_ref, update_ref,
     in_row, in_col, out_row, out_col, ex_row, ex_col, sh_row, sh_col) = outs
    heads = in_cols.shape[0]
    span = in_rows.shape[1]
    place = lax.broadcasted_iota(jnp.int32, (1, 128), 1)
    sums = carried_ref[...]
    sources = {"head": over_head_ref, "seq": over_seq_ref}

    def moment(name, old_at):
        axis, start, size, over = plan["cells"][name]
        old = old_ref[:, old_at:old_at + size]
        new = beta_two * old + (1.0 - beta_two) * (sources[axis][:, start:start + size] * (1.0 / over) + 1e-30)
        return new, lax.rsqrt(new)

    parts = {
        "in": (both_ref[:span], both_ref[span:], go_ref[:span]),
        "out": (outg_ref[...],),
        "expand": (ex_ref[...].astype(F32),),
        "shrink": (sh_ref[...].astype(F32),),
    }
    refs = {
        "in": (in_rows, in_cols, in_row, in_col), "out": (out_rows, out_cols, out_row, out_col),
        "expand": (ex_rows, ex_cols, ex_row, ex_col), "shrink": (sh_rows, sh_cols, sh_row, sh_col),
    }
    for slot, name in enumerate(parts):
        rows_new, row_root = moment(name + "_rows", plan["old"][name + "_rows"])
        cols_new, col_root = moment(name + "_cols", plan["old"][name + "_cols"])
        rows_ref, cols_ref, row_ref, col_ref = refs[name]
        column = as_column(row_root)
        row_ref[...] = column
        col_ref[...] = col_root
        total, start = 0.0, 0
        for part in parts[name]:
            size = part.shape[1]
            update = part * column * col_root[:, start:start + size]
            total = total + jnp.sum(update * update, axis=(0, 1), keepdims=True)
            start += size
        sums = sums + jnp.where(place == slot, total, 0.0)
        row_total = jnp.sum(rows_new, axis=(0, 1), keepdims=True) * (1.0 / plan["copies"][name])
        sums = sums + jnp.where(place == 4 + slot, row_total, 0.0)
        if name == "in":
            rows_ref[...] = rows_new
            width = heads * DV
            for h in range(heads):
                for i in range(3):
                    cols_ref[h:h + 1, i * DV:(i + 1) * DV] = cols_new[:, i * width + h * DV:i * width + (h + 1) * DV]
        elif name == "out":
            cols_ref[...] = cols_new
            for h in range(heads):
                rows_ref[h:h + 1] = rows_new[:, h * DV:(h + 1) * DV]
        elif name == "expand":
            rows_ref[...] = rows_new
            size = cols_ref.shape[1]
            for i in range(2):
                cols_ref[i:i + 1] = cols_new[:, i * size:(i + 1) * size]
        else:
            rows_ref[...] = rows_new
            cols_ref[...] = cols_new
    axis, start, _, _ = plan["cells"]["taps"]
    cut, width = kernel_ref.shape[2], heads * DV
    total = 0.0
    for j in range(KC):
        for h in range(heads):
            grad = jnp.zeros((1, cut), F32)
            for c in range(CW // cut):
                at = start + j * 2 * width + (c * cut) // DV * width + h * DV + (c * cut) % DV
                grad = grad + place_ref[0:1, c:c + 1] * sources[axis][:, at:at + cut]
            second = beta_two * conv_second_ref[j, h:h + 1, :] + (1.0 - beta_two) * (grad * grad + 1e-30)
            update = grad * lax.rsqrt(second)
            kernel_ref[j, h:h + 1, :] = grad
            second_ref[j, h:h + 1, :] = second
            update_ref[j, h:h + 1, :] = update
            total = total + jnp.sum(update * update, axis=(0, 1), keepdims=True)
    late_ref[:, :128] = sums + jnp.where(place == 13, total, 0.0)
    share = 1.0 / plan["head_count"]
    for name, at in (("gain_two", 128), ("head_gain", 128 + D)):
        axis, start, size, _ = plan["cells"][name]
        late_ref[:, at:at + size] = sources[axis][:, start:start + size] * share


def new_moments(plan, outs, operands):
    return pl.pallas_call(
        functools.partial(moments_kernel, plan),
        out_shape=[sds(a) for a in outs],
        compiler_params=pltpu.CompilerParams(vmem_limit_bytes=56 * 1024 * 1024),
        name="new_moments",
    )(*operands)


def cast_kernel(heads, in_ref, kv_ref, gate_ref):
    width = heads * DV
    for h in range(heads):
        at = slice(h * DV, (h + 1) * DV)
        kv_ref[:, at] = in_ref[:, h, :DV].astype(BF)
        kv_ref[:, width + h * DV:width + (h + 1) * DV] = in_ref[:, h, DV:2 * DV].astype(BF)
        gate_ref[:, at] = in_ref[:, h, 2 * DV:].astype(BF)


def cast_columns(weight, steps=4):
    heads, span = weight.shape[1], weight.shape[0] // steps
    width = heads * DV
    return call(
        functools.partial(cast_kernel, heads), "cast_columns", steps, 3,
        [pl.BlockSpec((span, heads, HC), lambda c: (c, 0, 0))],
        [(pl.BlockSpec((span, size), lambda c: (c, 0)), sds((weight.shape[0], size), BF)) for size in (2 * width, width)],
        [],
        weight,
    )


def joined_kernel(heads, keys_ref, vals_ref, gate_ref, out_ref):
    for h in range(heads):
        at = slice(h * DV, (h + 1) * DV)
        for i, ref in enumerate((keys_ref, vals_ref, gate_ref)):
            out_ref[:, h, i * DV:(i + 1) * DV] = ref[:, at]


def joined_columns(both, go, heads, steps=4):
    span, width = both.shape[0] // (2 * steps), both.shape[1]
    first = pl.BlockSpec((span, width), lambda c: (c, 0))
    return call(
        functools.partial(joined_kernel, heads), "joined_columns", steps, 3,
        [first, pl.BlockSpec((span, width), lambda c: (c + steps, 0)), first],
        [(pl.BlockSpec((span, heads, HC), lambda c: (c, 0, 0)), sds((both.shape[0] // 2, heads, HC)))],
        [],
        both, both, go,
    )[0]


def split_kernel(grad_ref, out_ref):
    size = out_ref.shape[2]
    for i in range(2):
        out_ref[:, i, :] = grad_ref[:, i * size:(i + 1) * size].astype(F32)


def split_columns(grad, steps=4):
    span, size = grad.shape[0] // steps, grad.shape[1] // 2
    return call(
        split_kernel, "split_columns", steps, 3,
        [pl.BlockSpec((span, 2 * size), lambda c: (c, 0))],
        [(pl.BlockSpec((span, 2, size), lambda c: (c, 0, 0)), sds((grad.shape[0], 2, size)))],
        [],
        grad,
    )[0]


def small_step(weight, gradient, second_old, beta_two):
    second_new = beta_two * second_old + (1.0 - beta_two) * (gradient * gradient + 1e-30)
    update = gradient * lax.rsqrt(second_new)
    root = jnp.sqrt(jnp.mean(update * update, axis=-1, keepdims=True))
    scale = 0.3 * jnp.maximum(0.001, jnp.sqrt(jnp.mean(weight * weight, axis=-1, keepdims=True)))
    return second_new, weight - scale * (update / jnp.maximum(1.0, root))


def weights_kernel(heads, late_ref, gains_ref, gains_second_ref, head_ref, head_second_ref, conv_ref, conv_update_ref,
                   in_ref, keys_ref, vals_ref, gate_ref, in_row, in_col, out_ref, outg_ref, out_row, out_col,
                   ex_ref, exg_ref, ex_row, ex_col, sh_ref, shg_ref, sh_row, sh_col,
                   gains_grad, gains_second_new, gains_new, head_grad, head_second_new, head_new, conv_new,
                   in_new, out_new, ex_new, sh_new):
    beta_two = 1.0 - STEP ** (-0.8)
    counts = ((D, HEAD_TOTAL * HC), (HEAD_TOTAL * DV, D), (D, 2 * FF), (FF, D))

    def cell(at):
        return late_ref[0:1, at:at + 1]

    def size_of(weight, entries):
        return 0.3 * jnp.maximum(0.001, jnp.sqrt(weight * (1.0 / entries)))

    def scale(slot):
        mean, entries = cell(4 + slot) * (1.0 / counts[slot][0]), counts[slot][0] * counts[slot][1]
        root = jnp.sqrt(cell(slot) * mean * (1.0 / entries))
        return size_of(cell(8 + slot), entries) * jnp.sqrt(mean) / jnp.maximum(1.0, root)

    scales = [scale(slot) for slot in range(4)]

    @pl.when(pl.program_id(0) == 0)
    def _():
        for row in range(2):
            first = 128 if row else 128 + D + DV
            grad = late_ref[0:1, first:first + D]
            at = slice(row, row + 1)
            gains_grad[at] = grad
            gains_second_new[at], gains_new[at] = small_step(gains_ref[at], grad, gains_second_ref[at], beta_two)
        grad = late_ref[0:1, 128 + D:128 + D + DV]
        head_grad[...] = grad
        head_second_new[...], head_new[...] = small_step(head_ref[...], grad, head_second_ref[...], beta_two)
        entries = KC * HEAD_TOTAL * CW
        factor = size_of(cell(12), entries) / jnp.maximum(1.0, jnp.sqrt(cell(13) * (1.0 / entries)))
        conv_new[...] = conv_ref[...] - conv_update_ref[...] * factor[None]

    def stepped(weight, grad, rows, cols, slot):
        return weight - (grad.astype(F32) * cols) * (rows * scales[slot])

    width = heads * DV
    for h in range(heads):
        for i, ref in enumerate((keys_ref, vals_ref, gate_ref)):
            col = in_col[:, i * width + h * DV:i * width + (h + 1) * DV]
            at = slice(i * DV, (i + 1) * DV)
            in_new[:, h, at] = stepped(in_ref[:, h, at], ref[:, h * DV:(h + 1) * DV], in_row[...], col, 0)
    out_new[...] = stepped(out_ref[...], outg_ref[...], out_row[...], out_col[...], 1)
    size = ex_ref.shape[2]
    for i in range(2):
        at = slice(i * size, (i + 1) * size)
        ex_new[:, i, :] = stepped(ex_ref[:, i, :], exg_ref[:, at], ex_row[...], ex_col[:, at], 2)
    sh_new[...] = stepped(sh_ref[...], shg_ref[...], sh_row[...], sh_col[...], 3)


def new_weights(heads, small, groups):
    ins, operands = [whole(a.shape) for a in small], list(small)
    late, gains, _, head = small[:4]
    outs = [(whole(a.shape), sds(a.shape)) for a in (gains, gains, gains, head, head, head, small[5])]
    steps = 8 if groups[3][0].shape[0] % 128 == 0 else 4

    def blocked(a, span, first=0):
        tail = a.shape[1:]
        return pl.BlockSpec((span,) + tail, lambda c: (c + first,) + (0,) * len(tail))

    for weight, parts, rows, cols in groups:
        span = weight.shape[0] // steps
        for i, a in enumerate((weight, *parts, rows)):
            ins.append(blocked(a, span, steps if len(parts) == 3 and i == 2 else 0))
            operands.append(a)
        ins.append(whole(cols.shape))
        operands.append(cols)
        outs.append((blocked(weight, span), sds(weight.shape)))
    return call(functools.partial(weights_kernel, heads), "new_weights", steps, 10, ins, outs, [], *operands, room=56)


def ring(x, by=1):
    n = lax.axis_size("seq")
    return lax.ppermute(x, "seq", [(i, (i + by) % n) for i in range(n)])


def ahead(x, by):
    n = lax.axis_size("seq")
    return lax.ppermute(x, "seq", [(i, i + by) for i in range(n) if 0 <= i + by < n])


def after(x, *others):
    return lax.optimization_barrier((x,) + others)[0]


def ring_gather(x, hold=None):
    slots = [x]
    for k in range(1, lax.axis_size("seq")):
        slots.append(ring(after(slots[-1], *(hold or {}).get(k, ()))))
    return slots


def vector_of(scalars, size, first=0):
    place = lax.broadcasted_iota(jnp.int32, (1, size), 1)
    return sum(jnp.where(place == first + i, a, 0.0) for i, a in enumerate(scalars))


def ring_scatter(part, hold=None):
    n = lax.axis_size("seq")
    total, totals = part(1).astype(BF), []
    for k in range(1, n):
        held = hold(k) if hold else ()
        total = ring(after(total, *held) if held else total).astype(F32) + part((k + 1) % n).astype(F32)
        total = total if k == n - 1 else total.astype(BF)
        totals.append(total)
    return total, totals


def seq_slot(x, k, axis=0):
    n, z = lax.axis_size("seq"), lax.axis_index("seq")
    span = x.shape[axis] // n
    return lax.dynamic_slice_in_dim(x, lax.rem(z - k + n, n) * span, span, axis)


def in_order(slots, axis=0):
    n, z = lax.axis_size("seq"), lax.axis_index("seq")
    span = slots[0].shape[axis]
    turned = jnp.concatenate(slots[::-1] + slots[:0:-1], axis)
    return lax.dynamic_slice_in_dim(turned, (n - 1 - z) * span, n * span, axis)


def gather_head(x, axis=0):
    return lax.all_gather(x, "head", axis=axis, tiled=True)


def scatter_head(x, axis=0):
    return lax.psum_scatter(x, "head", scatter_dimension=axis, tiled=True)


def total_over(axis, x):
    n = lax.axis_size(axis)
    if n & (n - 1):
        return lax.psum(x, axis)
    step = 1
    while step < n:
        x = x + lax.ppermute(x, axis, [(i, i ^ step) for i in range(n)])
        step *= 2
    return x


def dot(a, b, dims=((1,), (0,)), out=F32):
    return lax.dot_general(a, b, (dims, ((), ())), preferred_element_type=out)


def norm_rows(entries, scale_row):
    return entries * lax.rsqrt(jnp.mean(entries * entries, axis=-1, keepdims=True) + 1e-06) * scale_row


def nearby(last, backward):
    n, sign = lax.axis_size("seq"), -1 if backward else 1
    near = [ahead(last, sign * k) for k in range(1, n - 1)]
    return near + [ahead(last[..., DK:], sign * (n - 1))]


def local(
    hidden_in,
    out_grad,
    decays,
    strength,
    mixer_in,
    mixer_in_rows,
    mixer_in_cols,
    mixer_out,
    mixer_out_rows,
    mixer_out_cols,
    feed_in,
    feed_in_rows,
    feed_in_cols,
    feed_out,
    feed_out_rows,
    feed_out_cols,
    conv_kernel,
    conv_second,
    norm_gains,
    gains_second,
    head_gain,
    head_gain_second,
):
    beta_two = 1.0 - STEP ** (-0.8)
    n = lax.axis_size("seq")
    seq_count, head_count = n, lax.axis_size("head")
    tokens, heads = decays.shape
    blocks = tokens // CH
    in_span = mixer_in.shape[0]
    out_span = mixer_out.shape[2]
    feed_span, hidden_span = feed_in.shape[0], feed_in.shape[2]
    width = heads * DV

    def padded(pieces):
        found, cells, at = [], {}, 0
        for name, piece in pieces.items():
            piece = piece.reshape(1, -1)
            size = piece.shape[1]
            room = -(-size // 128) * 128
            found.append(jnp.pad(piece, ((0, 0), (0, room - size))))
            cells[name] = (at, size)
            at += room
        return jnp.concatenate(found, 1), cells

    old_moments, old_cells = padded(
        {
            "in_rows": mixer_in_rows,
            "in_cols": jnp.stack([mixer_in_cols[:, i * DV : (i + 1) * DV] for i in range(3)]),
            "out_rows": mixer_out_rows,
            "out_cols": mixer_out_cols,
            "expand_rows": feed_in_rows,
            "expand_cols": feed_in_cols,
            "shrink_rows": feed_out_rows,
            "shrink_cols": feed_out_cols,
        }
    )
    over_counts = {
        "in_rows": HEAD_TOTAL * HC, "in_cols": D, "out_rows": D, "out_cols": HEAD_TOTAL * DV,
        "expand_rows": 2 * FF, "expand_cols": D, "shrink_rows": D, "shrink_cols": FF,
    }
    place = jnp.where(lax.broadcasted_iota(jnp.int32, (1, 128), 1) == lax.axis_index("seq"), 1.0, 0.0)

    x = hidden_in.astype(F32)
    rows_all = gather_head(norm_rows(x, norm_gains[0]).astype(BF))
    kv_own, gate_own = cast_columns(mixer_in)
    taps_mine = conv_kernel.astype(BF).reshape(KC, heads * conv_kernel.shape[2])
    taps_slots = [taps_mine] + [ring(taps_mine, k) for k in range(1, n)]
    kv_slots = ring_gather(kv_own, {2: taps_slots[1:]})[:3]
    rim = ahead(rows_all[tokens - RIM :], 1)
    taps = in_order([t[None] for t in taps_slots]).reshape(n, KC, heads, -1)
    taps = jnp.moveaxis(taps, 0, 2).reshape(KC, heads, CW).astype(F32)
    taps = jnp.concatenate([taps[:, :, : 2 * DK].reshape(KC, width), taps[:, :, 2 * DK :].reshape(KC, width)], 1)

    lower = jnp.tril(jnp.ones((CH, CH), F32))
    log_sum = jnp.einsum(
        "ij,bjh->bih", lower, jnp.log(decays).reshape(blocks, CH, heads), precision=lax.Precision.HIGHEST
    )
    gcol = jnp.concatenate([log_sum.reshape(tokens, heads), strength, jnp.zeros((tokens, 8 - 2 * heads), F32)], 1)
    grow = jnp.concatenate([jnp.swapaxes(log_sum, 1, 2), jnp.zeros((blocks, 8 - heads, CH), F32)], 1)
    gain_row = head_gain[None]
    row_slots = [seq_slot(rows_all, k, 1) for k in range(n)]

    def projected(parts, slots, total=None):
        for part, slot in zip(parts, slots):
            found = dot(part, slot)
            total = found if total is None else total + found
        return total

    expand = gather_head(after(feed_in.astype(BF).reshape(feed_span, 2 * hidden_span), rows_all, kv_slots[1]))
    p_start = projected(row_slots[:2], kv_slots[:2])
    kv_held, p_start, rim = lax.optimization_barrier((kv_slots[2], p_start, rim))
    kv_slots[2] = kv_held
    for _ in range(3, n):
        kv_slots.append(ring(kv_slots[-1]))
    rim_slots = [seq_slot(rim, k, 1) for k in range(n)]
    p_kv, r_kv = projected(row_slots[2:], kv_slots[2:], p_start), projected(rim_slots, kv_slots)
    go_own = jnp.concatenate([gate_own, mixer_out.astype(BF).reshape(width, out_span).T], 0)
    go_slots = ring_gather(go_own, {1: (kv_slots[-1],)})[:2]
    (summed, q, k, tinv, scores, w, uv, qe, oz, m, pre, last) = delta_parts(
        p_kv, r_kv, taps, gcol, grow, tokens, heads
    )
    last, go_one, go_zero, expand = lax.optimization_barrier((last, go_slots[1], go_slots[0], expand))
    go_slots = [go_zero, go_one]
    for _ in range(2, n):
        go_slots.append(ring(go_slots[-1]))
    shrink = gather_head(after(feed_out.astype(BF), expand, last, go_slots[2]), 1)
    p_gate = projected(row_slots, [a[:in_span] for a in go_slots])
    states, o, gated, mixed = delta_outputs(
        nearby(last, False), go_slots, pre, qe, oz, p_gate, gain_row, in_span, tokens, heads
    )
    grad_slots = ring_gather(out_grad, {1: (go_slots[-1],)})
    grad_rows = jnp.concatenate(grad_slots, 0)
    mixed = scatter_head(after(mixed, shrink)).astype(F32)
    mixed = in_order([mixed[:, i * out_span : (i + 1) * out_span] for i in range(n)], 1)
    residual = x + mixed
    out_t = in_order([a[in_span:] for a in go_slots])
    w_all = in_order([jnp.concatenate([a, b[:in_span]], 1) for a, b in zip(kv_slots, go_slots)])
    weights_then = lax.optimization_barrier((mixer_in, mixer_out, feed_in, feed_out, gated))[:4]
    weight_sums = vector_of([jnp.sum(a * a) for a in (*weights_then, conv_kernel)], 128, 8)

    normed_two, norm_two_pull = jax.vjp(norm_rows, residual, norm_gains[1])
    d_hidden = lax.optimization_barrier(dot(grad_rows, shrink, ((1,), (1,))))
    feed_held, out_t, w_all, weight_sums, old_moments = lax.optimization_barrier(
        (normed_two.astype(BF), out_t, w_all, weight_sums, old_moments)
    )
    feed_slots = ring_gather(feed_held, {1: (grad_slots[-1],), 2: (d_hidden,)})
    feed_rows = jnp.concatenate(feed_slots, 0)
    gate_up = dot(feed_rows, expand)
    gate, up = gate_up[:, :hidden_span], gate_up[:, hidden_span:]
    sig = sigmoid(gate)
    silu = gate * sig
    hidden = (silu * up).astype(BF)
    d_gate_up = jnp.concatenate(
        [d_hidden * up * (sig * (1.0 + gate * (1.0 - sig))), d_hidden * silu], 1
    ).astype(BF)
    rows_here = hidden_in.shape[0]

    def slot_rows(a, k):
        return a[k * rows_here : (k + 1) * rows_here]

    d_feed_rows = dot(d_gate_up, expand, ((1,), (1,)))
    d_normed_two, _ = ring_scatter(lambda k: slot_rows(d_feed_rows, k))
    d_residual_part, d_gain_two = norm_two_pull(d_normed_two)
    d_residual = out_grad.astype(F32) + d_residual_part
    d_residual_low = d_residual.astype(BF)
    d_rows = gather_head(d_residual_low)
    hidden_then, feed_rows_then, _ = lax.optimization_barrier((hidden, feed_rows, d_residual_low))
    shrink_part = dot(hidden_then, grad_rows, ((0,), (0,)), BF)
    feed_part = dot(hidden_then, shrink, out=BF)
    feed_part = in_order([slot_rows(feed_part, i) for i in range(n)])
    expand_part = dot(feed_rows_then, d_gate_up, ((0,), (0,)), BF)
    shrink_part, expand_part, feed_part, d_rows = lax.optimization_barrier(
        (shrink_part, expand_part, feed_part, d_rows)
    )
    shrink_low = scatter_head(shrink_part, 1)

    do, d_gate, dc, d_last, d_head_gain = delta_states_back(d_rows, out_t, o, p_gate, gain_row, qe, m, last, tokens, heads)
    near = nearby(d_last, True)
    gate_then, d_rows_then, _ = lax.optimization_barrier((d_gate, d_rows, d_last))

    def go_part(k, out=F32, rows=d_rows_then):
        d_slot = seq_slot(rows, k, 1)
        return jnp.concatenate([dot(row_slots[k], gate_then, TL, out), dot(d_slot, gated, TL, out)], 0)

    def added(arrived, part):
        return arrived.astype(F32) + part.astype(F32)

    go, go_next = lax.optimization_barrier((go_part(1, BF), go_part(2 % n), *near))[:2]
    sent = ring(go)
    d_all, d_taps = delta_inputs_back(
        near, dc, m, states, do, uv, w, scores, tinv, q, k, summed, p_kv, d_gate, r_kv, taps, gcol, grow, tokens, heads
    )
    d_all, sent, go_next, gate_then, d_rows_then, shrink_low = lax.optimization_barrier(
        (d_all, sent, go_next, gate_then, d_rows_then, shrink_low)
    )
    more_slots = [jnp.concatenate([a, b], 0) for a, b in zip(row_slots, rim_slots)]
    expand_low = scatter_head(after(expand_part, shrink_low, d_all))
    shrink_g, expand_g = shrink_low.astype(F32), expand_low.astype(F32)

    def both_part(k, out=F32):
        found = [dot(more_slots[k], d_all[:, i * width : (i + 1) * width], TL, out) for i in range(2)]
        return jnp.concatenate(found, 0)

    go = added(sent, go_next).astype(BF)
    both = both_part(1, BF)
    sent = ring(jnp.concatenate([go, both], 0))
    d_rows_more = dot(after(d_all, both), w_all, ((1,), (1,)), BF)
    parts = [jnp.concatenate([go_part((step + 1) % n, F32, d_rows_then), both_part(step)], 0) for step in range(2, n)]
    rim_rows, last_part, *parts = lax.optimization_barrier((d_rows_more[tokens:], both_part(0), *parts))
    rim_back = ahead(rim_rows, -1)
    d_rows_in = jnp.concatenate([d_rows_more[: tokens - RIM], d_rows_more[tokens - RIM : tokens] + rim_back], 0)
    feed_sums = (jnp.sum(expand_g * expand_g, 0), jnp.sum(shrink_g * shrink_g, 1))
    feed_sums += (jnp.sum(expand_g * expand_g, 1), jnp.sum(shrink_g * shrink_g, 0))
    for step in range(2, n):
        total = added(sent, parts[step - 2])
        if step < n - 1:
            sent = ring(total.astype(BF))
    d_normed_low = scatter_head(after(d_rows_in, expand_low, sent))
    go, both = total[: 2 * in_span], total[2 * in_span :].astype(BF)
    both, *feed_sums = lax.optimization_barrier((both, *feed_sums))
    both_grad = added(ring(both), last_part)
    go = lax.optimization_barrier(go)
    out_g = lax.optimization_barrier(go[in_span:].T)
    d_normed = d_normed_low.astype(F32)

    _, norm_one_pull = jax.vjp(norm_rows, x, norm_gains[0])
    d_residual_one, d_gain_one = norm_one_pull(d_normed)
    input_grad = d_residual + d_residual_one


    out_sq, both_sq, gate_sq = out_g * out_g, both_grad * both_grad, go[:in_span] * go[:in_span]
    over_head, head_cells = padded(
        {
            "expand_cols": feed_sums[0],
            "shrink_rows": feed_sums[1],
            "gain_two": d_gain_two,
            "head_gain": d_head_gain,
            "out_cols": jnp.sum(out_sq, 0),
            "in_rows": jnp.sum(both_sq[:in_span], 1) + jnp.sum(both_sq[in_span:], 1) + jnp.sum(gate_sq, 1),
        }
    )
    over_seq, seq_cells = padded(
        {
            "expand_rows": feed_sums[2],
            "shrink_cols": feed_sums[3],
            "taps": d_taps,
            "out_rows": jnp.sum(out_sq, 1),
            "in_cols": jnp.concatenate([jnp.sum(a, 0) for a in (both_sq[:in_span], both_sq[in_span:], gate_sq)]),
        }
    )
    both_then, over_head, over_seq = lax.optimization_barrier((both_grad, over_head, over_seq))
    in_grad = joined_columns(both_then, go, heads)
    expand_out = split_columns(expand_low)
    over_head, over_seq = total_over("head", over_head), total_over("seq", over_seq)

    cells = {}
    for axis, found in (("head", head_cells), ("seq", seq_cells)):
        for name, (at, size) in found.items():
            cells[name] = (axis, at, size, over_counts.get(name))
    plan = {
        "cells": cells,
        "old": {name: at for name, (at, _) in old_cells.items()},
        "copies": {"in": head_count, "out": seq_count, "expand": seq_count, "shrink": head_count},
        "head_count": head_count,
    }
    shape = {name: (1, size) for name, (_, _, size, _) in cells.items()}
    conv_shape = conv_kernel.shape
    (in_rows_new, in_cols_new, out_rows_new, out_cols_new, expand_rows_new, expand_cols_new, shrink_rows_new,
     shrink_cols_new, late, kernel_grad, conv_second_new, conv_update, *roots) = new_moments(
        plan,
        [shape["in_rows"], (heads, HC), (heads, DV), shape["out_cols"], shape["expand_rows"], (2, hidden_span),
         shape["shrink_rows"], shape["shrink_cols"], (1, 128 + D + DV), conv_shape, conv_shape, conv_shape]
        + [a for name in ("in", "out", "expand", "shrink") for a in ((shape[name + "_rows"][1], 1), shape[name + "_cols"])],
        [over_head, over_seq, old_moments, weight_sums, place, conv_second,
         both_grad, go, out_g, expand_low, shrink_low],
    )
    feed_sum = lax.psum_scatter(after(feed_part, d_normed_low, late), "seq", scatter_dimension=0, tiled=True).astype(F32)
    block_out = (residual + feed_sum).astype(BF)

    late = total_over("seq", total_over("head", jnp.concatenate([late, d_gain_one[None]], 1)))
    (gains_grad, gains_second_new, gains_new, head_gain_grad, head_second_new, head_new, conv_new,
     in_new, out_new, expand_new, shrink_new) = new_weights(
        heads,
        (late, norm_gains, gains_second, head_gain[None], head_gain_second[None], conv_kernel, conv_update),
        [
            (mixer_in, (both_grad, both_grad, go), *roots[0:2]),
            (mixer_out.reshape(width, out_span), (out_g,), *roots[2:4]),
            (feed_in, (expand_low,), *roots[4:6]),
            (feed_out, (shrink_low,), *roots[6:8]),
        ],
    )
    return (
        block_out,
        input_grad,
        in_grad,
        in_rows_new.reshape(-1),
        in_cols_new,
        in_new,
        out_g.reshape(mixer_out.shape),
        out_rows_new,
        out_cols_new.reshape(-1),
        out_new.reshape(mixer_out.shape),
        expand_out,
        expand_rows_new.reshape(-1),
        expand_cols_new,
        expand_new,
        shrink_g,
        shrink_rows_new.reshape(-1),
        shrink_cols_new.reshape(-1),
        shrink_new,
        kernel_grad,
        conv_second_new,
        conv_new,
        gains_grad,
        gains_second_new,
        gains_new,
        head_gain_grad.reshape(-1),
        head_second_new.reshape(-1),
        head_new.reshape(-1),
    )


def solution(mesh):
    return jax.shard_map(
        local,
        mesh=mesh,
        in_specs=(
            P(("seq", "head"), None),
            P(("seq", "head"), None),
            P("seq", "head"),
            P("seq", "head"),
            P("seq", "head", None),
            P("seq"),
            P("head", None),
            P("head", None, "seq"),
            P("head", None),
            P("seq"),
            P("head", None, "seq"),
            P("head"),
            P(None, "seq"),
            P("seq", "head"),
            P("seq"),
            P("head"),
            P(None, "head", "seq"),
            P(None, "head", "seq"),
            P(),
            P(),
            P(),
            P(),
        ),
        out_specs=(
            P(("seq", "head"), None),
            P(("seq", "head"), None),
            P("seq", "head", None),
            P("seq"),
            P("head", None),
            P("seq", "head", None),
            P("head", None, "seq"),
            P("head", None),
            P("seq"),
            P("head", None, "seq"),
            P("head", None, "seq"),
            P("head"),
            P(None, "seq"),
            P("head", None, "seq"),
            P("seq", "head"),
            P("seq"),
            P("head"),
            P("seq", "head"),
            P(None, "head", "seq"),
            P(None, "head", "seq"),
            P(None, "head", "seq"),
            P(),
            P(),
            P(),
            P(),
            P(),
            P(),
        ),
        check_vma=False,
    )
```

```python
import functools
import jax
import jax.numpy as jnp
import numpy as np
from jax import lax
from jax.experimental import pallas as pl
from jax.experimental.pallas import tpu as pltpu
from jax.sharding import PartitionSpec as P

D = 2048
HEAD_TOTAL = 16
DK = 128
DV = 256
FF = 5632
KC = 4
STEP = 10
CH = 128
RIM = 16
HC = 2 * DK + 2 * DV
CW = 2 * DK + DV
F32 = jnp.float32
BF = jnp.bfloat16
TT = ((1,), (1,))
TL = ((0,), (0,))


def mm(a, b, dims=((1,), (0,))):
    return lax.dot_general(a.astype(BF), b.astype(BF), (dims, ((), ())), preferred_element_type=F32)


def mm3(a, b, dims=((1,), (0,))):
    ah, bh = a.astype(BF), b.astype(BF)
    al, bl = (a - ah.astype(F32)).astype(BF), (b - bh.astype(F32)).astype(BF)
    one = functools.partial(lax.dot_general, dimension_numbers=(dims, ((), ())), preferred_element_type=F32)
    return one(ah, bh) + (one(ah, bl) + one(al, bh))


def sigmoid(v):
    return 1.0 / (1.0 + jnp.exp(-v))


def square_index():
    rows = lax.broadcasted_iota(jnp.int32, (CH, CH), 0)
    cols = lax.broadcasted_iota(jnp.int32, (CH, CH), 1)
    return rows, cols


def invert(strict, rows, cols):
    apart = rows ^ cols
    xs = [jnp.where(rows == cols, 1.0, 0.0) - jnp.where(apart == 1, s, 0.0) for s in strict]
    size = 2
    while size < CH:
        here = (apart >= size) & (apart < 2 * size)
        left = [mm3(x, jnp.where(here, s, 0.0)) for x, s in zip(xs, strict)]
        xs = [x - mm3(y, x) for x, y in zip(xs, left)]
        size *= 2
    return xs


def parts_kernel(heads, p_ref, halo_ref, first_ref, taps_ref, gcol_ref, grow_ref,
                 sum_ref, q_ref, k_ref, tinv_ref, a_ref, w_ref, uv_ref, qe_ref, oz_ref, m_ref, pre_ref, last_ref, x_ref):
    rows, cols = square_index()
    eye = jnp.where(rows == cols, 1.0, 0.0)
    width = heads * DV

    @pl.when(pl.program_id(0) == 0)
    def _():
        for h in range(heads):
            x_ref[h] = jnp.concatenate([eye, jnp.zeros((DK, DV), F32)], 1)

    def convolved(at, size):
        before = jnp.where(pl.program_id(0) == 0, first_ref[RIM - 8:, at:at + size], halo_ref[:, at:at + size])
        ext = jnp.concatenate([before, p_ref[:, at:at + size]], 0)
        summed = taps_ref[0:1, at:at + size] * ext[5:5 + PER * CH]
        for j in range(1, KC):
            summed = summed + taps_ref[j:j + 1, at:at + size] * ext[5 + j:5 + j + PER * CH]
        sum_ref[:, at:at + size] = summed
        return summed * sigmoid(summed)

    stricts, held = [], []
    for h in range(heads):
        act = convolved(2 * h * DK, 2 * DK)
        values = convolved(width + h * DV, DV)
        for c in range(PER):
            at = slice(c * CH, (c + 1) * CH)
            q, k = act[at, :DK], act[at, DK:]
            q = q * (lax.rsqrt(jnp.sum(q * q, axis=-1, keepdims=True) + 1e-6) * DK ** -0.5)
            k = k * lax.rsqrt(jnp.sum(k * k, axis=-1, keepdims=True) + 1e-6)
            gcol, beta = gcol_ref[at, h:h + 1], gcol_ref[at, heads + h:heads + h + 1]
            grow = grow_ref[c, h:h + 1, :]
            ratio = jnp.exp(jnp.where(rows >= cols, gcol - grow, -1e30))
            stricts.append(jnp.where(rows > cols, beta * ratio * mm3(k, k, TT), 0.0))
            held.append((h, c, q, k, values[at], ratio, gcol, beta, grow[:, CH - 1:CH]))
    for (h, c, q, k, v, ratio, gcol, beta, glast), tinv in zip(held, invert(stricts, rows, cols)):
        at, key, val = slice(c * CH, (c + 1) * CH), slice(h * DK, (h + 1) * DK), slice(h * DV, (h + 1) * DV)
        eg = jnp.exp(gcol)
        kd = k * jnp.exp(glast - gcol)
        a = ratio * mm(q, k, TT)
        w = mm3(tinv, (beta * eg) * k)
        uv = mm3(tinv, beta * v)
        m = jnp.exp(glast) * eye - mm(kd, w, TL)
        x = x_ref[h]
        pre_ref[c, h] = x
        x = mm(m, x) + jnp.concatenate([jnp.zeros((DK, DK), F32), mm(kd, uv, TL)], 1)
        x_ref[h] = x
        last_ref[h] = x.astype(BF)
        q_ref[at, key] = q.astype(BF)
        k_ref[at, key] = k.astype(BF)
        tinv_ref[c, h] = tinv.astype(BF)
        a_ref[c, h] = a.astype(BF)
        w_ref[at, key] = w.astype(BF)
        uv_ref[at, val] = uv
        qe_ref[at, key] = (q * eg - mm(a, w)).astype(BF)
        oz_ref[at, val] = mm(a, uv)
        m_ref[c, h] = m.astype(BF)


def whole(shape):
    return pl.BlockSpec(shape, lambda c: (0,) * len(shape))


PER = 2


def by_rows(width, n, back=False):
    last = n // PER - 1
    return pl.BlockSpec((PER * CH, width), (lambda c: (last - c, 0)) if back else (lambda c: (c, 0)))


def by_chunk(shape, n, back=False):
    tail, last = (0,) * len(shape), n // PER - 1
    return pl.BlockSpec((PER,) + shape, (lambda c: (last - c,) + tail) if back else (lambda c: (c,) + tail))


def sds(shape, dt=F32):
    return jax.ShapeDtypeStruct(shape, dt)


def call(kernel, name, n, micros, ins, outs, scratch, *operands, room=48):
    return pl.pallas_call(
        kernel,
        grid=(n,),
        in_specs=ins,
        out_specs=[spec for spec, _ in outs],
        out_shape=[shape for _, shape in outs],
        scratch_shapes=scratch,
        compiler_params=pltpu.CompilerParams(
            vmem_limit_bytes=room * 1024 * 1024, dimension_semantics=("arbitrary",)
        ),
        cost_estimate=pl.CostEstimate(flops=micros * 10**5, bytes_accessed=micros * 10**3, transcendentals=0),
        name=name,
    )(*operands)


def delta_parts(p, first, taps, gcol, grow, tokens, heads):
    n, span, width = tokens // CH, PER * CH, heads * DV

    def rows(size, dt=F32):
        return pl.BlockSpec((span, size), lambda c: (c, 0)), sds((tokens, size), dt)

    def chunk(shape, dt=F32):
        tail = (0,) * len(shape)
        return pl.BlockSpec((PER,) + shape, lambda c: (c,) + tail), sds((n,) + shape, dt)

    halo = pl.BlockSpec((8, 2 * width), lambda c: (jnp.maximum(c * (span // 8) - 1, 0), 0))
    return call(
        functools.partial(parts_kernel, heads), "delta_parts", n // PER, 35 * tokens // 1024,
        [rows(2 * width)[0], halo, whole(first.shape), whole(taps.shape), rows(gcol.shape[1])[0], chunk(grow.shape[1:])[0]],
        [rows(2 * width), rows(heads * DK, BF), rows(heads * DK, BF), chunk((heads, CH, CH), BF), chunk((heads, CH, CH), BF),
         rows(heads * DK, BF), rows(width), rows(heads * DK, BF), rows(width), chunk((heads, DK, DK), BF),
         chunk((heads, DK, DK + DV)), (whole((heads, DK, DK + DV)), sds((heads, DK, DK + DV), BF))],
        [pltpu.VMEM((heads, DK, DK + DV), F32)],
        p, p, first, taps, gcol, grow,
    )


def entering(maps, offsets, dims):
    state = offsets[-1].astype(F32)
    for found, offset in zip(maps[::-1], offsets[-2::-1]):
        state = mm(found, state, dims) + offset.astype(F32)
    return state


def outputs_kernel(heads, count, rows_before, pre_ref, qe_ref, oz_ref, gate_ref, gain_ref, *refs):
    near, slots, (s_ref, o_ref, gated_ref, mixed_ref, start_ref) = refs[:count], refs[count:-5], refs[-5:]

    @pl.when(pl.program_id(0) == 0)
    def _():
        for h in range(heads):
            maps = [a[h, :, :DK] for a in near[:-1]]
            offsets = [a[h, :, DK:] for a in near[:-1]] + [near[-1][h]]
            start_ref[h] = entering(maps, offsets, ((1,), (0,)))

    for h in range(heads):
        at = slice(h * DV, (h + 1) * DV)
        found = []
        for c in range(PER):
            rows = slice(c * CH, (c + 1) * CH)
            pre = pre_ref[c, h]
            s = mm(pre[:, :DK], start_ref[h]) + pre[:, DK:]
            s_ref[c, h] = s.astype(BF)
            found.append(mm(qe_ref[rows, h * DK:(h + 1) * DK], s) + oz_ref[rows, at])
        o = jnp.concatenate(found, 0)
        o_ref[:, at] = o
        gate = gate_ref[:, at]
        n = o * lax.rsqrt(jnp.mean(o * o, axis=-1, keepdims=True) + 1e-5)
        gated_ref[:, at] = (n * gain_ref[...] * (gate * sigmoid(gate))).astype(BF)
    gated = gated_ref[...]
    size = slots[0].shape[0] - rows_before
    for i, slot in enumerate(slots):
        mixed_ref[:, i * size:(i + 1) * size] = mm(gated, slot[rows_before:], TT).astype(BF)


def delta_outputs(near, slots, pre, qe, oz, gate, gain, rows_before, tokens, heads):
    n = tokens // CH
    wide = by_rows(heads * DV, n)
    size = len(slots) * (slots[0].shape[0] - rows_before)
    return call(
        functools.partial(outputs_kernel, heads, len(near), rows_before), "delta_outputs", n // PER, 7 * tokens // 1024,
        [by_chunk((heads, DK, DK + DV), n), by_rows(heads * DK, n), wide, wide, whole((1, DV))]
        + [whole(a.shape) for a in (*near, *slots)],
        [(by_chunk((heads, DK, DV), n), sds((n, heads, DK, DV), BF)), (wide, sds((tokens, heads * DV))),
         (wide, sds((tokens, heads * DV), BF)), (by_rows(size, n), sds((tokens, size), BF))],
        [pltpu.VMEM((heads, DK, DV), F32)],
        pre, qe, oz, gate, gain, *near, *slots,
    )


def states_back_kernel(heads, drows_ref, out_ref, o_ref, gate_ref, gain_ref, qe_ref, m_ref,
                       do_ref, dgate_ref, dc_ref, last_ref, dgain_ref, d_ref):
    @pl.when(pl.program_id(0) == 0)
    def _():
        d_ref[...] = jnp.zeros_like(d_ref)
        dgain_ref[...] = jnp.zeros_like(dgain_ref)

    dgated = mm(drows_ref[...], out_ref[...])
    for h in range(heads):
        at = slice(h * DV, (h + 1) * DV)
        o, gate, dg, gain = o_ref[:, at], gate_ref[:, at], dgated[:, at], gain_ref[...]
        rstd = lax.rsqrt(jnp.mean(o * o, axis=-1, keepdims=True) + 1e-5)
        n = o * rstd
        sg = sigmoid(gate)
        act = gate * sg
        dgain_ref[...] += jnp.sum(dg * n * act, axis=0, keepdims=True)
        dgate_ref[:, at] = (dg * n * gain * (sg * (1.0 + gate * (1.0 - sg)))).astype(BF)
        dn = dg * gain * act
        do = rstd * (dn - n * jnp.mean(dn * n, axis=-1, keepdims=True))
        do_ref[:, at] = do.astype(BF)
        d = d_ref[h]
        for c in reversed(range(PER)):
            rows = slice(c * CH, (c + 1) * CH)
            dc = mm(qe_ref[rows, h * DK:(h + 1) * DK], do[rows], TL)
            dc_ref[c, h] = dc
            d = mm(m_ref[c, h], d, TL) + dc
        d_ref[h] = d
        last_ref[h] = d.astype(BF)


def delta_states_back(drows, out_t, o, gate, gain, qe, m, tokens, heads):
    n = tokens // CH
    wide = by_rows(heads * DV, n, True)
    return call(
        functools.partial(states_back_kernel, heads), "delta_states_back", n // PER, 7 * tokens // 1024,
        [by_rows(drows.shape[1], n, True), whole(out_t.shape), wide, wide, whole((1, DV)), by_rows(heads * DK, n, True), by_chunk((heads, DK, DK), n, True)],
        [(wide, sds((tokens, heads * DV), BF)), (wide, sds((tokens, heads * DV), BF)),
         (by_chunk((heads, DK, DV), n, True), sds((n, heads, DK, DV))),
         (whole((heads, DK, DV)), sds((heads, DK, DV), BF)), (whole((1, DV)), sds((1, DV)))],
        [pltpu.VMEM((heads, DK, DV), F32)],
        drows, out_t, o, gate, gain, qe, m,
    )


def normed_pull(raw, grad, scale):
    r = lax.rsqrt(jnp.sum(raw * raw, axis=-1, keepdims=True) + 1e-6)
    n = raw * r
    return (scale * r) * (grad - n * jnp.sum(grad * n, axis=-1, keepdims=True))


BACK = 1


def conv_back(dact, at, width, sum_ref, in_ref, taps_ref, out_ref, dtaps_ref, rim_ref):
    where = slice(at, at + width)
    summed = sum_ref[:, where]
    sg = sigmoid(summed)
    dsum = dact * (sg * (1.0 + summed * (1.0 - sg)))
    ext = jnp.concatenate([dsum, rim_ref[:, where]], 0)
    rim_ref[:, where] = dsum[:8]
    conv_in = in_ref[:, where]
    dconv = jnp.zeros((BACK * CH, width), F32)
    for j in range(KC):
        moved = ext[3 - j:3 - j + BACK * CH]
        dconv = dconv + taps_ref[j:j + 1, where] * moved
        dtaps_ref[j:j + 1, where] += jnp.sum(moved * conv_in, axis=0, keepdims=True)
    out_ref[:, where] = dconv.astype(BF)


def rim_back(first_ref, taps_ref, out_ref, out_at, dtaps_ref, rim_ref):
    before = jnp.concatenate([jnp.zeros_like(rim_ref), rim_ref[...]], 0)
    conv_in = first_ref[RIM - 8:]
    drim = jnp.zeros(rim_ref.shape, F32)
    for j in range(KC):
        moved = before[3 - j:3 - j + 8]
        drim = drim + taps_ref[j:j + 1] * moved
        dtaps_ref[j:j + 1] += jnp.sum(moved * conv_in, axis=0, keepdims=True)
    width = rim_ref.shape[1]
    out_ref[:RIM, out_at:out_at + width] = jnp.concatenate([jnp.zeros_like(drim), drim], 0).astype(BF)


def inputs_back_kernel(heads, dc_ref, m_ref, s_ref, do_ref, uv_ref, w_ref, a_ref, tinv_ref, q_ref, k_ref,
                       sum_ref, p_ref, dgate_ref, first_ref, taps_ref, gcol_ref, grow_ref, *refs):
    near, (dall_ref, dtaps_ref, ds_ref, rim_ref) = refs[:-4], refs[-4:]
    last = pl.num_programs(0) - 1

    @pl.when(pl.program_id(0) == 0)
    def _():
        for h in range(heads):
            half = (len(near) - 1) // 2
            ds_ref[h] = entering([a[h] for a in near[:half]], [a[h] for a in near[half:]], ((0,), (0,)))
        for ref in (rim_ref, dtaps_ref):
            ref[...] = jnp.zeros_like(ref)

    @pl.when(pl.program_id(0) == last)
    def _():
        rim_back(first_ref, taps_ref, dall_ref, 0, dtaps_ref, rim_ref)
        dall_ref[:RIM, 2 * heads * DV:] = jnp.zeros((RIM, heads * DV), BF)

    @pl.when(pl.program_id(0) < last)
    def _():
        rows, cols = square_index()
        dall_ref[:, 2 * heads * DV:] = dgate_ref[...]
        for h in range(heads):
            ds = ds_ref[h]
            key, val = slice(h * DK, (h + 1) * DK), slice(h * DV, (h + 1) * DV)
            dqs, dks, dvs = [None] * BACK, [None] * BACK, [None] * BACK
            for c in reversed(range(BACK)):
                at = slice(c * CH, (c + 1) * CH)
                s, do, q, k = s_ref[c, h], do_ref[at, val], q_ref[at, key], k_ref[at, key]
                gcol, beta = gcol_ref[at, h:h + 1], gcol_ref[at, heads + h:heads + h + 1]
                grow = grow_ref[c, h:h + 1, :]
                glast = grow[:, CH - 1:CH]
                ratio = jnp.exp(jnp.where(rows >= cols, gcol - grow, -1e30))
                eg = jnp.exp(gcol)
                el = jnp.exp(glast - gcol)
                u = uv_ref[at, val] - mm(w_ref[at, key], s)
                du = mm(a_ref[c, h], do, TL) + el * mm(k, ds)
                da = ratio * mm(do, u, TT)
                drv = mm(tinv_ref[c, h], du, TL)
                dl = jnp.where(rows > cols, (-beta) * ratio * mm(drv, u, TT), 0.0)
                dqs[c] = eg * mm(do, s, TT) + mm(da, k)
                dks[c] = (
                    el * mm(u, ds, TT) + mm(da, q, TL) - (beta * eg) * mm(drv, s, TT) + mm(dl, k) + mm(dl, k, TL)
                )
                dvs[c] = beta * drv
                ds = mm(m_ref[c, h], ds, TL) + dc_ref[c, h]
            ds_ref[h] = ds
            summed = sum_ref[:, 2 * h * DK:2 * (h + 1) * DK]
            act = summed * sigmoid(summed)
            dq, dk, dv = (jnp.concatenate(a, 0) for a in (dqs, dks, dvs))
            dact = jnp.concatenate([normed_pull(act[:, :DK], dq, DK ** -0.5), normed_pull(act[:, DK:], dk, 1.0)], 1)
            conv_back(dact, 2 * h * DK, 2 * DK, sum_ref, p_ref, taps_ref, dall_ref, dtaps_ref, rim_ref)
            conv_back(dv, (heads + h) * DV, DV, sum_ref, p_ref, taps_ref, dall_ref, dtaps_ref, rim_ref)


def delta_inputs_back(near, dc, m, s, do, uv, w, a, tinv, q, k, summed, p, dgate, first, taps, gcol, grow,
                      tokens, heads):
    n = tokens // CH

    def at(c):
        return jnp.maximum(n // BACK - 1 - c, 0)

    def rows(width):
        return pl.BlockSpec((BACK * CH, width), lambda c: (at(c), 0))

    def chunk(shape):
        return pl.BlockSpec((BACK,) + shape, lambda c: (at(c),) + (0,) * len(shape))

    width = heads * DV
    wide, key = rows(width), rows(heads * DK)
    steps = n // BACK
    out = pl.BlockSpec((BACK * CH, 3 * width), lambda c: (jnp.where(c == steps, steps, steps - 1 - c), 0))
    return call(
        functools.partial(inputs_back_kernel, heads), "delta_inputs_back", steps + 1, 19 * tokens // 1024,
        [chunk((heads, DK, DV)), chunk((heads, DK, DK)), chunk((heads, DK, DV)),
         wide, wide, key, chunk((heads, CH, CH)), chunk((heads, CH, CH)), key, key,
         rows(2 * width), rows(2 * width), wide, whole(first.shape), whole(taps.shape), rows(gcol.shape[1]),
         chunk(grow.shape[1:])] + [whole(a.shape) for a in near],
        [(out, sds((tokens + RIM, 3 * width), BF)),
         (whole(taps.shape), sds(taps.shape))],
        [pltpu.VMEM((heads, DK, DV), F32), pltpu.VMEM((8, 2 * width), F32)],
        dc, m, s, do, uv, w, a, tinv, q, k, summed, p, dgate, first, taps, gcol, grow, *near,
    )


def as_column(row):
    size = row.shape[1]
    found = []
    for at in range(0, size, CH):
        part = row[:, at:min(at + CH, size)]
        if part.shape[1] < CH:
            part = jnp.concatenate([part, jnp.zeros((1, CH - part.shape[1]), F32)], 1)
        found.append(jnp.broadcast_to(part, (CH, CH)).T[:min(CH, size - at), 0:1])
    return jnp.concatenate(found, 0)


def moments_kernel(plan, over_head_ref, over_seq_ref, old_ref, carried_ref, place_ref, conv_second_ref,
                   both_ref, go_ref, outg_ref, ex_ref, sh_ref, *outs):
    beta_two = 1.0 - STEP ** (-0.8)
    (in_rows, in_cols, out_rows, out_cols, ex_rows, ex_cols, sh_rows, sh_cols, late_ref, kernel_ref, second_ref, update_ref,
     in_row, in_col, out_row, out_col, ex_row, ex_col, sh_row, sh_col) = outs
    heads = in_cols.shape[0]
    span = in_rows.shape[1]
    place = lax.broadcasted_iota(jnp.int32, (1, 128), 1)
    sums = carried_ref[...]
    sources = {"head": over_head_ref, "seq": over_seq_ref}

    def moment(name, old_at):
        axis, start, size, over = plan["cells"][name]
        old = old_ref[:, old_at:old_at + size]
        new = beta_two * old + (1.0 - beta_two) * (sources[axis][:, start:start + size] * (1.0 / over) + 1e-30)
        return new, lax.rsqrt(new)

    parts = {
        "in": (both_ref[:span], both_ref[span:], go_ref[:span]),
        "out": (outg_ref[...],),
        "expand": (ex_ref[...].astype(F32),),
        "shrink": (sh_ref[...].astype(F32),),
    }
    refs = {
        "in": (in_rows, in_cols, in_row, in_col), "out": (out_rows, out_cols, out_row, out_col),
        "expand": (ex_rows, ex_cols, ex_row, ex_col), "shrink": (sh_rows, sh_cols, sh_row, sh_col),
    }
    for slot, name in enumerate(parts):
        rows_new, row_root = moment(name + "_rows", plan["old"][name + "_rows"])
        cols_new, col_root = moment(name + "_cols", plan["old"][name + "_cols"])
        rows_ref, cols_ref, row_ref, col_ref = refs[name]
        column = as_column(row_root)
        row_ref[...] = column
        col_ref[...] = col_root
        total, start = 0.0, 0
        for part in parts[name]:
            size = part.shape[1]
            update = part * column * col_root[:, start:start + size]
            total = total + jnp.sum(update * update, axis=(0, 1), keepdims=True)
            start += size
        sums = sums + jnp.where(place == slot, total, 0.0)
        row_total = jnp.sum(rows_new, axis=(0, 1), keepdims=True) * (1.0 / plan["copies"][name])
        sums = sums + jnp.where(place == 4 + slot, row_total, 0.0)
        if name == "in":
            rows_ref[...] = rows_new
            width = heads * DV
            for h in range(heads):
                for i in range(3):
                    cols_ref[h:h + 1, i * DV:(i + 1) * DV] = cols_new[:, i * width + h * DV:i * width + (h + 1) * DV]
        elif name == "out":
            cols_ref[...] = cols_new
            for h in range(heads):
                rows_ref[h:h + 1] = rows_new[:, h * DV:(h + 1) * DV]
        elif name == "expand":
            rows_ref[...] = rows_new
            size = cols_ref.shape[1]
            for i in range(2):
                cols_ref[i:i + 1] = cols_new[:, i * size:(i + 1) * size]
        else:
            rows_ref[...] = rows_new
            cols_ref[...] = cols_new
    axis, start, _, _ = plan["cells"]["taps"]
    cut, width = kernel_ref.shape[2], heads * DV
    total = 0.0
    for j in range(KC):
        for h in range(heads):
            grad = jnp.zeros((1, cut), F32)
            for c in range(CW // cut):
                at = start + j * 2 * width + (c * cut) // DV * width + h * DV + (c * cut) % DV
                grad = grad + place_ref[0:1, c:c + 1] * sources[axis][:, at:at + cut]
            second = beta_two * conv_second_ref[j, h:h + 1, :] + (1.0 - beta_two) * (grad * grad + 1e-30)
            update = grad * lax.rsqrt(second)
            kernel_ref[j, h:h + 1, :] = grad
            second_ref[j, h:h + 1, :] = second
            update_ref[j, h:h + 1, :] = update
            total = total + jnp.sum(update * update, axis=(0, 1), keepdims=True)
    late_ref[:, :128] = sums + jnp.where(place == 13, total, 0.0)
    share = 1.0 / plan["head_count"]
    for name, at in (("gain_two", 128), ("head_gain", 128 + D)):
        axis, start, size, _ = plan["cells"][name]
        late_ref[:, at:at + size] = sources[axis][:, start:start + size] * share


def new_moments(plan, outs, operands):
    return pl.pallas_call(
        functools.partial(moments_kernel, plan),
        out_shape=[sds(a) for a in outs],
        compiler_params=pltpu.CompilerParams(vmem_limit_bytes=56 * 1024 * 1024),
        name="new_moments",
    )(*operands)


def cast_kernel(heads, in_ref, kv_ref, gate_ref):
    width = heads * DV
    for h in range(heads):
        at = slice(h * DV, (h + 1) * DV)
        kv_ref[:, at] = in_ref[:, h, :DV].astype(BF)
        kv_ref[:, width + h * DV:width + (h + 1) * DV] = in_ref[:, h, DV:2 * DV].astype(BF)
        gate_ref[:, at] = in_ref[:, h, 2 * DV:].astype(BF)


def cast_columns(weight, steps=4):
    heads, span = weight.shape[1], weight.shape[0] // steps
    width = heads * DV
    return call(
        functools.partial(cast_kernel, heads), "cast_columns", steps, 3,
        [pl.BlockSpec((span, heads, HC), lambda c: (c, 0, 0))],
        [(pl.BlockSpec((span, size), lambda c: (c, 0)), sds((weight.shape[0], size), BF)) for size in (2 * width, width)],
        [],
        weight,
    )


def joined_kernel(heads, keys_ref, vals_ref, gate_ref, out_ref):
    for h in range(heads):
        at = slice(h * DV, (h + 1) * DV)
        for i, ref in enumerate((keys_ref, vals_ref, gate_ref)):
            out_ref[:, h, i * DV:(i + 1) * DV] = ref[:, at]


def joined_columns(both, go, heads, steps=4):
    span, width = both.shape[0] // (2 * steps), both.shape[1]
    first = pl.BlockSpec((span, width), lambda c: (c, 0))
    return call(
        functools.partial(joined_kernel, heads), "joined_columns", steps, 3,
        [first, pl.BlockSpec((span, width), lambda c: (c + steps, 0)), first],
        [(pl.BlockSpec((span, heads, HC), lambda c: (c, 0, 0)), sds((both.shape[0] // 2, heads, HC)))],
        [],
        both, both, go,
    )[0]


def split_kernel(grad_ref, out_ref):
    size = out_ref.shape[2]
    for i in range(2):
        out_ref[:, i, :] = grad_ref[:, i * size:(i + 1) * size].astype(F32)


def split_columns(grad, steps=4):
    span, size = grad.shape[0] // steps, grad.shape[1] // 2
    return call(
        split_kernel, "split_columns", steps, 3,
        [pl.BlockSpec((span, 2 * size), lambda c: (c, 0))],
        [(pl.BlockSpec((span, 2, size), lambda c: (c, 0, 0)), sds((grad.shape[0], 2, size)))],
        [],
        grad,
    )[0]


def small_step(weight, gradient, second_old, beta_two):
    second_new = beta_two * second_old + (1.0 - beta_two) * (gradient * gradient + 1e-30)
    update = gradient * lax.rsqrt(second_new)
    root = jnp.sqrt(jnp.mean(update * update, axis=-1, keepdims=True))
    scale = 0.3 * jnp.maximum(0.001, jnp.sqrt(jnp.mean(weight * weight, axis=-1, keepdims=True)))
    return second_new, weight - scale * (update / jnp.maximum(1.0, root))


def weights_kernel(heads, late_ref, gains_ref, gains_second_ref, head_ref, head_second_ref, conv_ref, conv_update_ref,
                   in_ref, keys_ref, vals_ref, gate_ref, in_row, in_col, out_ref, outg_ref, out_row, out_col,
                   ex_ref, exg_ref, ex_row, ex_col, sh_ref, shg_ref, sh_row, sh_col,
                   gains_grad, gains_second_new, gains_new, head_grad, head_second_new, head_new, conv_new,
                   in_new, out_new, ex_new, sh_new):
    beta_two = 1.0 - STEP ** (-0.8)
    counts = ((D, HEAD_TOTAL * HC), (HEAD_TOTAL * DV, D), (D, 2 * FF), (FF, D))

    def cell(at):
        return late_ref[0:1, at:at + 1]

    def size_of(weight, entries):
        return 0.3 * jnp.maximum(0.001, jnp.sqrt(weight * (1.0 / entries)))

    def scale(slot):
        mean, entries = cell(4 + slot) * (1.0 / counts[slot][0]), counts[slot][0] * counts[slot][1]
        root = jnp.sqrt(cell(slot) * mean * (1.0 / entries))
        return size_of(cell(8 + slot), entries) * jnp.sqrt(mean) / jnp.maximum(1.0, root)

    scales = [scale(slot) for slot in range(4)]

    @pl.when(pl.program_id(0) == 0)
    def _():
        for row in range(2):
            first = 128 if row else 128 + D + DV
            grad = late_ref[0:1, first:first + D]
            at = slice(row, row + 1)
            gains_grad[at] = grad
            gains_second_new[at], gains_new[at] = small_step(gains_ref[at], grad, gains_second_ref[at], beta_two)
        grad = late_ref[0:1, 128 + D:128 + D + DV]
        head_grad[...] = grad
        head_second_new[...], head_new[...] = small_step(head_ref[...], grad, head_second_ref[...], beta_two)
        entries = KC * HEAD_TOTAL * CW
        factor = size_of(cell(12), entries) / jnp.maximum(1.0, jnp.sqrt(cell(13) * (1.0 / entries)))
        conv_new[...] = conv_ref[...] - conv_update_ref[...] * factor[None]

    def stepped(weight, grad, rows, cols, slot):
        return weight - (grad.astype(F32) * cols) * (rows * scales[slot])

    width = heads * DV
    for h in range(heads):
        for i, ref in enumerate((keys_ref, vals_ref, gate_ref)):
            col = in_col[:, i * width + h * DV:i * width + (h + 1) * DV]
            at = slice(i * DV, (i + 1) * DV)
            in_new[:, h, at] = stepped(in_ref[:, h, at], ref[:, h * DV:(h + 1) * DV], in_row[...], col, 0)
    out_new[...] = stepped(out_ref[...], outg_ref[...], out_row[...], out_col[...], 1)
    size = ex_ref.shape[2]
    for i in range(2):
        at = slice(i * size, (i + 1) * size)
        ex_new[:, i, :] = stepped(ex_ref[:, i, :], exg_ref[:, at], ex_row[...], ex_col[:, at], 2)
    sh_new[...] = stepped(sh_ref[...], shg_ref[...], sh_row[...], sh_col[...], 3)


def new_weights(heads, small, groups):
    ins, operands = [whole(a.shape) for a in small], list(small)
    late, gains, _, head = small[:4]
    outs = [(whole(a.shape), sds(a.shape)) for a in (gains, gains, gains, head, head, head, small[5])]
    steps = 8 if groups[3][0].shape[0] % 128 == 0 else 4

    def blocked(a, span, first=0):
        tail = a.shape[1:]
        return pl.BlockSpec((span,) + tail, lambda c: (c + first,) + (0,) * len(tail))

    for weight, parts, rows, cols in groups:
        span = weight.shape[0] // steps
        for i, a in enumerate((weight, *parts, rows)):
            ins.append(blocked(a, span, steps if len(parts) == 3 and i == 2 else 0))
            operands.append(a)
        ins.append(whole(cols.shape))
        operands.append(cols)
        outs.append((blocked(weight, span), sds(weight.shape)))
    return call(functools.partial(weights_kernel, heads), "new_weights", steps, 10, ins, outs, [], *operands, room=56)


def ring(x, by=1):
    n = lax.axis_size("seq")
    return lax.ppermute(x, "seq", [(i, (i + by) % n) for i in range(n)])


def ahead(x, by):
    n = lax.axis_size("seq")
    return lax.ppermute(x, "seq", [(i, i + by) for i in range(n) if 0 <= i + by < n])


def after(x, *others):
    return lax.optimization_barrier((x,) + others)[0]


def ring_gather(x, hold=None):
    slots = [x]
    for k in range(1, lax.axis_size("seq")):
        slots.append(ring(after(slots[-1], *(hold or {}).get(k, ()))))
    return slots


def vector_of(scalars, size, first=0):
    place = lax.broadcasted_iota(jnp.int32, (1, size), 1)
    return sum(jnp.where(place == first + i, a, 0.0) for i, a in enumerate(scalars))


def ring_scatter(part, hold=None):
    n = lax.axis_size("seq")
    total, totals = part(1).astype(BF), []
    for k in range(1, n):
        held = hold(k) if hold else ()
        total = ring(after(total, *held) if held else total).astype(F32) + part((k + 1) % n).astype(F32)
        total = total if k == n - 1 else total.astype(BF)
        totals.append(total)
    return total, totals


def seq_slot(x, k, axis=0):
    n, z = lax.axis_size("seq"), lax.axis_index("seq")
    span = x.shape[axis] // n
    return lax.dynamic_slice_in_dim(x, lax.rem(z - k + n, n) * span, span, axis)


def in_order(slots, axis=0):
    n, z = lax.axis_size("seq"), lax.axis_index("seq")
    span = slots[0].shape[axis]
    turned = jnp.concatenate(slots[::-1] + slots[:0:-1], axis)
    return lax.dynamic_slice_in_dim(turned, (n - 1 - z) * span, n * span, axis)


def gather_head(x, axis=0):
    return lax.all_gather(x, "head", axis=axis, tiled=True)


def scatter_head(x, axis=0):
    return lax.psum_scatter(x, "head", scatter_dimension=axis, tiled=True)


def total_over(axis, x):
    n = lax.axis_size(axis)
    if n & (n - 1):
        return lax.psum(x, axis)
    step = 1
    while step < n:
        x = x + lax.ppermute(x, axis, [(i, i ^ step) for i in range(n)])
        step *= 2
    return x


def dot(a, b, dims=((1,), (0,)), out=F32):
    return lax.dot_general(a, b, (dims, ((), ())), preferred_element_type=out)


def norm_rows(entries, scale_row):
    return entries * lax.rsqrt(jnp.mean(entries * entries, axis=-1, keepdims=True) + 1e-06) * scale_row


def nearby(last):
    n = lax.axis_size("seq")
    return [ahead(last, k) for k in range(1, n - 1)] + [ahead(last[..., DK:], n - 1)]


def local(
    hidden_in,
    out_grad,
    decays,
    strength,
    mixer_in,
    mixer_in_rows,
    mixer_in_cols,
    mixer_out,
    mixer_out_rows,
    mixer_out_cols,
    feed_in,
    feed_in_rows,
    feed_in_cols,
    feed_out,
    feed_out_rows,
    feed_out_cols,
    conv_kernel,
    conv_second,
    norm_gains,
    gains_second,
    head_gain,
    head_gain_second,
):
    beta_two = 1.0 - STEP ** (-0.8)
    n = lax.axis_size("seq")
    seq_count, head_count = n, lax.axis_size("head")
    tokens, heads = decays.shape
    blocks = tokens // CH
    in_span = mixer_in.shape[0]
    out_span = mixer_out.shape[2]
    feed_span, hidden_span = feed_in.shape[0], feed_in.shape[2]
    width = heads * DV

    def padded(pieces):
        found, cells, at = [], {}, 0
        for name, piece in pieces.items():
            piece = piece.reshape(1, -1)
            size = piece.shape[1]
            room = -(-size // 128) * 128
            found.append(jnp.pad(piece, ((0, 0), (0, room - size))))
            cells[name] = (at, size)
            at += room
        return jnp.concatenate(found, 1), cells

    old_moments, old_cells = padded(
        {
            "in_rows": mixer_in_rows,
            "in_cols": jnp.stack([mixer_in_cols[:, i * DV : (i + 1) * DV] for i in range(3)]),
            "out_rows": mixer_out_rows,
            "out_cols": mixer_out_cols,
            "expand_rows": feed_in_rows,
            "expand_cols": feed_in_cols,
            "shrink_rows": feed_out_rows,
            "shrink_cols": feed_out_cols,
        }
    )
    over_counts = {
        "in_rows": HEAD_TOTAL * HC, "in_cols": D, "out_rows": D, "out_cols": HEAD_TOTAL * DV,
        "expand_rows": 2 * FF, "expand_cols": D, "shrink_rows": D, "shrink_cols": FF,
    }
    place = jnp.where(lax.broadcasted_iota(jnp.int32, (1, 128), 1) == lax.axis_index("seq"), 1.0, 0.0)

    x = hidden_in.astype(F32)
    rows_all = gather_head(norm_rows(x, norm_gains[0]).astype(BF))
    kv_own, gate_own = cast_columns(mixer_in)
    taps_mine = conv_kernel.astype(BF).reshape(KC, heads * conv_kernel.shape[2])
    taps_slots = [taps_mine] + [ring(taps_mine, k) for k in range(1, n)]
    kv_slots = ring_gather(kv_own, {1: taps_slots[1:]})[:3]
    rim = ahead(rows_all[tokens - RIM :], 1)
    taps = in_order([t[None] for t in taps_slots]).reshape(n, KC, heads, -1)
    taps = jnp.moveaxis(taps, 0, 2).reshape(KC, heads, CW).astype(F32)
    taps = jnp.concatenate([taps[:, :, : 2 * DK].reshape(KC, width), taps[:, :, 2 * DK :].reshape(KC, width)], 1)

    lower = jnp.tril(jnp.ones((CH, CH), F32))
    log_sum = jnp.einsum(
        "ij,bjh->bih", lower, jnp.log(decays).reshape(blocks, CH, heads), precision=lax.Precision.HIGHEST
    )
    gcol = jnp.concatenate([log_sum.reshape(tokens, heads), strength, jnp.zeros((tokens, 8 - 2 * heads), F32)], 1)
    grow = jnp.concatenate([jnp.swapaxes(log_sum, 1, 2), jnp.zeros((blocks, 8 - heads, CH), F32)], 1)
    gain_row = head_gain[None]
    row_slots = [seq_slot(rows_all, k, 1) for k in range(n)]

    def projected(parts, slots, total=None):
        for part, slot in zip(parts, slots):
            found = dot(part, slot)
            total = found if total is None else total + found
        return total

    expand = gather_head(after(feed_in.astype(BF).reshape(feed_span, 2 * hidden_span), rows_all, kv_slots[1]))
    p_start = projected(row_slots[:2], kv_slots[:2])
    kv_held, p_start, rim = lax.optimization_barrier((kv_slots[2], p_start, rim))
    kv_slots[2] = kv_held
    for _ in range(3, n):
        kv_slots.append(ring(kv_slots[-1]))
    rim_slots = [seq_slot(rim, k, 1) for k in range(n)]
    p_kv, r_kv = projected(row_slots[2:], kv_slots[2:], p_start), projected(rim_slots, kv_slots)
    go_own = jnp.concatenate([gate_own, mixer_out.astype(BF).reshape(width, out_span).T], 0)
    go_slots = ring_gather(go_own, {1: (kv_slots[-1],)})[:2]
    (summed, q, k, tinv, scores, w, uv, qe, oz, m, pre, last) = delta_parts(
        p_kv, r_kv, taps, gcol, grow, tokens, heads
    )
    last, go_one, go_zero, expand = lax.optimization_barrier((last, go_slots[1], go_slots[0], expand))
    go_slots = [go_zero, go_one]
    for _ in range(2, n):
        go_slots.append(ring(go_slots[-1]))
    shrink = gather_head(after(feed_out.astype(BF), expand, last, go_slots[2]), 1)
    p_gate = projected(row_slots, [a[:in_span] for a in go_slots])
    states, o, gated, mixed = delta_outputs(
        nearby(last), go_slots, pre, qe, oz, p_gate, gain_row, in_span, tokens, heads
    )
    maps_after = [ahead(last[..., :DK], -k) for k in range(1, n - 1)]
    grad_slots = ring_gather(out_grad, {1: (go_slots[-1],), 2: maps_after})
    grad_rows = jnp.concatenate(grad_slots, 0)
    mixed = scatter_head(after(mixed, shrink)).astype(F32)
    mixed = in_order([mixed[:, i * out_span : (i + 1) * out_span] for i in range(n)], 1)
    residual = x + mixed
    out_t = in_order([a[in_span:] for a in go_slots])
    w_all = in_order([jnp.concatenate([a, b[:in_span]], 1) for a, b in zip(kv_slots, go_slots)])
    weights_then = lax.optimization_barrier((mixer_in, mixer_out, feed_in, feed_out, gated))[:4]
    weight_sums = vector_of([jnp.sum(a * a) for a in (*weights_then, conv_kernel)], 128, 8)

    normed_two, norm_two_pull = jax.vjp(norm_rows, residual, norm_gains[1])
    d_hidden = lax.optimization_barrier(dot(grad_rows, shrink, ((1,), (1,))))
    feed_held, out_t, w_all, weight_sums, old_moments = lax.optimization_barrier(
        (normed_two.astype(BF), out_t, w_all, weight_sums, old_moments)
    )
    rows_here = hidden_in.shape[0]

    def slot_rows(a, k):
        return a[k * rows_here : (k + 1) * rows_here]

    def fed(rows, first):
        gate_up = dot(rows, expand)
        gate, up = gate_up[:, :hidden_span], gate_up[:, hidden_span:]
        d_here = d_hidden[first * rows_here : first * rows_here + rows.shape[0]]
        sig = sigmoid(gate)
        silu = gate * sig
        d_gate_up = jnp.concatenate([d_here * up * (sig * (1.0 + gate * (1.0 - sig))), d_here * silu], 1).astype(BF)
        return (silu * up).astype(BF), d_gate_up, dot(d_gate_up, expand, ((1,), (1,)))

    feed_slots = ring_gather(feed_held, {1: (grad_slots[-1],), 2: (d_hidden,)})[:3]
    hidden_one, d_gate_up_one, d_feed_one = fed(jnp.concatenate(feed_slots[:2], 0), 0)
    feed_held, d_feed_one = lax.optimization_barrier((feed_slots[2], d_feed_one))
    feed_slots[2] = feed_held
    for _ in range(3, n):
        feed_slots.append(ring(feed_slots[-1]))
    shrink_sum = ring(slot_rows(d_feed_one, 1).astype(BF))
    feed_rows = jnp.concatenate(feed_slots, 0)
    hidden_two, d_gate_up_two, d_feed_two = fed(jnp.concatenate(feed_slots[2:], 0), 2)
    hidden = jnp.concatenate([hidden_one, hidden_two], 0)
    d_gate_up = jnp.concatenate([d_gate_up_one, d_gate_up_two], 0)
    for step in range(2, n):
        shrink_sum = ring((shrink_sum.astype(F32) + slot_rows(d_feed_two, step - 2)).astype(BF))
    d_normed_two = shrink_sum.astype(F32) + slot_rows(d_feed_one, 0)
    d_residual_part, d_gain_two = norm_two_pull(d_normed_two)
    d_residual = out_grad.astype(F32) + d_residual_part
    d_residual_low = d_residual.astype(BF)
    d_rows = gather_head(d_residual_low)
    hidden_then, feed_rows_then, _ = lax.optimization_barrier((hidden, feed_rows, d_residual_low))
    shrink_part = dot(hidden_then, grad_rows, ((0,), (0,)), BF)
    feed_part = dot(hidden_then, shrink, out=BF)
    feed_part = in_order([slot_rows(feed_part, i) for i in range(n)])
    expand_part = dot(feed_rows_then, d_gate_up, ((0,), (0,)), BF)
    shrink_part, expand_part, feed_part, d_rows = lax.optimization_barrier(
        (shrink_part, expand_part, feed_part, d_rows)
    )
    shrink_low = scatter_head(shrink_part, 1)

    do, d_gate, dc, d_last, d_head_gain = delta_states_back(d_rows, out_t, o, p_gate, gain_row, qe, m, tokens, heads)
    near = maps_after + [ahead(d_last, -k) for k in range(1, n)]
    gate_then, d_rows_then, _ = lax.optimization_barrier((d_gate, d_rows, d_last))

    def go_part(k, out=F32, rows=d_rows_then):
        d_slot = seq_slot(rows, k, 1)
        return jnp.concatenate([dot(row_slots[k], gate_then, TL, out), dot(d_slot, gated, TL, out)], 0)

    def added(arrived, part):
        return arrived.astype(F32) + part.astype(F32)

    go, go_next = lax.optimization_barrier((go_part(1, BF), go_part(2 % n), *near))[:2]
    sent = ring(go)
    d_all, d_taps = delta_inputs_back(
        near, dc, m, states, do, uv, w, scores, tinv, q, k, summed, p_kv, d_gate, r_kv, taps, gcol, grow, tokens, heads
    )
    d_all, sent, go_next, gate_then, d_rows_then = lax.optimization_barrier(
        (d_all, sent, go_next, gate_then, d_rows_then)
    )
    more_slots = [jnp.concatenate([a, b], 0) for a, b in zip(row_slots, rim_slots)]

    def both_dots(k, out):
        return [dot(more_slots[k], d_all[:, i * width : (i + 1) * width], TL, out) for i in range(2)]

    def both_part(k, out=F32):
        return jnp.concatenate(both_dots(k, out), 0)

    first_dots = both_dots(1, BF)
    go = added(sent, go_next).astype(BF)
    sending = jnp.concatenate([go, *first_dots], 0)
    d_all_then, sending = lax.optimization_barrier((d_all, sending))
    sent = ring(sending)
    d_rows_more = dot(d_all_then, w_all, ((1,), (1,)), BF)
    expand_low = scatter_head(after(expand_part, shrink_low, sending))
    shrink_g, expand_g = shrink_low.astype(F32), expand_low.astype(F32)
    parts = [jnp.concatenate([go_part((step + 1) % n, F32, d_rows_then), both_part(step)], 0) for step in range(2, n)]
    rim_rows, last_part, *parts = lax.optimization_barrier((d_rows_more[tokens:], both_part(0), *parts))
    rim_back = ahead(rim_rows, -1)
    d_rows_in = jnp.concatenate([d_rows_more[: tokens - RIM], d_rows_more[tokens - RIM : tokens] + rim_back], 0)
    feed_sums = (jnp.sum(expand_g * expand_g, 0), jnp.sum(shrink_g * shrink_g, 1))
    feed_sums += (jnp.sum(expand_g * expand_g, 1), jnp.sum(shrink_g * shrink_g, 0))
    for step in range(2, n):
        gone, part = sent, parts[step - 2]
        if step < n - 1:
            sent = ring(added(gone, part).astype(BF))
    d_normed_low = scatter_head(after(d_rows_in, expand_low, sent))
    both = added(gone[2 * in_span :], part[2 * in_span :]).astype(BF)
    last_sent = ring(both)
    go = added(gone[: 2 * in_span], part[: 2 * in_span])
    go, last_sent, *feed_sums = lax.optimization_barrier((go, last_sent, *feed_sums))
    both_grad = added(last_sent, last_part)
    go = lax.optimization_barrier(go)
    out_g = lax.optimization_barrier(go[in_span:].T)
    d_normed = d_normed_low.astype(F32)

    _, norm_one_pull = jax.vjp(norm_rows, x, norm_gains[0])
    d_residual_one, d_gain_one = norm_one_pull(d_normed)
    input_grad = d_residual + d_residual_one


    out_sq, both_sq, gate_sq = out_g * out_g, both_grad * both_grad, go[:in_span] * go[:in_span]
    over_head, head_cells = padded(
        {
            "expand_cols": feed_sums[0],
            "shrink_rows": feed_sums[1],
            "gain_two": d_gain_two,
            "head_gain": d_head_gain,
            "out_cols": jnp.sum(out_sq, 0),
            "in_rows": jnp.sum(both_sq[:in_span], 1) + jnp.sum(both_sq[in_span:], 1) + jnp.sum(gate_sq, 1),
        }
    )
    over_seq, seq_cells = padded(
        {
            "expand_rows": feed_sums[2],
            "shrink_cols": feed_sums[3],
            "taps": d_taps,
            "out_rows": jnp.sum(out_sq, 1),
            "in_cols": jnp.concatenate([jnp.sum(a, 0) for a in (both_sq[:in_span], both_sq[in_span:], gate_sq)]),
        }
    )
    both_then, over_head, over_seq = lax.optimization_barrier((both_grad, over_head, over_seq))
    in_grad = joined_columns(both_then, go, heads)
    expand_out = split_columns(expand_low)
    over_head, over_seq = total_over("head", over_head), total_over("seq", over_seq)

    cells = {}
    for axis, found in (("head", head_cells), ("seq", seq_cells)):
        for name, (at, size) in found.items():
            cells[name] = (axis, at, size, over_counts.get(name))
    plan = {
        "cells": cells,
        "old": {name: at for name, (at, _) in old_cells.items()},
        "copies": {"in": head_count, "out": seq_count, "expand": seq_count, "shrink": head_count},
        "head_count": head_count,
    }
    shape = {name: (1, size) for name, (_, _, size, _) in cells.items()}
    conv_shape = conv_kernel.shape
    (in_rows_new, in_cols_new, out_rows_new, out_cols_new, expand_rows_new, expand_cols_new, shrink_rows_new,
     shrink_cols_new, late, kernel_grad, conv_second_new, conv_update, *roots) = new_moments(
        plan,
        [shape["in_rows"], (heads, HC), (heads, DV), shape["out_cols"], shape["expand_rows"], (2, hidden_span),
         shape["shrink_rows"], shape["shrink_cols"], (1, 128 + D + DV), conv_shape, conv_shape, conv_shape]
        + [a for name in ("in", "out", "expand", "shrink") for a in ((shape[name + "_rows"][1], 1), shape[name + "_cols"])],
        [over_head, over_seq, old_moments, weight_sums, place, conv_second,
         both_grad, go, out_g, expand_low, shrink_low],
    )
    feed_sum = lax.psum_scatter(after(feed_part, d_normed_low, late), "seq", scatter_dimension=0, tiled=True).astype(F32)
    block_out = (residual + feed_sum).astype(BF)

    late = total_over("seq", total_over("head", jnp.concatenate([late, d_gain_one[None]], 1)))
    (gains_grad, gains_second_new, gains_new, head_gain_grad, head_second_new, head_new, conv_new,
     in_new, out_new, expand_new, shrink_new) = new_weights(
        heads,
        (late, norm_gains, gains_second, head_gain[None], head_gain_second[None], conv_kernel, conv_update),
        [
            (mixer_in, (both_grad, both_grad, go), *roots[0:2]),
            (mixer_out.reshape(width, out_span), (out_g,), *roots[2:4]),
            (feed_in, (expand_low,), *roots[4:6]),
            (feed_out, (shrink_low,), *roots[6:8]),
        ],
    )
    return (
        block_out,
        input_grad,
        in_grad,
        in_rows_new.reshape(-1),
        in_cols_new,
        in_new,
        out_g.reshape(mixer_out.shape),
        out_rows_new,
        out_cols_new.reshape(-1),
        out_new.reshape(mixer_out.shape),
        expand_out,
        expand_rows_new.reshape(-1),
        expand_cols_new,
        expand_new,
        shrink_g,
        shrink_rows_new.reshape(-1),
        shrink_cols_new.reshape(-1),
        shrink_new,
        kernel_grad,
        conv_second_new,
        conv_new,
        gains_grad,
        gains_second_new,
        gains_new,
        head_gain_grad.reshape(-1),
        head_second_new.reshape(-1),
        head_new.reshape(-1),
    )


def solution(mesh):
    return jax.shard_map(
        local,
        mesh=mesh,
        in_specs=(
            P(("seq", "head"), None),
            P(("seq", "head"), None),
            P("seq", "head"),
            P("seq", "head"),
            P("seq", "head", None),
            P("seq"),
            P("head", None),
            P("head", None, "seq"),
            P("head", None),
            P("seq"),
            P("head", None, "seq"),
            P("head"),
            P(None, "seq"),
            P("seq", "head"),
            P("seq"),
            P("head"),
            P(None, "head", "seq"),
            P(None, "head", "seq"),
            P(),
            P(),
            P(),
            P(),
        ),
        out_specs=(
            P(("seq", "head"), None),
            P(("seq", "head"), None),
            P("seq", "head", None),
            P("seq"),
            P("head", None),
            P("seq", "head", None),
            P("head", None, "seq"),
            P("head", None),
            P("seq"),
            P("head", None, "seq"),
            P("head", None, "seq"),
            P("head"),
            P(None, "seq"),
            P("head", None, "seq"),
            P("seq", "head"),
            P("seq"),
            P("head"),
            P("seq", "head"),
            P(None, "head", "seq"),
            P(None, "head", "seq"),
            P(None, "head", "seq"),
            P(),
            P(),
            P(),
            P(),
            P(),
            P(),
        ),
        check_vma=False,
    )
```

```python
import functools
import jax
import jax.numpy as jnp
import numpy as np
from jax import lax
from jax.experimental import pallas as pl
from jax.experimental.pallas import tpu as pltpu
from jax.sharding import PartitionSpec as P

D = 2048
HEAD_TOTAL = 16
DK = 128
DV = 256
FF = 5632
KC = 4
STEP = 10
CH = 128
RIM = 16
HC = 2 * DK + 2 * DV
CW = 2 * DK + DV
F32 = jnp.float32
BF = jnp.bfloat16
TT = ((1,), (1,))
TL = ((0,), (0,))


def mm(a, b, dims=((1,), (0,))):
    return lax.dot_general(a.astype(BF), b.astype(BF), (dims, ((), ())), preferred_element_type=F32)


def mm3(a, b, dims=((1,), (0,))):
    ah, bh = a.astype(BF), b.astype(BF)
    al, bl = (a - ah.astype(F32)).astype(BF), (b - bh.astype(F32)).astype(BF)
    one = functools.partial(lax.dot_general, dimension_numbers=(dims, ((), ())), preferred_element_type=F32)
    return one(ah, bh) + (one(ah, bl) + one(al, bh))


def sigmoid(v):
    return 1.0 / (1.0 + jnp.exp(-v))


def square_index():
    rows = lax.broadcasted_iota(jnp.int32, (CH, CH), 0)
    cols = lax.broadcasted_iota(jnp.int32, (CH, CH), 1)
    return rows, cols


def invert(strict, rows, cols):
    apart = rows ^ cols
    xs = [jnp.where(rows == cols, 1.0, 0.0) - jnp.where(apart == 1, s, 0.0) for s in strict]
    size = 2
    while size < CH:
        here = (apart >= size) & (apart < 2 * size)
        left = [mm3(x, jnp.where(here, s, 0.0)) for x, s in zip(xs, strict)]
        xs = [x - mm3(y, x) for x, y in zip(xs, left)]
        size *= 2
    return xs


def parts_kernel(heads, p_ref, halo_ref, first_ref, taps_ref, gcol_ref, grow_ref,
                 sum_ref, q_ref, k_ref, tinv_ref, a_ref, w_ref, uv_ref, qe_ref, oz_ref, m_ref, pre_ref, last_ref, x_ref):
    rows, cols = square_index()
    eye = jnp.where(rows == cols, 1.0, 0.0)
    width = heads * DV

    @pl.when(pl.program_id(0) == 0)
    def _():
        for h in range(heads):
            x_ref[h] = jnp.concatenate([eye, jnp.zeros((DK, DV), F32)], 1)

    def convolved(at, size):
        before = jnp.where(pl.program_id(0) == 0, first_ref[RIM - 8:, at:at + size], halo_ref[:, at:at + size])
        ext = jnp.concatenate([before, p_ref[:, at:at + size]], 0)
        summed = taps_ref[0:1, at:at + size] * ext[5:5 + FRONT * CH]
        for j in range(1, KC):
            summed = summed + taps_ref[j:j + 1, at:at + size] * ext[5 + j:5 + j + FRONT * CH]
        sum_ref[:, at:at + size] = summed
        return summed * sigmoid(summed)

    stricts, held = [], []
    for h in range(heads):
        act = convolved(2 * h * DK, 2 * DK)
        values = convolved(width + h * DV, DV)
        for c in range(FRONT):
            at = slice(c * CH, (c + 1) * CH)
            q, k = act[at, :DK], act[at, DK:]
            q = q * (lax.rsqrt(jnp.sum(q * q, axis=-1, keepdims=True) + 1e-6) * DK ** -0.5)
            k = k * lax.rsqrt(jnp.sum(k * k, axis=-1, keepdims=True) + 1e-6)
            gcol, beta = gcol_ref[at, h:h + 1], gcol_ref[at, heads + h:heads + h + 1]
            grow = grow_ref[c, h:h + 1, :]
            ratio = jnp.exp(jnp.where(rows >= cols, gcol - grow, -1e30))
            stricts.append(jnp.where(rows > cols, beta * ratio * mm3(k, k, TT), 0.0))
            held.append((h, c, q, k, values[at], ratio, gcol, beta, grow[:, CH - 1:CH]))
    for (h, c, q, k, v, ratio, gcol, beta, glast), tinv in zip(held, invert(stricts, rows, cols)):
        at, key, val = slice(c * CH, (c + 1) * CH), slice(h * DK, (h + 1) * DK), slice(h * DV, (h + 1) * DV)
        eg = jnp.exp(gcol)
        kd = k * jnp.exp(glast - gcol)
        a = ratio * mm(q, k, TT)
        w = mm3(tinv, (beta * eg) * k)
        uv = mm3(tinv, beta * v)
        m = jnp.exp(glast) * eye - mm(kd, w, TL)
        x = x_ref[h]
        pre_ref[c, h] = x
        x = mm(m, x) + jnp.concatenate([jnp.zeros((DK, DK), F32), mm(kd, uv, TL)], 1)
        x_ref[h] = x
        last_ref[h] = x.astype(BF)
        q_ref[at, key] = q.astype(BF)
        k_ref[at, key] = k.astype(BF)
        tinv_ref[c, h] = tinv.astype(BF)
        a_ref[c, h] = a.astype(BF)
        w_ref[at, key] = w.astype(BF)
        uv_ref[at, val] = uv
        qe_ref[at, key] = (q * eg - mm(a, w)).astype(BF)
        oz_ref[at, val] = mm(a, uv)
        m_ref[c, h] = m.astype(BF)


def whole(shape):
    return pl.BlockSpec(shape, lambda c: (0,) * len(shape))


PER = 2
FRONT = 4


def by_rows(width, n, back=False):
    last = n // PER - 1
    return pl.BlockSpec((PER * CH, width), (lambda c: (last - c, 0)) if back else (lambda c: (c, 0)))


def by_chunk(shape, n, back=False):
    tail, last = (0,) * len(shape), n // PER - 1
    return pl.BlockSpec((PER,) + shape, (lambda c: (last - c,) + tail) if back else (lambda c: (c,) + tail))


def sds(shape, dt=F32):
    return jax.ShapeDtypeStruct(shape, dt)


def call(kernel, name, n, micros, ins, outs, scratch, *operands, room=48):
    return pl.pallas_call(
        kernel,
        grid=(n,),
        in_specs=ins,
        out_specs=[spec for spec, _ in outs],
        out_shape=[shape for _, shape in outs],
        scratch_shapes=scratch,
        compiler_params=pltpu.CompilerParams(
            vmem_limit_bytes=room * 1024 * 1024, dimension_semantics=("arbitrary",)
        ),
        cost_estimate=pl.CostEstimate(flops=micros * 10**5, bytes_accessed=micros * 10**3, transcendentals=0),
        name=name,
    )(*operands)


def delta_parts(p, first, taps, gcol, grow, tokens, heads):
    n, span, width = tokens // CH, FRONT * CH, heads * DV

    def rows(size, dt=F32):
        return pl.BlockSpec((span, size), lambda c: (c, 0)), sds((tokens, size), dt)

    def chunk(shape, dt=F32):
        tail = (0,) * len(shape)
        return pl.BlockSpec((FRONT,) + shape, lambda c: (c,) + tail), sds((n,) + shape, dt)

    halo = pl.BlockSpec((8, 2 * width), lambda c: (jnp.maximum(c * (span // 8) - 1, 0), 0))
    return call(
        functools.partial(parts_kernel, heads), "delta_parts", n // FRONT, 35 * tokens // 1024,
        [rows(2 * width)[0], halo, whole(first.shape), whole(taps.shape), rows(gcol.shape[1])[0], chunk(grow.shape[1:])[0]],
        [rows(2 * width), rows(heads * DK, BF), rows(heads * DK, BF), chunk((heads, CH, CH), BF), chunk((heads, CH, CH), BF),
         rows(heads * DK, BF), rows(width), rows(heads * DK, BF), rows(width), chunk((heads, DK, DK), BF),
         chunk((heads, DK, DK + DV)), (whole((heads, DK, DK + DV)), sds((heads, DK, DK + DV), BF))],
        [pltpu.VMEM((heads, DK, DK + DV), F32)],
        p, p, first, taps, gcol, grow,
    )


def entering(maps, offsets, dims):
    state = offsets[-1].astype(F32)
    for found, offset in zip(maps[::-1], offsets[-2::-1]):
        state = mm(found, state, dims) + offset.astype(F32)
    return state


def outputs_kernel(heads, count, rows_before, pre_ref, qe_ref, oz_ref, gate_ref, gain_ref, *refs):
    near, slots, (s_ref, o_ref, gated_ref, mixed_ref, start_ref) = refs[:count], refs[count:-5], refs[-5:]

    @pl.when(pl.program_id(0) == 0)
    def _():
        for h in range(heads):
            maps = [a[h, :, :DK] for a in near[:-1]]
            offsets = [a[h, :, DK:] for a in near[:-1]] + [near[-1][h]]
            start_ref[h] = entering(maps, offsets, ((1,), (0,)))

    for h in range(heads):
        at = slice(h * DV, (h + 1) * DV)
        found = []
        for c in range(PER):
            rows = slice(c * CH, (c + 1) * CH)
            pre = pre_ref[c, h]
            s = mm(pre[:, :DK], start_ref[h]) + pre[:, DK:]
            s_ref[c, h] = s.astype(BF)
            found.append(mm(qe_ref[rows, h * DK:(h + 1) * DK], s) + oz_ref[rows, at])
        o = jnp.concatenate(found, 0)
        o_ref[:, at] = o
        gate = gate_ref[:, at]
        n = o * lax.rsqrt(jnp.mean(o * o, axis=-1, keepdims=True) + 1e-5)
        gated_ref[:, at] = (n * gain_ref[...] * (gate * sigmoid(gate))).astype(BF)
    gated = gated_ref[...]
    size = slots[0].shape[0] - rows_before
    for i, slot in enumerate(slots):
        mixed_ref[:, i * size:(i + 1) * size] = mm(gated, slot[rows_before:], TT).astype(BF)


def delta_outputs(near, slots, pre, qe, oz, gate, gain, rows_before, tokens, heads):
    n = tokens // CH
    wide = by_rows(heads * DV, n)
    size = len(slots) * (slots[0].shape[0] - rows_before)
    return call(
        functools.partial(outputs_kernel, heads, len(near), rows_before), "delta_outputs", n // PER, 7 * tokens // 1024,
        [by_chunk((heads, DK, DK + DV), n), by_rows(heads * DK, n), wide, wide, whole((1, DV))]
        + [whole(a.shape) for a in (*near, *slots)],
        [(by_chunk((heads, DK, DV), n), sds((n, heads, DK, DV), BF)), (wide, sds((tokens, heads * DV))),
         (wide, sds((tokens, heads * DV), BF)), (by_rows(size, n), sds((tokens, size), BF))],
        [pltpu.VMEM((heads, DK, DV), F32)],
        pre, qe, oz, gate, gain, *near, *slots,
    )


def states_back_kernel(heads, drows_ref, out_ref, o_ref, gate_ref, gain_ref, qe_ref, m_ref,
                       do_ref, dgate_ref, dc_ref, last_ref, dgain_ref, d_ref):
    @pl.when(pl.program_id(0) == 0)
    def _():
        d_ref[...] = jnp.zeros_like(d_ref)
        dgain_ref[...] = jnp.zeros_like(dgain_ref)

    dgated = mm(drows_ref[...], out_ref[...])
    for h in range(heads):
        at = slice(h * DV, (h + 1) * DV)
        o, gate, dg, gain = o_ref[:, at], gate_ref[:, at], dgated[:, at], gain_ref[...]
        rstd = lax.rsqrt(jnp.mean(o * o, axis=-1, keepdims=True) + 1e-5)
        n = o * rstd
        sg = sigmoid(gate)
        act = gate * sg
        dgain_ref[...] += jnp.sum(dg * n * act, axis=0, keepdims=True)
        dgate_ref[:, at] = (dg * n * gain * (sg * (1.0 + gate * (1.0 - sg)))).astype(BF)
        dn = dg * gain * act
        do = rstd * (dn - n * jnp.mean(dn * n, axis=-1, keepdims=True))
        do_ref[:, at] = do.astype(BF)
        d = d_ref[h]
        for c in reversed(range(PER)):
            rows = slice(c * CH, (c + 1) * CH)
            dc = mm(qe_ref[rows, h * DK:(h + 1) * DK], do[rows], TL)
            dc_ref[c, h] = dc
            d = mm(m_ref[c, h], d, TL) + dc
        d_ref[h] = d
        last_ref[h] = d.astype(BF)


def delta_states_back(drows, out_t, o, gate, gain, qe, m, tokens, heads):
    n = tokens // CH
    wide = by_rows(heads * DV, n, True)
    return call(
        functools.partial(states_back_kernel, heads), "delta_states_back", n // PER, 7 * tokens // 1024,
        [by_rows(drows.shape[1], n, True), whole(out_t.shape), wide, wide, whole((1, DV)), by_rows(heads * DK, n, True), by_chunk((heads, DK, DK), n, True)],
        [(wide, sds((tokens, heads * DV), BF)), (wide, sds((tokens, heads * DV), BF)),
         (by_chunk((heads, DK, DV), n, True), sds((n, heads, DK, DV))),
         (whole((heads, DK, DV)), sds((heads, DK, DV), BF)), (whole((1, DV)), sds((1, DV)))],
        [pltpu.VMEM((heads, DK, DV), F32)],
        drows, out_t, o, gate, gain, qe, m,
    )


def normed_pull(raw, grad, scale):
    r = lax.rsqrt(jnp.sum(raw * raw, axis=-1, keepdims=True) + 1e-6)
    n = raw * r
    return (scale * r) * (grad - n * jnp.sum(grad * n, axis=-1, keepdims=True))


BACK = 1


def conv_back(dact, at, width, sum_ref, in_ref, taps_ref, out_ref, dtaps_ref, rim_ref):
    where = slice(at, at + width)
    summed = sum_ref[:, where]
    sg = sigmoid(summed)
    dsum = dact * (sg * (1.0 + summed * (1.0 - sg)))
    ext = jnp.concatenate([dsum, rim_ref[:, where]], 0)
    rim_ref[:, where] = dsum[:8]
    conv_in = in_ref[:, where]
    dconv = jnp.zeros((BACK * CH, width), F32)
    for j in range(KC):
        moved = ext[3 - j:3 - j + BACK * CH]
        dconv = dconv + taps_ref[j:j + 1, where] * moved
        dtaps_ref[j:j + 1, where] += jnp.sum(moved * conv_in, axis=0, keepdims=True)
    out_ref[:, where] = dconv.astype(BF)


def rim_back(first_ref, taps_ref, out_ref, out_at, dtaps_ref, rim_ref):
    before = jnp.concatenate([jnp.zeros_like(rim_ref), rim_ref[...]], 0)
    conv_in = first_ref[RIM - 8:]
    drim = jnp.zeros(rim_ref.shape, F32)
    for j in range(KC):
        moved = before[3 - j:3 - j + 8]
        drim = drim + taps_ref[j:j + 1] * moved
        dtaps_ref[j:j + 1] += jnp.sum(moved * conv_in, axis=0, keepdims=True)
    width = rim_ref.shape[1]
    out_ref[:RIM, out_at:out_at + width] = jnp.concatenate([jnp.zeros_like(drim), drim], 0).astype(BF)


def inputs_back_kernel(heads, dc_ref, m_ref, s_ref, do_ref, uv_ref, w_ref, a_ref, tinv_ref, q_ref, k_ref,
                       sum_ref, p_ref, dgate_ref, first_ref, taps_ref, gcol_ref, grow_ref, *refs):
    near, (dall_ref, dtaps_ref, ds_ref, rim_ref) = refs[:-4], refs[-4:]
    last = pl.num_programs(0) - 1

    @pl.when(pl.program_id(0) == 0)
    def _():
        for h in range(heads):
            half = (len(near) - 1) // 2
            ds_ref[h] = entering([a[h] for a in near[:half]], [a[h] for a in near[half:]], ((0,), (0,)))
        for ref in (rim_ref, dtaps_ref):
            ref[...] = jnp.zeros_like(ref)

    @pl.when(pl.program_id(0) == last)
    def _():
        rim_back(first_ref, taps_ref, dall_ref, 0, dtaps_ref, rim_ref)
        dall_ref[:RIM, 2 * heads * DV:] = jnp.zeros((RIM, heads * DV), BF)

    @pl.when(pl.program_id(0) < last)
    def _():
        rows, cols = square_index()
        dall_ref[:, 2 * heads * DV:] = dgate_ref[...]
        for h in range(heads):
            ds = ds_ref[h]
            key, val = slice(h * DK, (h + 1) * DK), slice(h * DV, (h + 1) * DV)
            dqs, dks, dvs = [None] * BACK, [None] * BACK, [None] * BACK
            for c in reversed(range(BACK)):
                at = slice(c * CH, (c + 1) * CH)
                s, do, q, k = s_ref[c, h], do_ref[at, val], q_ref[at, key], k_ref[at, key]
                gcol, beta = gcol_ref[at, h:h + 1], gcol_ref[at, heads + h:heads + h + 1]
                grow = grow_ref[c, h:h + 1, :]
                glast = grow[:, CH - 1:CH]
                ratio = jnp.exp(jnp.where(rows >= cols, gcol - grow, -1e30))
                eg = jnp.exp(gcol)
                el = jnp.exp(glast - gcol)
                u = uv_ref[at, val] - mm(w_ref[at, key], s)
                du = mm(a_ref[c, h], do, TL) + el * mm(k, ds)
                da = ratio * mm(do, u, TT)
                drv = mm(tinv_ref[c, h], du, TL)
                dl = jnp.where(rows > cols, (-beta) * ratio * mm(drv, u, TT), 0.0)
                dqs[c] = eg * mm(do, s, TT) + mm(da, k)
                dks[c] = (
                    el * mm(u, ds, TT) + mm(da, q, TL) - (beta * eg) * mm(drv, s, TT) + mm(dl, k) + mm(dl, k, TL)
                )
                dvs[c] = beta * drv
                ds = mm(m_ref[c, h], ds, TL) + dc_ref[c, h]
            ds_ref[h] = ds
            summed = sum_ref[:, 2 * h * DK:2 * (h + 1) * DK]
            act = summed * sigmoid(summed)
            dq, dk, dv = (jnp.concatenate(a, 0) for a in (dqs, dks, dvs))
            dact = jnp.concatenate([normed_pull(act[:, :DK], dq, DK ** -0.5), normed_pull(act[:, DK:], dk, 1.0)], 1)
            conv_back(dact, 2 * h * DK, 2 * DK, sum_ref, p_ref, taps_ref, dall_ref, dtaps_ref, rim_ref)
            conv_back(dv, (heads + h) * DV, DV, sum_ref, p_ref, taps_ref, dall_ref, dtaps_ref, rim_ref)


def delta_inputs_back(near, dc, m, s, do, uv, w, a, tinv, q, k, summed, p, dgate, first, taps, gcol, grow,
                      tokens, heads):
    n = tokens // CH

    def at(c):
        return jnp.maximum(n // BACK - 1 - c, 0)

    def rows(width):
        return pl.BlockSpec((BACK * CH, width), lambda c: (at(c), 0))

    def chunk(shape):
        return pl.BlockSpec((BACK,) + shape, lambda c: (at(c),) + (0,) * len(shape))

    width = heads * DV
    wide, key = rows(width), rows(heads * DK)
    steps = n // BACK
    out = pl.BlockSpec((BACK * CH, 3 * width), lambda c: (jnp.where(c == steps, steps, steps - 1 - c), 0))
    return call(
        functools.partial(inputs_back_kernel, heads), "delta_inputs_back", steps + 1, 19 * tokens // 1024,
        [chunk((heads, DK, DV)), chunk((heads, DK, DK)), chunk((heads, DK, DV)),
         wide, wide, key, chunk((heads, CH, CH)), chunk((heads, CH, CH)), key, key,
         rows(2 * width), rows(2 * width), wide, whole(first.shape), whole(taps.shape), rows(gcol.shape[1]),
         chunk(grow.shape[1:])] + [whole(a.shape) for a in near],
        [(out, sds((tokens + RIM, 3 * width), BF)),
         (whole(taps.shape), sds(taps.shape))],
        [pltpu.VMEM((heads, DK, DV), F32), pltpu.VMEM((8, 2 * width), F32)],
        dc, m, s, do, uv, w, a, tinv, q, k, summed, p, dgate, first, taps, gcol, grow, *near,
    )


def as_column(row):
    size = row.shape[1]
    found = []
    for at in range(0, size, CH):
        part = row[:, at:min(at + CH, size)]
        if part.shape[1] < CH:
            part = jnp.concatenate([part, jnp.zeros((1, CH - part.shape[1]), F32)], 1)
        found.append(jnp.broadcast_to(part, (CH, CH)).T[:min(CH, size - at), 0:1])
    return jnp.concatenate(found, 0)


def moments_kernel(plan, over_head_ref, over_seq_ref, old_ref, carried_ref, place_ref, conv_second_ref,
                   both_ref, go_ref, outg_ref, ex_ref, sh_ref, *outs):
    beta_two = 1.0 - STEP ** (-0.8)
    (in_rows, in_cols, out_rows, out_cols, ex_rows, ex_cols, sh_rows, sh_cols, late_ref, kernel_ref, second_ref, update_ref,
     in_row, in_col, out_row, out_col, ex_row, ex_col, sh_row, sh_col) = outs
    heads = in_cols.shape[0]
    span = in_rows.shape[1]
    place = lax.broadcasted_iota(jnp.int32, (1, 128), 1)
    sums = carried_ref[...]
    sources = {"head": over_head_ref, "seq": over_seq_ref}

    def moment(name, old_at):
        axis, start, size, over = plan["cells"][name]
        old = old_ref[:, old_at:old_at + size]
        new = beta_two * old + (1.0 - beta_two) * (sources[axis][:, start:start + size] * (1.0 / over) + 1e-30)
        return new, lax.rsqrt(new)

    parts = {
        "in": (both_ref[:span], both_ref[span:], go_ref[...]),
        "out": (outg_ref[...],),
        "expand": (ex_ref[...].astype(F32),),
        "shrink": (sh_ref[...].astype(F32),),
    }
    refs = {
        "in": (in_rows, in_cols, in_row, in_col), "out": (out_rows, out_cols, out_row, out_col),
        "expand": (ex_rows, ex_cols, ex_row, ex_col), "shrink": (sh_rows, sh_cols, sh_row, sh_col),
    }
    for slot, name in enumerate(parts):
        rows_new, row_root = moment(name + "_rows", plan["old"][name + "_rows"])
        cols_new, col_root = moment(name + "_cols", plan["old"][name + "_cols"])
        rows_ref, cols_ref, row_ref, col_ref = refs[name]
        column = as_column(row_root)
        row_ref[...] = column
        col_ref[...] = col_root
        total, start = 0.0, 0
        for part in parts[name]:
            size = part.shape[1]
            update = part * column * col_root[:, start:start + size]
            total = total + jnp.sum(update * update, axis=(0, 1), keepdims=True)
            start += size
        sums = sums + jnp.where(place == slot, total, 0.0)
        row_total = jnp.sum(rows_new, axis=(0, 1), keepdims=True) * (1.0 / plan["copies"][name])
        sums = sums + jnp.where(place == 4 + slot, row_total, 0.0)
        if name == "in":
            rows_ref[...] = rows_new
            width = heads * DV
            for h in range(heads):
                for i in range(3):
                    cols_ref[h:h + 1, i * DV:(i + 1) * DV] = cols_new[:, i * width + h * DV:i * width + (h + 1) * DV]
        elif name == "out":
            cols_ref[...] = cols_new
            for h in range(heads):
                rows_ref[h:h + 1] = rows_new[:, h * DV:(h + 1) * DV]
        elif name == "expand":
            rows_ref[...] = rows_new
            size = cols_ref.shape[1]
            for i in range(2):
                cols_ref[i:i + 1] = cols_new[:, i * size:(i + 1) * size]
        else:
            rows_ref[...] = rows_new
            cols_ref[...] = cols_new
    axis, start, _, _ = plan["cells"]["taps"]
    cut, width = kernel_ref.shape[2], heads * DV
    total = 0.0
    for j in range(KC):
        for h in range(heads):
            grad = jnp.zeros((1, cut), F32)
            for c in range(CW // cut):
                at = start + j * 2 * width + (c * cut) // DV * width + h * DV + (c * cut) % DV
                grad = grad + place_ref[0:1, c:c + 1] * sources[axis][:, at:at + cut]
            second = beta_two * conv_second_ref[j, h:h + 1, :] + (1.0 - beta_two) * (grad * grad + 1e-30)
            update = grad * lax.rsqrt(second)
            kernel_ref[j, h:h + 1, :] = grad
            second_ref[j, h:h + 1, :] = second
            update_ref[j, h:h + 1, :] = update
            total = total + jnp.sum(update * update, axis=(0, 1), keepdims=True)
    late_ref[:, :128] = sums + jnp.where(place == 13, total, 0.0)
    share = 1.0 / plan["head_count"]
    for name, at in (("gain_two", 128), ("head_gain", 128 + D)):
        axis, start, size, _ = plan["cells"][name]
        late_ref[:, at:at + size] = sources[axis][:, start:start + size] * share


def new_moments(plan, outs, operands):
    return pl.pallas_call(
        functools.partial(moments_kernel, plan),
        out_shape=[sds(a) for a in outs],
        compiler_params=pltpu.CompilerParams(vmem_limit_bytes=56 * 1024 * 1024),
        name="new_moments",
    )(*operands)


def cast_kernel(heads, in_ref, kv_ref, gate_ref):
    width = heads * DV
    for h in range(heads):
        at = slice(h * DV, (h + 1) * DV)
        kv_ref[:, at] = in_ref[:, h, :DV].astype(BF)
        kv_ref[:, width + h * DV:width + (h + 1) * DV] = in_ref[:, h, DV:2 * DV].astype(BF)
        gate_ref[:, at] = in_ref[:, h, 2 * DV:].astype(BF)


def cast_columns(weight, steps=4):
    heads, span = weight.shape[1], weight.shape[0] // steps
    width = heads * DV
    return call(
        functools.partial(cast_kernel, heads), "cast_columns", steps, 3,
        [pl.BlockSpec((span, heads, HC), lambda c: (c, 0, 0))],
        [(pl.BlockSpec((span, size), lambda c: (c, 0)), sds((weight.shape[0], size), BF)) for size in (2 * width, width)],
        [],
        weight,
    )


def split_kernel(grad_ref, out_ref):
    size = out_ref.shape[2]
    for i in range(2):
        out_ref[:, i, :] = grad_ref[:, i * size:(i + 1) * size].astype(F32)


def split_columns(grad, steps=4):
    span, size = grad.shape[0] // steps, grad.shape[1] // 2
    return call(
        split_kernel, "split_columns", steps, 3,
        [pl.BlockSpec((span, 2 * size), lambda c: (c, 0))],
        [(pl.BlockSpec((span, 2, size), lambda c: (c, 0, 0)), sds((grad.shape[0], 2, size)))],
        [],
        grad,
    )[0]


def small_step(weight, gradient, second_old, beta_two):
    second_new = beta_two * second_old + (1.0 - beta_two) * (gradient * gradient + 1e-30)
    update = gradient * lax.rsqrt(second_new)
    root = jnp.sqrt(jnp.mean(update * update, axis=-1, keepdims=True))
    scale = 0.3 * jnp.maximum(0.001, jnp.sqrt(jnp.mean(weight * weight, axis=-1, keepdims=True)))
    return second_new, weight - scale * (update / jnp.maximum(1.0, root))


def weights_kernel(heads, late_ref, gains_ref, gains_second_ref, head_ref, head_second_ref, conv_ref, conv_update_ref,
                   in_ref, keys_ref, vals_ref, gate_ref, in_row, in_col, out_ref, outg_ref, out_row, out_col,
                   ex_ref, exg_ref, ex_row, ex_col, sh_ref, shg_ref, sh_row, sh_col,
                   gains_grad, gains_second_new, gains_new, head_grad, head_second_new, head_new, conv_new,
                   in_new, out_new, ex_new, sh_new, in_grad):
    beta_two = 1.0 - STEP ** (-0.8)
    counts = ((D, HEAD_TOTAL * HC), (HEAD_TOTAL * DV, D), (D, 2 * FF), (FF, D))

    def cell(at):
        return late_ref[0:1, at:at + 1]

    def size_of(weight, entries):
        return 0.3 * jnp.maximum(0.001, jnp.sqrt(weight * (1.0 / entries)))

    def scale(slot):
        mean, entries = cell(4 + slot) * (1.0 / counts[slot][0]), counts[slot][0] * counts[slot][1]
        root = jnp.sqrt(cell(slot) * mean * (1.0 / entries))
        return size_of(cell(8 + slot), entries) * jnp.sqrt(mean) / jnp.maximum(1.0, root)

    scales = [scale(slot) for slot in range(4)]

    @pl.when(pl.program_id(0) == 0)
    def _():
        for row in range(2):
            first = 128 if row else 128 + D + DV
            grad = late_ref[0:1, first:first + D]
            at = slice(row, row + 1)
            gains_grad[at] = grad
            gains_second_new[at], gains_new[at] = small_step(gains_ref[at], grad, gains_second_ref[at], beta_two)
        grad = late_ref[0:1, 128 + D:128 + D + DV]
        head_grad[...] = grad
        head_second_new[...], head_new[...] = small_step(head_ref[...], grad, head_second_ref[...], beta_two)
        entries = KC * HEAD_TOTAL * CW
        factor = size_of(cell(12), entries) / jnp.maximum(1.0, jnp.sqrt(cell(13) * (1.0 / entries)))
        conv_new[...] = conv_ref[...] - conv_update_ref[...] * factor[None]

    def stepped(weight, grad, rows, cols, slot):
        return weight - (grad.astype(F32) * cols) * (rows * scales[slot])

    width = heads * DV
    for h in range(heads):
        for i, ref in enumerate((keys_ref, vals_ref, gate_ref)):
            col = in_col[:, i * width + h * DV:i * width + (h + 1) * DV]
            at = slice(i * DV, (i + 1) * DV)
            grad = ref[:, h * DV:(h + 1) * DV]
            in_grad[:, h, at] = grad
            in_new[:, h, at] = stepped(in_ref[:, h, at], grad, in_row[...], col, 0)
    out_new[...] = stepped(out_ref[...], outg_ref[...], out_row[...], out_col[...], 1)
    size = ex_ref.shape[2]
    for i in range(2):
        at = slice(i * size, (i + 1) * size)
        ex_new[:, i, :] = stepped(ex_ref[:, i, :], exg_ref[:, at], ex_row[...], ex_col[:, at], 2)
    sh_new[...] = stepped(sh_ref[...], shg_ref[...], sh_row[...], sh_col[...], 3)


def new_weights(heads, small, groups):
    ins, operands = [whole(a.shape) for a in small], list(small)
    late, gains, _, head = small[:4]
    outs = [(whole(a.shape), sds(a.shape)) for a in (gains, gains, gains, head, head, head, small[5])]
    steps = 8 if groups[3][0].shape[0] % 128 == 0 else 4

    def blocked(a, span, first=0):
        tail = a.shape[1:]
        return pl.BlockSpec((span,) + tail, lambda c: (c + first,) + (0,) * len(tail))

    for weight, parts, rows, cols in groups:
        span = weight.shape[0] // steps
        for i, a in enumerate((weight, *parts, rows)):
            ins.append(blocked(a, span, steps if len(parts) == 3 and i == 2 else 0))
            operands.append(a)
        ins.append(whole(cols.shape))
        operands.append(cols)
        outs.append((blocked(weight, span), sds(weight.shape)))
    weight = groups[0][0]
    outs.append((blocked(weight, weight.shape[0] // steps), sds(weight.shape)))
    return call(functools.partial(weights_kernel, heads), "new_weights", steps, 10, ins, outs, [], *operands, room=56)


def ring(x, by=1):
    n = lax.axis_size("seq")
    return lax.ppermute(x, "seq", [(i, (i + by) % n) for i in range(n)])


def ahead(x, by):
    n = lax.axis_size("seq")
    return lax.ppermute(x, "seq", [(i, i + by) for i in range(n) if 0 <= i + by < n])


def after(x, *others):
    return lax.optimization_barrier((x,) + others)[0]


def ring_gather(x, hold=None):
    slots = [x]
    for k in range(1, lax.axis_size("seq")):
        slots.append(ring(after(slots[-1], *(hold or {}).get(k, ()))))
    return slots


def vector_of(scalars, size, first=0):
    place = lax.broadcasted_iota(jnp.int32, (1, size), 1)
    return sum(jnp.where(place == first + i, a, 0.0) for i, a in enumerate(scalars))


def ring_scatter(part, hold=None):
    n = lax.axis_size("seq")
    total, totals = part(1).astype(BF), []
    for k in range(1, n):
        held = hold(k) if hold else ()
        total = ring(after(total, *held) if held else total).astype(F32) + part((k + 1) % n).astype(F32)
        total = total if k == n - 1 else total.astype(BF)
        totals.append(total)
    return total, totals


def seq_slot(x, k, axis=0):
    n, z = lax.axis_size("seq"), lax.axis_index("seq")
    span = x.shape[axis] // n
    return lax.dynamic_slice_in_dim(x, lax.rem(z - k + n, n) * span, span, axis)


def in_order(slots, axis=0):
    n, z = lax.axis_size("seq"), lax.axis_index("seq")
    span = slots[0].shape[axis]
    turned = jnp.concatenate(slots[::-1] + slots[:0:-1], axis)
    return lax.dynamic_slice_in_dim(turned, (n - 1 - z) * span, n * span, axis)


def gather_head(x, axis=0):
    return lax.all_gather(x, "head", axis=axis, tiled=True)


def scatter_head(x, axis=0):
    return lax.psum_scatter(x, "head", scatter_dimension=axis, tiled=True)


def total_over(axis, x, arrived=None):
    n = lax.axis_size(axis)
    if n & (n - 1):
        return lax.psum(x, axis)
    step = 1
    while step < n:
        other = lax.ppermute(x, axis, [(i, i ^ step) for i in range(n)])
        if arrived is not None:
            arrived.append(other)
        x = x + other
        step *= 2
    return x


def dot(a, b, dims=((1,), (0,)), out=F32):
    return lax.dot_general(a, b, (dims, ((), ())), preferred_element_type=out)


def norm_rows(entries, scale_row):
    return entries * lax.rsqrt(jnp.mean(entries * entries, axis=-1, keepdims=True) + 1e-06) * scale_row


def nearby(last):
    n = lax.axis_size("seq")
    return [ahead(last, k) for k in range(1, n - 1)] + [ahead(last[..., DK:], n - 1)]


def local(
    hidden_in,
    out_grad,
    decays,
    strength,
    mixer_in,
    mixer_in_rows,
    mixer_in_cols,
    mixer_out,
    mixer_out_rows,
    mixer_out_cols,
    feed_in,
    feed_in_rows,
    feed_in_cols,
    feed_out,
    feed_out_rows,
    feed_out_cols,
    conv_kernel,
    conv_second,
    norm_gains,
    gains_second,
    head_gain,
    head_gain_second,
):
    beta_two = 1.0 - STEP ** (-0.8)
    n = lax.axis_size("seq")
    seq_count, head_count = n, lax.axis_size("head")
    tokens, heads = decays.shape
    blocks = tokens // CH
    in_span = mixer_in.shape[0]
    out_span = mixer_out.shape[2]
    feed_span, hidden_span = feed_in.shape[0], feed_in.shape[2]
    width = heads * DV

    def padded(pieces):
        found, cells, at = [], {}, 0
        for name, piece in pieces.items():
            piece = piece.reshape(1, -1)
            size = piece.shape[1]
            room = -(-size // 128) * 128
            found.append(jnp.pad(piece, ((0, 0), (0, room - size))))
            cells[name] = (at, size)
            at += room
        return jnp.concatenate(found, 1), cells

    old_moments, old_cells = padded(
        {
            "in_rows": mixer_in_rows,
            "in_cols": jnp.stack([mixer_in_cols[:, i * DV : (i + 1) * DV] for i in range(3)]),
            "out_rows": mixer_out_rows,
            "out_cols": mixer_out_cols,
            "expand_rows": feed_in_rows,
            "expand_cols": feed_in_cols,
            "shrink_rows": feed_out_rows,
            "shrink_cols": feed_out_cols,
        }
    )
    over_counts = {
        "in_rows": HEAD_TOTAL * HC, "in_cols": D, "out_rows": D, "out_cols": HEAD_TOTAL * DV,
        "expand_rows": 2 * FF, "expand_cols": D, "shrink_rows": D, "shrink_cols": FF,
    }
    place = jnp.where(lax.broadcasted_iota(jnp.int32, (1, 128), 1) == lax.axis_index("seq"), 1.0, 0.0)

    x = hidden_in.astype(F32)
    rows_all = gather_head(norm_rows(x, norm_gains[0]).astype(BF))
    kv_own, gate_own = cast_columns(mixer_in)
    taps_mine = conv_kernel.astype(BF).reshape(KC, heads * conv_kernel.shape[2])
    taps_slots = [taps_mine] + [ring(taps_mine, k) for k in range(1, n)]
    kv_slots = ring_gather(kv_own, {1: taps_slots[1:]})[:3]
    rim = ahead(rows_all[tokens - RIM :], 1)
    taps = in_order([t[None] for t in taps_slots]).reshape(n, KC, heads, -1)
    taps = jnp.moveaxis(taps, 0, 2).reshape(KC, heads, CW).astype(F32)
    taps = jnp.concatenate([taps[:, :, : 2 * DK].reshape(KC, width), taps[:, :, 2 * DK :].reshape(KC, width)], 1)

    lower = jnp.tril(jnp.ones((CH, CH), F32))
    log_sum = jnp.einsum(
        "ij,bjh->bih", lower, jnp.log(decays).reshape(blocks, CH, heads), precision=lax.Precision.HIGHEST
    )
    gcol = jnp.concatenate([log_sum.reshape(tokens, heads), strength, jnp.zeros((tokens, 8 - 2 * heads), F32)], 1)
    grow = jnp.concatenate([jnp.swapaxes(log_sum, 1, 2), jnp.zeros((blocks, 8 - heads, CH), F32)], 1)
    gain_row = head_gain[None]
    row_slots = [seq_slot(rows_all, k, 1) for k in range(n)]

    def projected(parts, slots, total=None):
        for part, slot in zip(parts, slots):
            found = dot(part, slot)
            total = found if total is None else total + found
        return total

    expand = gather_head(after(feed_in.astype(BF).reshape(feed_span, 2 * hidden_span), rows_all, kv_slots[1]))
    p_start = projected(row_slots[:2], kv_slots[:2])
    kv_held, p_start, rim = lax.optimization_barrier((kv_slots[2], p_start, rim))
    kv_slots[2] = kv_held
    for _ in range(3, n):
        kv_slots.append(ring(kv_slots[-1]))
    rim_slots = [seq_slot(rim, k, 1) for k in range(n)]
    p_kv, r_kv = projected(row_slots[2:], kv_slots[2:], p_start), projected(rim_slots, kv_slots)
    go_own = jnp.concatenate([gate_own, mixer_out.astype(BF).reshape(width, out_span).T], 0)
    go_slots = ring_gather(go_own, {1: (kv_slots[-1],)})[:2]
    (summed, q, k, tinv, scores, w, uv, qe, oz, m, pre, last) = delta_parts(
        p_kv, r_kv, taps, gcol, grow, tokens, heads
    )
    last, go_one, go_zero, expand = lax.optimization_barrier((last, go_slots[1], go_slots[0], expand))
    go_slots = [go_zero, go_one]
    for _ in range(2, n):
        go_slots.append(ring(go_slots[-1]))
    shrink = gather_head(after(feed_out.astype(BF), expand, last, go_slots[2]), 1)
    p_gate = projected(row_slots, [a[:in_span] for a in go_slots])
    states, o, gated, mixed = delta_outputs(
        nearby(last), go_slots, pre, qe, oz, p_gate, gain_row, in_span, tokens, heads
    )
    maps_after = [ahead(last[..., :DK], -k) for k in range(1, n - 1)]
    grad_slots = ring_gather(out_grad, {1: (go_slots[-1],), 2: maps_after})
    grad_rows = jnp.concatenate(grad_slots, 0)
    mixed = scatter_head(after(mixed, shrink)).astype(F32)
    mixed = in_order([mixed[:, i * out_span : (i + 1) * out_span] for i in range(n)], 1)
    residual = x + mixed
    out_t = in_order([a[in_span:] for a in go_slots])
    w_all = in_order([jnp.concatenate([a, b[:in_span]], 1) for a, b in zip(kv_slots, go_slots)])
    weights_then = lax.optimization_barrier((mixer_in, mixer_out, feed_in, feed_out, gated))[:4]
    weight_sums = vector_of([jnp.sum(a * a) for a in (*weights_then, conv_kernel)], 128, 8)

    normed_two, norm_two_pull = jax.vjp(norm_rows, residual, norm_gains[1])
    d_hidden = lax.optimization_barrier(dot(grad_rows, shrink, ((1,), (1,))))
    feed_held, out_t, w_all, weight_sums, old_moments = lax.optimization_barrier(
        (normed_two.astype(BF), out_t, w_all, weight_sums, old_moments)
    )
    rows_here = hidden_in.shape[0]

    def slot_rows(a, k):
        return a[k * rows_here : (k + 1) * rows_here]

    def fed(rows, first):
        gate_up = dot(rows, expand)
        gate, up = gate_up[:, :hidden_span], gate_up[:, hidden_span:]
        d_here = d_hidden[first * rows_here : first * rows_here + rows.shape[0]]
        sig = sigmoid(gate)
        silu = gate * sig
        d_gate_up = jnp.concatenate([d_here * up * (sig * (1.0 + gate * (1.0 - sig))), d_here * silu], 1).astype(BF)
        return (silu * up).astype(BF), d_gate_up, dot(d_gate_up, expand, ((1,), (1,)))

    feed_slots = ring_gather(feed_held, {1: (grad_slots[-1],), 2: (d_hidden,)})[:3]
    hidden_one, d_gate_up_one, d_feed_one = fed(jnp.concatenate(feed_slots[:2], 0), 0)
    feed_held, d_feed_one = lax.optimization_barrier((feed_slots[2], d_feed_one))
    feed_slots[2] = feed_held
    for _ in range(3, n):
        feed_slots.append(ring(feed_slots[-1]))
    shrink_sum = ring(slot_rows(d_feed_one, 1).astype(BF))
    feed_rows = jnp.concatenate(feed_slots, 0)
    hidden_two, d_gate_up_two, d_feed_two = fed(jnp.concatenate(feed_slots[2:], 0), 2)
    hidden = jnp.concatenate([hidden_one, hidden_two], 0)
    d_gate_up = jnp.concatenate([d_gate_up_one, d_gate_up_two], 0)
    for step in range(2, n):
        shrink_sum = ring((shrink_sum.astype(F32) + slot_rows(d_feed_two, step - 2)).astype(BF))
    d_normed_two = shrink_sum.astype(F32) + slot_rows(d_feed_one, 0)
    d_residual_part, d_gain_two = norm_two_pull(d_normed_two)
    d_residual = out_grad.astype(F32) + d_residual_part
    d_residual_low = d_residual.astype(BF)
    d_rows = gather_head(d_residual_low)
    hidden_then, feed_rows_then, _ = lax.optimization_barrier((hidden, feed_rows, d_residual_low))
    shrink_part = dot(hidden_then, grad_rows, ((0,), (0,)), BF)
    feed_part = dot(hidden_then, shrink, out=BF)
    feed_part = in_order([slot_rows(feed_part, i) for i in range(n)])
    expand_part = dot(feed_rows_then, d_gate_up, ((0,), (0,)), BF)
    shrink_part, expand_part, feed_part, d_rows = lax.optimization_barrier(
        (shrink_part, expand_part, feed_part, d_rows)
    )
    shrink_low = scatter_head(shrink_part, 1)

    do, d_gate, dc, d_last, d_head_gain = delta_states_back(d_rows, out_t, o, p_gate, gain_row, qe, m, tokens, heads)
    near = maps_after + [ahead(d_last, -k) for k in range(1, n)]
    gate_then, d_rows_then, _ = lax.optimization_barrier((d_gate, d_rows, d_last))

    def go_part(k, out=F32, rows=d_rows_then):
        d_slot = seq_slot(rows, k, 1)
        return jnp.concatenate([dot(row_slots[k], gate_then, TL, out), dot(d_slot, gated, TL, out)], 0)

    def added(arrived, part):
        return arrived.astype(F32) + part.astype(F32)

    go, go_next = lax.optimization_barrier((go_part(1, BF), go_part(2 % n), *near))[:2]
    sent = ring(go)
    d_all, d_taps = delta_inputs_back(
        near, dc, m, states, do, uv, w, scores, tinv, q, k, summed, p_kv, d_gate, r_kv, taps, gcol, grow, tokens, heads
    )
    d_all, sent, go_next, gate_then, d_rows_then = lax.optimization_barrier(
        (d_all, sent, go_next, gate_then, d_rows_then)
    )
    more_slots = [jnp.concatenate([a, b], 0) for a, b in zip(row_slots, rim_slots)]

    def both_dots(k, out):
        return [dot(more_slots[k], d_all[:, i * width : (i + 1) * width], TL, out) for i in range(2)]

    def both_part(k, out=F32):
        return jnp.concatenate(both_dots(k, out), 0)

    first_dots = both_dots(1, BF)
    go = added(sent, go_next).astype(BF)
    sending = jnp.concatenate([go, *first_dots], 0)
    d_all_then, sending = lax.optimization_barrier((d_all, sending))
    sent = ring(sending)
    d_rows_more = dot(d_all_then, w_all, ((1,), (1,)), BF)
    expand_low = scatter_head(after(expand_part, shrink_low, sending))
    shrink_g, expand_g = shrink_low.astype(F32), expand_low.astype(F32)
    parts = [jnp.concatenate([go_part((step + 1) % n, F32, d_rows_then), both_part(step)], 0) for step in range(2, n)]
    rim_rows, last_part, *parts = lax.optimization_barrier((d_rows_more[tokens:], both_part(0), *parts))
    rim_back = ahead(rim_rows, -1)
    d_rows_in = jnp.concatenate([d_rows_more[: tokens - RIM], d_rows_more[tokens - RIM : tokens] + rim_back], 0)
    feed_sums = (jnp.sum(expand_g * expand_g, 0), jnp.sum(shrink_g * shrink_g, 1))
    feed_sums += (jnp.sum(expand_g * expand_g, 1), jnp.sum(shrink_g * shrink_g, 0))
    for step in range(2, n - 1):
        total = added(sent, parts[step - 2]).astype(BF)
        if step < n - 2:
            sent = ring(total)
    gate_held, sent = total[:in_span], ring(total[in_span:])
    d_normed_low = scatter_head(after(d_rows_in, expand_low, sent))
    part = parts[-1]
    both = added(sent[in_span:], part[2 * in_span :]).astype(BF)
    last_sent = ring(jnp.concatenate([gate_held, both], 0))
    out_g = added(sent[:in_span], part[in_span : 2 * in_span])
    expand_out = split_columns(expand_low)
    out_g, last_sent, expand_out, *feed_sums = lax.optimization_barrier((out_g.T, last_sent, expand_out, *feed_sums))
    both_grad, go = added(last_sent[in_span:], last_part), added(last_sent[:in_span], part[:in_span])
    d_normed = d_normed_low.astype(F32)

    _, norm_one_pull = jax.vjp(norm_rows, x, norm_gains[0])
    d_residual_one, d_gain_one = norm_one_pull(d_normed)
    input_grad = d_residual + d_residual_one


    out_sq, both_sq, gate_sq = out_g * out_g, both_grad * both_grad, go * go
    over_head, head_cells = padded(
        {
            "expand_cols": feed_sums[0],
            "shrink_rows": feed_sums[1],
            "gain_two": d_gain_two,
            "head_gain": d_head_gain,
            "out_cols": jnp.sum(out_sq, 0),
            "in_rows": jnp.sum(both_sq[:in_span], 1) + jnp.sum(both_sq[in_span:], 1) + jnp.sum(gate_sq, 1),
        }
    )
    over_seq, seq_cells = padded(
        {
            "expand_rows": feed_sums[2],
            "shrink_cols": feed_sums[3],
            "taps": d_taps,
            "out_rows": jnp.sum(out_sq, 1),
            "in_cols": jnp.concatenate([jnp.sum(a, 0) for a in (both_sq[:in_span], both_sq[in_span:], gate_sq)]),
        }
    )
    arrived = []
    over_head, over_seq = total_over("head", over_head, arrived), total_over("seq", over_seq, arrived)

    cells = {}
    for axis, found in (("head", head_cells), ("seq", seq_cells)):
        for name, (at, size) in found.items():
            cells[name] = (axis, at, size, over_counts.get(name))
    plan = {
        "cells": cells,
        "old": {name: at for name, (at, _) in old_cells.items()},
        "copies": {"in": head_count, "out": seq_count, "expand": seq_count, "shrink": head_count},
        "head_count": head_count,
    }
    shape = {name: (1, size) for name, (_, _, size, _) in cells.items()}
    conv_shape = conv_kernel.shape
    (in_rows_new, in_cols_new, out_rows_new, out_cols_new, expand_rows_new, expand_cols_new, shrink_rows_new,
     shrink_cols_new, late, kernel_grad, conv_second_new, conv_update, *roots) = new_moments(
        plan,
        [shape["in_rows"], (heads, HC), (heads, DV), shape["out_cols"], shape["expand_rows"], (2, hidden_span),
         shape["shrink_rows"], shape["shrink_cols"], (1, 128 + D + DV), conv_shape, conv_shape, conv_shape]
        + [a for name in ("in", "out", "expand", "shrink") for a in ((shape[name + "_rows"][1], 1), shape[name + "_cols"])],
        [over_head, over_seq, old_moments, weight_sums, place, conv_second,
         both_grad, go, out_g, expand_low, shrink_low],
    )
    feed_sum = lax.psum_scatter(after(feed_part, d_normed_low, arrived[1], arrived[-1]), "seq", scatter_dimension=0, tiled=True).astype(F32)
    block_out = (residual + feed_sum).astype(BF)

    late = total_over("seq", total_over("head", jnp.concatenate([late, d_gain_one[None]], 1)))
    (gains_grad, gains_second_new, gains_new, head_gain_grad, head_second_new, head_new, conv_new,
     in_new, out_new, expand_new, shrink_new, in_grad) = new_weights(
        heads,
        (late, norm_gains, gains_second, head_gain[None], head_gain_second[None], conv_kernel, conv_update),
        [
            (mixer_in, (both_grad, both_grad, go), *roots[0:2]),
            (mixer_out.reshape(width, out_span), (out_g,), *roots[2:4]),
            (feed_in, (expand_low,), *roots[4:6]),
            (feed_out, (shrink_low,), *roots[6:8]),
        ],
    )
    return (
        block_out,
        input_grad,
        in_grad,
        in_rows_new.reshape(-1),
        in_cols_new,
        in_new,
        out_g.reshape(mixer_out.shape),
        out_rows_new,
        out_cols_new.reshape(-1),
        out_new.reshape(mixer_out.shape),
        expand_out,
        expand_rows_new.reshape(-1),
        expand_cols_new,
        expand_new,
        shrink_g,
        shrink_rows_new.reshape(-1),
        shrink_cols_new.reshape(-1),
        shrink_new,
        kernel_grad,
        conv_second_new,
        conv_new,
        gains_grad,
        gains_second_new,
        gains_new,
        head_gain_grad.reshape(-1),
        head_second_new.reshape(-1),
        head_new.reshape(-1),
    )


def solution(mesh):
    return jax.shard_map(
        local,
        mesh=mesh,
        in_specs=(
            P(("seq", "head"), None),
            P(("seq", "head"), None),
            P("seq", "head"),
            P("seq", "head"),
            P("seq", "head", None),
            P("seq"),
            P("head", None),
            P("head", None, "seq"),
            P("head", None),
            P("seq"),
            P("head", None, "seq"),
            P("head"),
            P(None, "seq"),
            P("seq", "head"),
            P("seq"),
            P("head"),
            P(None, "head", "seq"),
            P(None, "head", "seq"),
            P(),
            P(),
            P(),
            P(),
        ),
        out_specs=(
            P(("seq", "head"), None),
            P(("seq", "head"), None),
            P("seq", "head", None),
            P("seq"),
            P("head", None),
            P("seq", "head", None),
            P("head", None, "seq"),
            P("head", None),
            P("seq"),
            P("head", None, "seq"),
            P("head", None, "seq"),
            P("head"),
            P(None, "seq"),
            P("head", None, "seq"),
            P("seq", "head"),
            P("seq"),
            P("head"),
            P("seq", "head"),
            P(None, "head", "seq"),
            P(None, "head", "seq"),
            P(None, "head", "seq"),
            P(),
            P(),
            P(),
            P(),
            P(),
            P(),
        ),
        check_vma=False,
    )
```
